32 devices in a mesh: ctx: 8 (over y, x, core), ch: 4 (over z).
Axes of the slice: x: 2, y: 2, z: 4, core: 2. Of those that a mesh axis runs over, the one named last changes fastest.
Arguments:
- grad_out: bfloat16 [8, 2, 256, 4096], P('ctx', None, None, 'ch'), may hold values from -6 to 6
- out_weight: bfloat16 [4096, 4096], P('ch'), may hold values from -0.09375 to 0.09375
- gate: bfloat16 [8, 2, 256, 4096], P('ctx', None, None, 'ch'), may hold values from -6 to 6
- filter_taps: float32 [768, 4096], P(None, 'ch'), may hold values from -0.21875 to 0.21875
- doc_starts: int32 [32], replicated, may hold values from 0 to 4096, as said below
Outputs:
- grad_input: float32 [8, 2, 256, 4096], P('ctx', None, None, 'ch')
The draws below stay inside these ranges and needn't reach their ends.
Inputs may be any that keep to these rules, and one draw needn't show every extreme that they name: `doc_starts`: Non-decreasing; the first is 0; offsets below 4096 start documents, the others equal 4096. Every document is at most 768 tokens long and every one but the last at least 128; one has exactly 768 tokens and one exactly 128.
All inputs are finite; a program needn't handle non-finite values.
Results may differ from the reference program's by a relative error of at most 0.0029.
Values may be sent and summed in bfloat16 or wider, within the bound.
No kernel may reach another device: no remote copies, remote signals or barrier semaphores. Data moves between devices by JAX's collectives and lax.ppermute only.
A program may use at most 192 MiB of HBM per device.

```python
import jax
import jax.numpy as jnp
from jax import lax

C = 4096
CL = 256
REACH = 3
PAIRS = 8
NCH = 16
SEQ = 4096
N2 = 512
FL = 768
NDOC = 32


def draw_doc_starts(key, part):
    gap_key, first_key, second_key = jax.random.split(key, 3)
    gaps = jax.random.randint(gap_key, (NDOC,), CL // 2, FL + 1)
    longest = jax.random.randint(first_key, (), 0, 2)
    shortest = longest + 1 + jax.random.randint(second_key, (), 0, 2)
    order = jnp.arange(NDOC)
    gaps = jnp.where(order == longest, FL, gaps)
    gaps = jnp.where(order == shortest, CL // 2, gaps)
    starts = jnp.concatenate([jnp.zeros((1,), jnp.int32), jnp.cumsum(gaps)[:-1].astype(jnp.int32)])
    return jnp.minimum(starts, SEQ).astype(jnp.int32)


def levels(key, dims, pieces, smallest, largest):
    factor_of = 1.0
    for axis_at, shards_of in pieces:
        draws = jax.random.uniform(jax.random.fold_in(jax.random.fold_in(key, 6), axis_at), (shards_of,), jnp.float32, smallest / len(pieces), largest / len(pieces))
        factor_of = factor_of * jnp.repeat(jnp.exp(draws), dims[axis_at] // shards_of).reshape((-1,) + (1,) * (len(dims) - 1 - axis_at))
    return factor_of


def normal_values(key, dims, width, limit, pieces=(), kind=jnp.bfloat16):
    values = width * jax.random.normal(key, dims, jnp.float32)
    if pieces:
        values = values * levels(key, dims, pieces, -0.22, 0.18)
    return jnp.clip(values, -limit, limit).astype(kind)


def setup_inputs(seed: int = 0) -> dict:
    seeds = jax.random.split(jax.random.key(seed), 6)
    grad_out = normal_values(seeds[0], (PAIRS, 2, CL, C), 1.0, 6.0, ((0, 8), (3, 4)))
    out_weight = normal_values(seeds[1], (C, C), C ** -0.5, 0.09375, ((0, 4),))
    gate = normal_values(seeds[2], (PAIRS, 2, CL, C), 1.0, 6.0, ((0, 8), (3, 4)))
    filter_taps = normal_values(seeds[3], (FL, C), FL ** -0.5, 0.21875, ((1, 4),), jnp.float32)
    doc_starts = draw_doc_starts(jax.random.fold_in(seeds[5], 71), 0)
    return {"grad_out": grad_out, "out_weight": out_weight, "gate": gate, "filter_taps": filter_taps, "doc_starts": doc_starts}


def to_bfloat(values):
    return lax.optimization_barrier(values.astype(jnp.bfloat16)).astype(jnp.float32)


def unfold(folded):
    return jnp.concatenate([folded[:, 0], folded[::-1, 1]], axis=0)


def fold(blocks):
    return jnp.stack([blocks[:PAIRS], blocks[PAIRS:][::-1]], axis=1)


def reference(grad_out, out_weight, gate, filter_taps, doc_starts):
    rows = grad_out.reshape(-1, C)
    projected = jnp.dot(rows, out_weight.T, preferred_element_type=jnp.float32).reshape(grad_out.shape)
    conv_grad = to_bfloat(projected * gate.astype(jnp.float32))
    blocks = unfold(conv_grad)
    positions = jnp.arange(SEQ, dtype=jnp.int32)
    doc_index = jnp.sum((doc_starts[None, :] <= positions[:, None]).astype(jnp.int32), axis=1) - 1
    doc_index = doc_index.reshape(NCH, CL)
    first_doc = doc_index[:, 0]
    last_doc = doc_index[:, -1]
    segment = doc_index - first_doc[:, None]
    taps = filter_taps.astype(jnp.float32)
    offsets = jnp.arange(N2, dtype=jnp.int32)

    def kernel_spectrum(distance):
        lag = jnp.where(offsets < CL, distance * CL - offsets, distance * CL + N2 - offsets)
        valid = (lag >= 0) & (lag < FL)
        kernel = jnp.where(valid[:, None], taps[jnp.clip(lag, 0, FL - 1)], 0.0)
        return jnp.fft.rfft(kernel, axis=0)

    def spectrum(values):
        padded = jnp.concatenate([values, jnp.zeros_like(values)], axis=1)
        return jnp.fft.rfft(padded, axis=1)

    def inverse(product):
        return jnp.fft.irfft(product, n=N2, axis=1)[:, :CL]

    result = jnp.zeros((NCH, CL, C), jnp.float32)
    base = kernel_spectrum(0)
    leading = None
    for part in range(3):
        mask = (segment == part)[:, :, None]
        masked = jnp.where(mask, blocks, 0.0)
        spec_part = spectrum(masked)
        if part == 0:
            leading = spec_part
        result = result + jnp.where(mask, inverse(base[None] * spec_part), 0.0)
    tail_mask = (doc_index == last_doc[:, None])[:, :, None]
    for distance in range(1, REACH + 1):
        later = jnp.concatenate([leading[distance:], jnp.zeros_like(leading[:distance])], axis=0)
        later_first = jnp.concatenate([first_doc[distance:], jnp.full((distance,), -1, jnp.int32)])
        joined = (later_first == last_doc)[:, None, None]
        term = inverse(kernel_spectrum(distance)[None] * later)
        result = result + jnp.where(joined & tail_mask, term, 0.0)
    return fold(result)
```

```python
import functools
import math

import jax
import jax.numpy as jnp
import ml_dtypes
import numpy as np
from jax import lax
from jax.experimental import pallas as pl
from jax.experimental.pallas import tpu as pltpu
from jax.sharding import PartitionSpec as P

REACH = 3
LANES = 256
MIB = 1024 * 1024
F32 = jnp.float32
BF16 = jnp.bfloat16


def parts_of(table):
    high = table.astype(np.float32).astype(ml_dtypes.bfloat16)
    low = (table - high.astype(np.float64)).astype(np.float32).astype(ml_dtypes.bfloat16)
    return high, low


@functools.lru_cache(maxsize=None)
def tables(length):
    angle = np.outer(2 * np.arange(length) + 1, np.arange(length)) % (4 * length)
    angle = angle.astype(np.float64) * (math.pi / (2 * length))
    forward = np.concatenate([np.cos(angle), -np.sin(angle)], axis=0)
    high, low = parts_of(forward)
    stacked = np.concatenate([high, low], axis=0)
    back_high, back_low = parts_of(forward.T / length)
    return stacked, np.concatenate([back_high, back_low], axis=0)


def nn(a, b):
    return lax.dot_general(a, b, (((1,), (0,)), ((), ())), preferred_element_type=F32)


def nt(a, b):
    return lax.dot_general(a, b, (((1,), (1,)), ((), ())), preferred_element_type=F32)


def project_kernel(g_ref, w_ref, gate_ref, out_ref):
    total = nt(g_ref[...], w_ref[...])
    out_ref[...] = (total * gate_ref[...].astype(F32)).astype(BF16)


def project(gathered, weight, gate):
    rows, depth = gathered.shape
    width = weight.shape[0]
    tile = LANES
    return pl.pallas_call(
        project_kernel,
        grid=(width // tile,),
        out_shape=jax.ShapeDtypeStruct((rows, width), BF16),
        in_specs=[
            pl.BlockSpec((rows, depth), lambda c: (0, 0)),
            pl.BlockSpec((tile, depth), lambda c: (c, 0)),
            pl.BlockSpec((rows, tile), lambda c: (0, c)),
        ],
        out_specs=pl.BlockSpec((rows, tile), lambda c: (0, c)),
        compiler_params=pltpu.CompilerParams(vmem_limit_bytes=40 * MIB),
        cost_estimate=pl.CostEstimate(
            flops=2 * rows * depth * width,
            bytes_accessed=2 * (rows * depth + width * depth + 2 * rows * width),
            transcendentals=0,
        ),
    )(gathered, weight, gate)


def spectrum_kernel(table_ref, taps_ref, out_ref):
    length = table_ref.shape[1]
    table_high = table_ref[: 2 * length, :]
    table = table_ref[...]
    freq = lax.broadcasted_iota(jnp.int32, (length, 1), 0)
    sign = jnp.where(freq % 2 == 0, 1.0, -1.0).astype(F32)
    before = None
    for part in range(REACH + 1):
        if part < REACH:
            values = taps_ref[part * length : (part + 1) * length, :]
            high = values.astype(BF16)
            low = (values - high.astype(F32)).astype(BF16)
            both = nn(table, high)
            full = both[: 2 * length] + (both[2 * length :] + nn(table_high, low))
            real, imag = full[:length], -full[length:]
        else:
            real, imag = None, None
        if before is None:
            out_real, out_imag = real, imag
        else:
            turned_real, turned_imag = sign * before[1], -sign * before[0]
            if real is None:
                out_real, out_imag = turned_real, turned_imag
            else:
                out_real, out_imag = real + turned_real, imag + turned_imag
        out_ref[part, :length, :] = out_real
        out_ref[part, length:, :] = out_imag
        before = (real, imag)


def tap_spectra(table, taps):
    count, width = taps.shape
    length = count // REACH
    return pl.pallas_call(
        spectrum_kernel,
        grid=(width // LANES,),
        out_shape=jax.ShapeDtypeStruct((REACH + 1, 2 * length, width), F32),
        in_specs=[
            pl.BlockSpec((4 * length, length), lambda c: (0, 0)),
            pl.BlockSpec((count, LANES), lambda c: (0, c)),
        ],
        out_specs=pl.BlockSpec((REACH + 1, 2 * length, LANES), lambda c: (0, 0, c)),
        compiler_params=pltpu.CompilerParams(vmem_limit_bytes=40 * MIB),
        cost_estimate=pl.CostEstimate(
            flops=2 * 3 * 2 * count * length * width,
            bytes_accessed=4 * (count * width + 8 * length * width),
            transcendentals=0,
        ),
    )(table, taps)


def conv_kernel(pieces, with_alt, aliased, *refs):
    facts_ref, table_ref, back_ref, spec_ref = refs[:4]
    refs = refs[4:]
    own_refs, refs = refs[:pieces], refs[pieces:]
    halo_refs, refs = refs[: REACH * pieces], refs[REACH * pieces :]
    if with_alt:
        alt_refs, refs = refs[:REACH], refs[REACH:]
    if aliased:
        refs = refs[1:]
    out_ref, acc_ref = refs
    length = table_ref.shape[1]
    row = lax.broadcasted_iota(jnp.int32, (length, LANES), 0)

    def joined(some):
        if len(some) == 1:
            return some[0][...]
        return jnp.concatenate([one[...] for one in some], axis=0)

    def term(values, low, high, distance):
        kept = jnp.where((row >= low) & (row < high), values.astype(F32), 0.0).astype(BF16)
        both = nn(table_ref[...], kept)
        full = both[: 2 * length] + both[2 * length :]
        real, imag = full[:length], full[length:]
        k_real = spec_ref[distance, :length, :]
        k_imag = spec_ref[distance, length:, :]
        return k_real * real - k_imag * imag, k_real * imag + k_imag * real

    def back(real, imag):
        total = jnp.concatenate([real.astype(BF16), imag.astype(BF16)], axis=0)
        both = nn(back_ref[...], total)
        return both[:length] + both[length:]

    first_end, last_start = facts_ref[0], facts_ref[1]
    own = joined(own_refs)
    real, imag = term(own, last_start, length, 0)
    acc_ref[:length, :] = real
    acc_ref[length:, :] = imag
    for distance in range(1, REACH + 1):
        reach = facts_ref[1 + distance]

        @pl.when(reach > 0)
        def _(distance=distance, reach=reach):
            values = joined(halo_refs[(distance - 1) * pieces : distance * pieces])
            if with_alt:
                values = values.astype(F32) + alt_refs[distance - 1][...].astype(F32)
            real, imag = term(values, 0, reach, distance)
            acc_ref[:length, :] += real
            acc_ref[length:, :] += imag

    out_ref[0, 0] = back(acc_ref[:length, :], acc_ref[length:, :])

    @pl.when(last_start > 0)
    def _():
        signal = back(*term(own, 0, first_end, 0))
        out_ref[0, 0] = jnp.where(row < first_end, signal, out_ref[0, 0])

    @pl.when(last_start > first_end)
    def _():
        signal = back(*term(own, first_end, last_start, 0))
        keep = (row >= first_end) & (row < last_start)
        out_ref[0, 0] = jnp.where(keep, signal, out_ref[0, 0])


def convolve(slot, facts, table, back, spectra, own, halos, alts=None, result=None):
    length = table.shape[1]
    width = own[0].shape[1]
    pieces = len(own)
    piece_spec = pl.BlockSpec((length // pieces, LANES), lambda c: (0, c))
    operands = [facts, table, back, spectra, *own]
    for halo in halos:
        operands.extend(halo)
    specs = [
        pl.BlockSpec(memory_space=pltpu.SMEM),
        pl.BlockSpec((4 * length, length), lambda c: (0, 0)),
        pl.BlockSpec((2 * length, 2 * length), lambda c: (0, 0)),
        pl.BlockSpec((REACH + 1, 2 * length, LANES), lambda c: (0, 0, c)),
    ]
    specs += [piece_spec] * (pieces * (1 + REACH))
    if alts is not None:
        operands.extend(alts)
        specs += [pl.BlockSpec((length, LANES), lambda c: (0, c))] * REACH
    aliases = {}
    if result is not None:
        aliases = {len(operands): 0}
        operands.append(result)
        specs.append(pl.BlockSpec(memory_space=pl.ANY))
    return pl.pallas_call(
        functools.partial(conv_kernel, pieces, alts is not None, result is not None),
        grid=(width // LANES,),
        out_shape=jax.ShapeDtypeStruct((1, 2, length, width), F32),
        in_specs=specs,
        out_specs=pl.BlockSpec((1, 1, length, LANES), lambda c: (0, slot, 0, c)),
        scratch_shapes=[pltpu.VMEM((2 * length, LANES), F32)],
        input_output_aliases=aliases,
        compiler_params=pltpu.CompilerParams(vmem_limit_bytes=40 * MIB),
        cost_estimate=pl.CostEstimate(
            flops=2 * 10 * 2 * length * length * width,
            bytes_accessed=4 * (8 * length * width + 3 * length * width),
            transcendentals=0,
        ),
    )(*operands)


def shifted(value, steps):
    count = lax.axis_size("ctx")
    initial, last = (max(0, -steps), min(count, count - steps))
    return lax.ppermute(value, "ctx", [(source, source + steps) for source in range(initial, last)])


def block_facts(doc_starts, block, length, end):
    start = block * length

    def after(where):
        return jnp.min(jnp.where(doc_starts > where, doc_starts, end))

    first_end = jnp.clip(after(start) - start, 0, length)
    last_start = jnp.max(jnp.where(doc_starts <= start + length - 1, doc_starts, 0)) - start
    last_start = jnp.clip(last_start, 0, length)
    reaches = after(start + length - 1) - start
    facts = [first_end, last_start]
    facts += [jnp.clip(reaches - distance * length, 0, length) for distance in range(1, REACH + 1)]
    return jnp.stack(facts).astype(jnp.int32)


def on_device(grad_out, out_weight, gate, filter_taps, doc_starts):
    pairs = lax.axis_size("ctx")
    place = lax.axis_index("ctx")
    length = grad_out.shape[2]
    blocks = 2 * pairs
    table_np, back_np = tables(length)
    table, back = jnp.asarray(table_np), jnp.asarray(back_np)
    half = length // 2

    def gather(piece):
        return lax.all_gather(piece, "ch", axis=1, tiled=True)

    upper_in = gather(grad_out[0, 1])
    first_in = gather(grad_out[0, 0, :half])
    second_in = gather(grad_out[0, 0, half:])

    spectra = tap_spectra(table, filter_taps)
    lower_facts = block_facts(doc_starts, place, length, blocks * length)
    upper_facts = block_facts(doc_starts, blocks - 1 - place, length, blocks * length)

    upper = project(upper_in, out_weight, gate[0, 1])
    upper_halo = [shifted(upper, distance) for distance in range(1, REACH + 1)]
    fold_one = lax.ppermute(upper, "ctx", [(pairs - 1, pairs - 2)])
    fold_two = lax.ppermute(fold_one, "ctx", [(pairs - 2, pairs - 3)])
    result = convolve(
        1, upper_facts, table, back, spectra, [upper], [[halo] for halo in upper_halo]
    )
    last = place == pairs - 1
    alts = [
        jnp.where(last, upper, jnp.zeros_like(upper)),
        jnp.where(last, upper_halo[0], fold_one),
        jnp.where(last, upper_halo[1], jnp.where(place == pairs - 2, upper, fold_two)),
    ]

    first = project(first_in, out_weight, gate[0, 0, :half])
    first_halo = [shifted(first, -distance) for distance in range(1, REACH + 1)]
    second = project(second_in, out_weight, gate[0, 0, half:])
    second_halo = [shifted(second, -distance) for distance in range(1, REACH + 1)]
    halos = [list(both) for both in zip(first_halo, second_halo)]
    return convolve(
        0, lower_facts, table, back, spectra, [first, second], halos, alts, result
    )


def solution(mesh):
    in_specs = (
        P("ctx", None, None, "ch"),
        P("ch", None),
        P("ctx", None, None, "ch"),
        P(None, "ch"),
        P(),
    )
    out_specs = P("ctx", None, None, "ch")
    return jax.shard_map(
        on_device, mesh=mesh, in_specs=in_specs, out_specs=out_specs, check_vma=False
    )
```

```python
import functools
import math

import jax
import jax.numpy as jnp
import ml_dtypes
import numpy as np
from jax import lax
from jax.experimental import pallas as pl
from jax.experimental.pallas import tpu as pltpu
from jax.sharding import PartitionSpec as P

REACH = 3
LANES = 256
VMEM = 60 * 1024 * 1024
F32 = jnp.float32
BF16 = jnp.bfloat16


def parts_of(table):
    high = table.astype(np.float32).astype(ml_dtypes.bfloat16)
    low = (table - high.astype(np.float64)).astype(np.float32).astype(ml_dtypes.bfloat16)
    return high, low


@functools.lru_cache(maxsize=None)
def tables(length):
    angle = np.outer(2 * np.arange(length) + 1, np.arange(length)) % (4 * length)
    angle = angle.astype(np.float64) * (math.pi / (2 * length))
    forward = np.concatenate([np.cos(angle), -np.sin(angle)], axis=0)
    high, low = parts_of(forward)
    stacked = np.concatenate([high, low], axis=0)
    back_high, back_low = parts_of(forward.T / length)
    return stacked, np.concatenate([back_high, back_low], axis=0)


def nn(a, b):
    return lax.dot_general(a, b, (((1,), (0,)), ((), ())), preferred_element_type=F32)


def nt(a, b):
    return lax.dot_general(a, b, (((1,), (1,)), ((), ())), preferred_element_type=F32)


def project_kernel(place_ref, *refs):
    count = (len(refs) - 2) // 2
    gate_ref, out_ref = refs[-2:]
    total = nt(refs[0][...], refs[count][...])
    for step in range(1, count):
        total = total + nt(refs[step][...], refs[count + step][...])
    out_ref[...] = (total * gate_ref[...].astype(F32)).astype(BF16)


def project(place, shards, weight, gate):
    count = len(shards)
    rows, depth = shards[0].shape
    width = weight.shape[0]
    tile = LANES

    def weight_spec(step):
        return pl.BlockSpec((tile, depth), lambda c, at: (c, lax.rem(at[0] + count - step, count)))

    return pl.pallas_call(
        project_kernel,
        grid_spec=pltpu.PrefetchScalarGridSpec(
            num_scalar_prefetch=1,
            grid=(width // tile,),
            in_specs=[pl.BlockSpec((rows, depth), lambda c, at: (0, 0))] * count
            + [weight_spec(step) for step in range(count)]
            + [pl.BlockSpec((rows, tile), lambda c, at: (0, c))],
            out_specs=pl.BlockSpec((rows, tile), lambda c, at: (0, c)),
        ),
        out_shape=jax.ShapeDtypeStruct((rows, width), BF16),
        compiler_params=pltpu.CompilerParams(vmem_limit_bytes=VMEM),
        cost_estimate=pl.CostEstimate(
            flops=2 * rows * depth * count * width,
            bytes_accessed=2 * (rows * depth * count + width * depth * count + 2 * rows * width),
            transcendentals=0,
        ),
    )(place, *shards, *([weight] * count), gate)


def spectrum_kernel(table_ref, taps_ref, out_ref):
    length = table_ref.shape[1]
    table_high = table_ref[: 2 * length, :]
    table = table_ref[...]
    freq = lax.broadcasted_iota(jnp.int32, (length, 1), 0)
    sign = jnp.where(freq % 2 == 0, 1.0, -1.0).astype(F32)
    before = None
    for part in range(REACH + 1):
        if part < REACH:
            values = taps_ref[part * length : (part + 1) * length, :]
            high = values.astype(BF16)
            low = (values - high.astype(F32)).astype(BF16)
            both = nn(table, high)
            full = both[: 2 * length] + (both[2 * length :] + nn(table_high, low))
            real, imag = full[:length], -full[length:]
        else:
            real, imag = None, None
        if before is None:
            out_real, out_imag = real, imag
        else:
            turned_real, turned_imag = sign * before[1], -sign * before[0]
            if real is None:
                out_real, out_imag = turned_real, turned_imag
            else:
                out_real, out_imag = real + turned_real, imag + turned_imag
        out_ref[part, :length, :] = out_real
        out_ref[part, length:, :] = out_imag
        before = (real, imag)


def tap_spectra(table, taps):
    count, width = taps.shape
    length = count // REACH
    return pl.pallas_call(
        spectrum_kernel,
        grid=(width // LANES,),
        out_shape=jax.ShapeDtypeStruct((REACH + 1, 2 * length, width), F32),
        in_specs=[
            pl.BlockSpec((4 * length, length), lambda c: (0, 0)),
            pl.BlockSpec((count, LANES), lambda c: (0, c)),
        ],
        out_specs=pl.BlockSpec((REACH + 1, 2 * length, LANES), lambda c: (0, 0, c)),
        compiler_params=pltpu.CompilerParams(vmem_limit_bytes=VMEM),
        cost_estimate=pl.CostEstimate(
            flops=2 * 3 * 2 * count * length * width,
            bytes_accessed=4 * (count * width + 8 * length * width),
            transcendentals=0,
        ),
    )(table, taps)


def conv_kernel(pieces, with_alt, aliased, *refs):
    facts_ref, table_ref, back_ref, spec_ref = refs[:4]
    refs = refs[4:]
    own_refs, refs = refs[:pieces], refs[pieces:]
    halo_refs, refs = refs[: 4 * pieces], refs[4 * pieces :]
    if with_alt:
        alt_refs, refs = refs[:REACH], refs[REACH:]
    if aliased:
        refs = refs[1:]
    out_ref, acc_ref = refs
    length = table_ref.shape[1]
    row = lax.broadcasted_iota(jnp.int32, (length, LANES), 0)

    def joined(some):
        if len(some) == 1:
            return some[0][...]
        return jnp.concatenate([one[...] for one in some], axis=0)

    def halo(distance):
        two, swapped, mate, far = (
            halo_refs[at * pieces : (at + 1) * pieces] for at in range(4)
        )
        if distance == 2:
            return joined(two)
        inner = facts_ref[5] == 1
        if distance == 1:
            return jnp.where(inner, joined(mate), joined(swapped))
        return jnp.where(inner, joined(swapped), joined(far))

    def term(values, low, high, distance):
        kept = jnp.where((row >= low) & (row < high), values.astype(F32), 0.0).astype(BF16)
        both = nn(table_ref[...], kept)
        full = both[: 2 * length] + both[2 * length :]
        real, imag = full[:length], full[length:]
        k_real = spec_ref[distance, :length, :]
        k_imag = spec_ref[distance, length:, :]
        return k_real * real - k_imag * imag, k_real * imag + k_imag * real

    def back(real, imag):
        total = jnp.concatenate([real.astype(BF16), imag.astype(BF16)], axis=0)
        both = nn(back_ref[...], total)
        return both[:length] + both[length:]

    first_end, last_start = facts_ref[0], facts_ref[1]
    own = joined(own_refs)
    real, imag = term(own, last_start, length, 0)
    acc_ref[:length, :] = real
    acc_ref[length:, :] = imag
    for distance in range(1, REACH + 1):
        reach = facts_ref[1 + distance]

        @pl.when(reach > 0)
        def _(distance=distance, reach=reach):
            values = halo(distance)
            if with_alt:
                values = values.astype(F32) + alt_refs[distance - 1][...].astype(F32)
            real, imag = term(values, 0, reach, distance)
            acc_ref[:length, :] += real
            acc_ref[length:, :] += imag

    out_ref[0, 0] = back(acc_ref[:length, :], acc_ref[length:, :])

    @pl.when(last_start > 0)
    def _():
        signal = back(*term(own, 0, first_end, 0))
        out_ref[0, 0] = jnp.where(row < first_end, signal, out_ref[0, 0])

    @pl.when(last_start > first_end)
    def _():
        signal = back(*term(own, first_end, last_start, 0))
        keep = (row >= first_end) & (row < last_start)
        out_ref[0, 0] = jnp.where(keep, signal, out_ref[0, 0])


def convolve(slot, facts, table, back, spectra, own, halos, alts=None, result=None):
    length = table.shape[1]
    width = own[0].shape[1]
    pieces = len(own)
    piece_spec = pl.BlockSpec((length // pieces, LANES), lambda c: (0, c))
    operands = [facts, table, back, spectra, *own]
    for halo in halos:
        operands.extend(halo)
    specs = [
        pl.BlockSpec(memory_space=pltpu.SMEM),
        pl.BlockSpec((4 * length, length), lambda c: (0, 0)),
        pl.BlockSpec((2 * length, 2 * length), lambda c: (0, 0)),
        pl.BlockSpec((REACH + 1, 2 * length, LANES), lambda c: (0, 0, c)),
    ]
    specs += [piece_spec] * (pieces * 5)
    if alts is not None:
        operands.extend(alts)
        specs += [pl.BlockSpec((length, LANES), lambda c: (0, c))] * REACH
    aliases = {}
    if result is not None:
        aliases = {len(operands): 0}
        operands.append(result)
        specs.append(pl.BlockSpec(memory_space=pl.ANY))
    return pl.pallas_call(
        functools.partial(conv_kernel, pieces, alts is not None, result is not None),
        grid=(width // LANES,),
        out_shape=jax.ShapeDtypeStruct((1, 2, length, width), F32),
        in_specs=specs,
        out_specs=pl.BlockSpec((1, 1, length, LANES), lambda c: (0, slot, 0, c)),
        scratch_shapes=[pltpu.VMEM((2 * length, LANES), F32)],
        input_output_aliases=aliases,
        compiler_params=pltpu.CompilerParams(vmem_limit_bytes=VMEM),
        cost_estimate=pl.CostEstimate(
            flops=2 * 10 * 2 * length * length * width,
            bytes_accessed=4 * (8 * length * width + 3 * length * width),
            transcendentals=0,
        ),
    )(*operands)


def shifted(value, steps):
    count = lax.axis_size("ctx")
    initial, last = (max(0, -steps), min(count, count - steps))
    return lax.ppermute(value, "ctx", [(source, source + steps) for source in range(initial, last)])


def core_swapped(value):
    count = lax.axis_size("ctx")
    return lax.ppermute(value, "ctx", [(source, source ^ 1) for source in range(count)])


def halo_of(value, way):
    count = lax.axis_size("ctx")
    two = shifted(value, 2 * way)
    outer = 1 if way > 0 else 0
    far = [
        (source, source + 3 * way)
        for source in range(outer, count, 2)
        if 0 <= source + 3 * way < count
    ]
    return [two, core_swapped(two), core_swapped(value), lax.ppermute(value, "ctx", far)]


def block_facts(doc_starts, block, length, end, inner):
    start = block * length

    def after(where):
        return jnp.min(jnp.where(doc_starts > where, doc_starts, end))

    first_end = jnp.clip(after(start) - start, 0, length)
    last_start = jnp.max(jnp.where(doc_starts <= start + length - 1, doc_starts, 0)) - start
    last_start = jnp.clip(last_start, 0, length)
    reaches = after(start + length - 1) - start
    facts = [first_end, last_start]
    facts += [jnp.clip(reaches - distance * length, 0, length) for distance in range(1, REACH + 1)]
    facts.append(inner)
    return jnp.stack(facts).astype(jnp.int32)


def on_device(grad_out, out_weight, gate, filter_taps, doc_starts):
    pairs = lax.axis_size("ctx")
    place = lax.axis_index("ctx")
    length = grad_out.shape[2]
    blocks = 2 * pairs
    table_np, back_np = tables(length)
    table, back = jnp.asarray(table_np), jnp.asarray(back_np)
    half = length // 2
    count = lax.axis_size("ch")
    lane = lax.axis_index("ch").astype(jnp.int32)[None]
    around = [(source, (source + 1) % count) for source in range(count)]

    def ring(piece):
        shards = [piece]
        for _ in range(1, count):
            shards.append(lax.ppermute(shards[-1], "ch", around))
        return shards

    upper_in = ring(grad_out[0, 1])
    first_in = ring(grad_out[0, 0, :half])
    second_in = ring(grad_out[0, 0, half:])

    spectra = tap_spectra(table, filter_taps)
    odd = place % 2
    lower_facts = block_facts(doc_starts, place, length, blocks * length, 1 - odd)
    upper_facts = block_facts(doc_starts, blocks - 1 - place, length, blocks * length, odd)

    upper = project(lane, upper_in, out_weight, gate[0, 1])
    upper_halo = halo_of(upper, 1)
    result = convolve(
        1, upper_facts, table, back, spectra, [upper], [[halo] for halo in upper_halo]
    )
    last, near = place == pairs - 1, place == pairs - 2
    fold = lax.ppermute(upper, "ctx", [(pairs - 1, pairs - 3)])
    two, _, mate, _ = upper_halo
    nothing = jnp.zeros_like(upper)
    alts = [
        jnp.where(last, upper, nothing),
        jnp.where(last | near, mate, nothing),
        jnp.where(last, two, jnp.where(near, upper, fold)),
    ]

    first = project(lane, first_in, out_weight, gate[0, 0, :half])
    first_halo = halo_of(first, -1)
    second = project(lane, second_in, out_weight, gate[0, 0, half:])
    second_halo = halo_of(second, -1)
    halos = [list(both) for both in zip(first_halo, second_halo)]
    return convolve(
        0, lower_facts, table, back, spectra, [first, second], halos, alts, result
    )


def solution(mesh):
    in_specs = (
        P("ctx", None, None, "ch"),
        P("ch", None),
        P("ctx", None, None, "ch"),
        P(None, "ch"),
        P(),
    )
    out_specs = P("ctx", None, None, "ch")
    return jax.shard_map(
        on_device, mesh=mesh, in_specs=in_specs, out_specs=out_specs, check_vma=False
    )
```

```python
import functools
import math

import jax
import jax.numpy as jnp
import ml_dtypes
import numpy as np
from jax import lax
from jax.experimental import pallas as pl
from jax.experimental.pallas import tpu as pltpu
from jax.sharding import PartitionSpec as P

REACH = 3
LANES = 256
VMEM = 20 * 1024 * 1024
F32 = jnp.float32
BF16 = jnp.bfloat16
WHOLE = pl.BlockSpec(memory_space=pltpu.VMEM)
ANYWHERE = pl.BlockSpec(memory_space=pl.ANY)
SCALARS = pl.BlockSpec(memory_space=pltpu.SMEM)


def parts_of(table):
    high = table.astype(np.float32).astype(ml_dtypes.bfloat16)
    low = (table - high.astype(np.float64)).astype(np.float32).astype(ml_dtypes.bfloat16)
    return high, low


@functools.lru_cache(maxsize=None)
def tables(length):
    angle = np.outer(2 * np.arange(length) + 1, np.arange(length)) % (4 * length)
    angle = angle.astype(np.float64) * (math.pi / (2 * length))
    forward = np.concatenate([np.cos(angle), -np.sin(angle)], axis=0)
    high, low = parts_of(forward)
    stacked = np.concatenate([high, low], axis=0)
    back_high, back_low = parts_of(forward.T / length)
    return stacked, np.concatenate([back_high, back_low], axis=0)


def nn(a, b):
    return lax.dot_general(a, b, (((1,), (0,)), ((), ())), preferred_element_type=F32)


def nt(a, b):
    return lax.dot_general(a, b, (((1,), (1,)), ((), ())), preferred_element_type=F32)


def params():
    return pltpu.CompilerParams(vmem_limit_bytes=VMEM)


def lanes_at(tile):
    return pl.ds(pl.multiple_of(tile * LANES, LANES), LANES)


def prepare_kernel(*refs):
    table_ref, back_ref, taps_ref, weight_ref, gate_ref = refs[:5]
    spec_out, weight_out, gate_out, table_out, back_out, sems = refs[-6:]
    copies = [
        pltpu.make_async_copy(source, target, sems.at[at])
        for at, (source, target) in enumerate(
            [(weight_ref, weight_out), (gate_ref, gate_out), (back_ref, back_out)]
        )
    ]
    step = pl.program_id(0)

    @pl.when(step == 0)
    def _():
        for copy in copies:
            copy.start()
        table_out[...] = table_ref[...]

    length = table_ref.shape[1]
    freq = lax.broadcasted_iota(jnp.int32, (length, 1), 0)
    sign = jnp.where(freq % 2 == 0, 1.0, -1.0).astype(F32)
    lanes = lanes_at(step)
    before = None
    for part in range(REACH + 1):
        if part < REACH:
            values = taps_ref[part * length : (part + 1) * length, :]
            high = values.astype(BF16)
            low = (values - high.astype(F32)).astype(BF16)
            both = nn(table_ref[...], high)
            full = both[: 2 * length] + (both[2 * length :] + nn(table_ref[: 2 * length, :], low))
            now = (full[:length], -full[length:])
        else:
            now = None
        if before is None:
            real, imag = now
        else:
            real, imag = sign * before[1], -sign * before[0]
            if now is not None:
                real, imag = now[0] + real, now[1] + imag
        spec_out[part, :length, lanes] = real
        spec_out[part, length:, lanes] = imag
        before = now

    @pl.when(step == pl.num_programs(0) - 1)
    def _():
        for copy in copies:
            copy.wait()


def prepare(table, back, taps, weight, gate, after):
    count, width = taps.shape
    length = count // REACH
    return pl.pallas_call(
        prepare_kernel,
        grid=(width // LANES,),
        out_shape=(
            pltpu.VMEM((REACH + 1, 2 * length, width), F32),
            pltpu.VMEM(weight.shape, BF16),
            pltpu.VMEM(gate.shape, BF16),
            pltpu.VMEM(table.shape, BF16),
            pltpu.VMEM(back.shape, BF16),
        ),
        in_specs=[
            pl.BlockSpec((4 * length, length), lambda c: (0, 0)),
            ANYWHERE,
            pl.BlockSpec((count, LANES), lambda c: (0, c)),
            ANYWHERE,
            ANYWHERE,
        ]
        + [ANYWHERE] * len(after),
        out_specs=(WHOLE,) * 5,
        scratch_shapes=[pltpu.SemaphoreType.DMA((3,))],
        compiler_params=params(),
        cost_estimate=pl.CostEstimate(
            flops=2 * 3 * 2 * count * length * width,
            bytes_accessed=4 * (count * width + 8 * length * width),
            transcendentals=0,
        ),
    )(table, back, taps, weight, gate, *after)


def project_kernel(steps, slot, start, first, last, place_ref, *refs):
    shards, refs = refs[: len(steps)], refs[len(steps) :]
    weight_ref, gate_ref, out_ref = refs[0], refs[1], refs[-1]
    before_ref = None if first else refs[2]
    rows, depth = shards[0].shape
    count = weight_ref.shape[1] // depth
    for tile in range(weight_ref.shape[0] // LANES):
        lanes = pl.ds(tile * LANES, LANES)
        total = None if first else before_ref[:, lanes]
        for shard, step in zip(shards, steps):
            at = lax.rem(place_ref[0] + count - step, count)
            features = pl.ds(pl.multiple_of(at * depth, depth), depth)
            part = nt(shard[...], weight_ref[lanes, features])
            total = part if total is None else total + part
        if last:
            gate = gate_ref[0, slot, start : start + rows, lanes].astype(F32)
            out_ref[:, lanes] = (total * gate).astype(BF16)
        else:
            out_ref[:, lanes] = total


def project(place, shards, steps, weight, gate, slot, start, before=None, last=True, after=()):
    rows, depth = shards[0].shape
    width = weight.shape[0]
    operands = [place, *shards, weight, gate]
    if before is not None:
        operands.append(before)
    body = functools.partial(project_kernel, steps, slot, start, before is None, last)
    return pl.pallas_call(
        body,
        out_shape=pltpu.VMEM((rows, width), BF16 if last else F32),
        in_specs=[SCALARS] + [WHOLE] * (len(operands) - 1) + [ANYWHERE] * len(after),
        out_specs=WHOLE,
        compiler_params=params(),
        cost_estimate=pl.CostEstimate(
            flops=2 * rows * depth * len(shards) * width,
            bytes_accessed=2 * (rows + width) * depth * len(shards),
            transcendentals=0,
        ),
    )(*operands, *after)


class Conv:
    def __init__(self, facts, table, back, spectra):
        self.facts, self.table, self.back, self.spectra = facts, table, back, spectra
        self.length = table.shape[1]
        self.lanes = lanes_at(pl.program_id(0))
        self.row = lax.broadcasted_iota(jnp.int32, (self.length, LANES), 0)

    def joined(self, pieces):
        tiles = [piece[:, self.lanes] for piece in pieces]
        return tiles[0] if len(tiles) == 1 else jnp.concatenate(tiles, axis=0)

    def within(self, low, high):
        return (self.row >= low) & (self.row < high)

    def term(self, values, low, high, distance):
        length = self.length
        kept = jnp.where(self.within(low, high), values.astype(F32), 0.0).astype(BF16)
        both = nn(self.table[...], kept)
        full = both[: 2 * length] + both[2 * length :]
        real, imag = full[:length], full[length:]
        k_real = self.spectra[distance, :length, self.lanes]
        k_imag = self.spectra[distance, length:, self.lanes]
        return k_real * real - k_imag * imag, k_real * imag + k_imag * real

    def signal(self, real, imag):
        total = jnp.concatenate([real.astype(BF16), imag.astype(BF16)], axis=0)
        both = nn(self.back[...], total)
        return both[: self.length] + both[self.length :]

    def far_terms(self, acc, values_of):
        for distance in range(1, REACH + 1):
            reach = self.facts[1 + distance]

            @pl.when(reach > 0)
            def _(distance=distance, reach=reach):
                real, imag = self.term(values_of(distance), 0, reach, distance)
                acc[: self.length, :] += real
                acc[self.length :, :] += imag

    def inner_documents(self, own, read, write):
        first_end, last_start = self.facts[0], self.facts[1]

        @pl.when(last_start > 0)
        def _():
            signal = self.signal(*self.term(own, 0, first_end, 0))
            write(jnp.where(self.row < first_end, signal, read()))

        @pl.when(last_start > first_end)
        def _():
            signal = self.signal(*self.term(own, first_end, last_start, 0))
            write(jnp.where(self.within(first_end, last_start), signal, read()))

    def halo(self, pieces, distance):
        count = len(pieces) // 4
        two, swapped, mate, far = (pieces[at * count : (at + 1) * count] for at in range(4))
        if distance == 2:
            return self.joined(two)
        inner = self.facts[5] == 1
        if distance == 1:
            return jnp.where(inner, self.joined(mate), self.joined(swapped))
        return jnp.where(inner, self.joined(swapped), self.joined(far))


def upper_kernel(facts_ref, table_ref, back_ref, spec_ref, own_ref, *refs):
    halos, (out_ref, acc_ref) = refs[:4], refs[-2:]
    conv = Conv(facts_ref, table_ref, back_ref, spec_ref)
    own = conv.joined([own_ref])
    real, imag = conv.term(own, facts_ref[1], conv.length, 0)
    acc_ref[: conv.length, :] = real
    acc_ref[conv.length :, :] = imag
    conv.far_terms(acc_ref, lambda distance: conv.halo(halos, distance))
    out_ref[0, 0] = conv.signal(acc_ref[: conv.length, :], acc_ref[conv.length :, :])

    def write(value):
        out_ref[0, 0] = value

    conv.inner_documents(own, lambda: out_ref[0, 0], write)


def own_kernel(pieces, facts_ref, table_ref, back_ref, spec_ref, *refs):
    own_refs, out_ref = refs[:pieces], refs[-1]
    conv = Conv(facts_ref, table_ref, back_ref, spec_ref)
    own = conv.joined(own_refs)
    out_ref[:, conv.lanes] = conv.signal(*conv.term(own, facts_ref[1], conv.length, 0))

    def write(value):
        out_ref[:, conv.lanes] = value

    conv.inner_documents(own, lambda: out_ref[:, conv.lanes], write)


def far_kernel(pieces, facts_ref, table_ref, back_ref, spec_ref, *refs):
    near_ref, upper_ref, mate_ref, two_ref, fold_ref = refs[:5]
    halos = refs[5 : 5 + 4 * pieces]
    out_ref, acc_ref = refs[-2:]
    conv = Conv(facts_ref, table_ref, back_ref, spec_ref)
    role = facts_ref[6]

    def values_of(distance):
        value = conv.halo(halos, distance)
        if distance == 1:
            return jnp.where(role == 1, conv.joined([upper_ref]), value)
        if distance == 2:
            return jnp.where((role == 1) | (role == 2), conv.joined([mate_ref]), value)
        value = jnp.where(role == 1, conv.joined([two_ref]), value)
        value = jnp.where(role == 2, conv.joined([upper_ref]), value)
        return jnp.where(role == 3, conv.joined([fold_ref]), value)

    reaches = facts_ref[2] > 0

    @pl.when(reaches)
    def _():
        acc_ref[...] = jnp.zeros_like(acc_ref)
        conv.far_terms(acc_ref, values_of)
        signal = conv.signal(acc_ref[: conv.length, :], acc_ref[conv.length :, :])
        kept = jnp.where(conv.row >= facts_ref[1], signal, 0.0)
        out_ref[0, 0] = near_ref[:, conv.lanes] + kept

    @pl.when(jnp.logical_not(reaches))
    def _():
        out_ref[0, 0] = near_ref[:, conv.lanes]


def conv_call(body, tabs, facts, arrays, out_shape, out_spec, scratch, terms, after=(), result=None):
    table, back, spectra = tabs
    length = table.shape[1]
    width = spectra.shape[2]
    operands = [facts, table, back, spectra, *arrays]
    specs = [SCALARS] + [WHOLE] * (len(operands) - 1)
    operands.extend(after)
    specs += [ANYWHERE] * len(after)
    aliases = {}
    if result is not None:
        aliases = {len(operands): 0}
        operands.append(result)
        specs.append(ANYWHERE)
    return pl.pallas_call(
        body,
        grid=(width // LANES,),
        out_shape=out_shape,
        in_specs=specs,
        out_specs=out_spec,
        scratch_shapes=[pltpu.VMEM((2 * length, LANES), F32)] * scratch,
        input_output_aliases=aliases,
        compiler_params=params(),
        cost_estimate=pl.CostEstimate(
            flops=8 * terms * length * length * width,
            bytes_accessed=4 * length * width,
            transcendentals=0,
        ),
    )(*operands)


def shifted(value, steps):
    count = lax.axis_size("ctx")
    initial, last = (max(0, -steps), min(count, count - steps))
    return lax.ppermute(value, "ctx", [(source, source + steps) for source in range(initial, last)])


def core_swapped(value):
    count = lax.axis_size("ctx")
    return lax.ppermute(value, "ctx", [(source, source ^ 1) for source in range(count)])


def halo_of(value, way):
    count = lax.axis_size("ctx")
    two = shifted(value, 2 * way)
    outer = 1 if way > 0 else 0
    far = [
        (source, source + 3 * way)
        for source in range(outer, count, 2)
        if 0 <= source + 3 * way < count
    ]
    return [two, core_swapped(two), core_swapped(value), lax.ppermute(value, "ctx", far)]


def block_facts(doc_starts, block, length, end, inner, role):
    start = block * length

    def after(where):
        return jnp.min(jnp.where(doc_starts > where, doc_starts, end))

    first_end = jnp.clip(after(start) - start, 0, length)
    last_start = jnp.max(jnp.where(doc_starts <= start + length - 1, doc_starts, 0)) - start
    last_start = jnp.clip(last_start, 0, length)
    reaches = after(start + length - 1) - start
    facts = [first_end, last_start]
    facts += [jnp.clip(reaches - distance * length, 0, length) for distance in range(1, REACH + 1)]
    facts += [inner, role]
    return jnp.stack(facts).astype(jnp.int32)


def on_device(grad_out, out_weight, gate, filter_taps, doc_starts):
    pairs = lax.axis_size("ctx")
    place = lax.axis_index("ctx")
    length = grad_out.shape[2]
    width = out_weight.shape[0]
    blocks = 2 * pairs
    half = length // 2
    count = lax.axis_size("ch")
    lane = lax.axis_index("ch").astype(jnp.int32)[None]
    around = [(source, (source + 1) % count) for source in range(count)]
    everything = tuple(range(count))

    def ring(piece):
        shards = [piece]
        for _ in range(1, count):
            shards.append(lax.ppermute(shards[-1], "ch", around))
        return shards

    upper_in = ring(grad_out[0, 1])
    first_in = ring(grad_out[0, 0, :half])
    second_in = ring(grad_out[0, 0, half:])

    odd = place % 2
    role = jnp.where(place >= pairs - 3, pairs - place, 0)
    end = blocks * length
    lower_facts = block_facts(doc_starts, place, length, end, 1 - odd, role)
    upper_facts = block_facts(doc_starts, blocks - 1 - place, length, end, odd, role)
    table, back = (jnp.asarray(one) for one in tables(length))
    spectra, weight, gates, table, back = prepare(
        table, back, filter_taps, out_weight, gate, [lower_facts, upper_facts]
    )
    tabs = (table, back, spectra)

    upper = project(lane, upper_in, everything, weight, gates, 1, 0)
    upper_halo = halo_of(upper, 1)
    fold = lax.ppermute(upper, "ctx", [(pairs - 1, pairs - 3)])
    out_shape = jax.ShapeDtypeStruct((1, 2, length, width), F32)
    result = conv_call(
        upper_kernel,
        tabs,
        upper_facts,
        [upper, *upper_halo],
        out_shape,
        pl.BlockSpec((1, 1, length, LANES), lambda c: (0, 1, 0, c)),
        1,
        6,
    )

    first = project(lane, first_in, everything, weight, gates, 0, 0)
    first_halo = halo_of(first, -1)
    partial = project(
        lane, second_in[:-1], everything[:-1], weight, gates, 0, half, last=False
    )
    second = project(
        lane, second_in[-1:], everything[-1:], weight, gates, 0, half, partial, after=[result]
    )
    second_halo = halo_of(second, -1)
    near = conv_call(
        functools.partial(own_kernel, 2),
        tabs,
        lower_facts,
        [first, second],
        pltpu.VMEM((length, width), F32),
        WHOLE,
        0,
        4,
    )
    two, _, mate, _ = upper_halo
    halos = [piece for both in zip(first_halo, second_halo) for piece in both]
    return conv_call(
        functools.partial(far_kernel, 2),
        tabs,
        lower_facts,
        [near, upper, mate, two, fold, *halos],
        out_shape,
        pl.BlockSpec((1, 1, length, LANES), lambda c: (0, 0, 0, c)),
        1,
        4,
        result=result,
    )


def solution(mesh):
    in_specs = (
        P("ctx", None, None, "ch"),
        P("ch", None),
        P("ctx", None, None, "ch"),
        P(None, "ch"),
        P(),
    )
    out_specs = P("ctx", None, None, "ch")
    return jax.shard_map(
        on_device, mesh=mesh, in_specs=in_specs, out_specs=out_specs, check_vma=False
    )
```

```python
import functools
import math

import jax
import jax.numpy as jnp
import ml_dtypes
import numpy as np
from jax import lax
from jax.experimental import pallas as pl
from jax.experimental.pallas import tpu as pltpu
from jax.sharding import PartitionSpec as P

REACH = 3
LANES = 256
VMEM = 20 * 1024 * 1024
F32 = jnp.float32
BF16 = jnp.bfloat16
WHOLE = pl.BlockSpec(memory_space=pltpu.VMEM)
ANYWHERE = pl.BlockSpec(memory_space=pl.ANY)
OUTSIDE = pl.BlockSpec(memory_space=pltpu.HBM)
TOKEN = pl.BlockSpec((8, 128), lambda *at: (0, 0))
SCALARS = pl.BlockSpec(memory_space=pltpu.SMEM)


def parts_of(table):
    high = table.astype(np.float32).astype(ml_dtypes.bfloat16)
    low = (table - high.astype(np.float64)).astype(np.float32).astype(ml_dtypes.bfloat16)
    return high, low


@functools.lru_cache(maxsize=None)
def tables(length):
    angle = np.outer(2 * np.arange(length) + 1, np.arange(length)) % (4 * length)
    angle = angle.astype(np.float64) * (math.pi / (2 * length))
    forward = np.concatenate([np.cos(angle), -np.sin(angle)], axis=0)
    high, low = parts_of(forward)
    back_high, back_low = parts_of(forward.T / length)
    return np.concatenate([high, low], axis=1), np.concatenate([back_high, back_low], axis=1)


def nn(a, b):
    return lax.dot_general(a, b, (((1,), (0,)), ((), ())), preferred_element_type=F32)


def nt(a, b):
    return lax.dot_general(a, b, (((1,), (1,)), ((), ())), preferred_element_type=F32)


def params(limit=VMEM):
    return pltpu.CompilerParams(vmem_limit_bytes=limit)


def lanes_at(tile):
    return pl.ds(pl.multiple_of(tile * LANES, LANES), LANES)


def prepare_kernel(*refs):
    table_ref, back_ref, taps_ref, weight_ref, gate_ref = refs[:5]
    spec_out, weight_out, gate_out, table_out, back_out, token_out, sems = refs[-7:]
    token_out[...] = jnp.zeros_like(token_out)
    copies = [
        pltpu.make_async_copy(source, target, sems.at[at])
        for at, (source, target) in enumerate(
            [(weight_ref, weight_out), (gate_ref, gate_out), (back_ref, back_out)]
        )
    ]
    step = pl.program_id(0)

    @pl.when(step == 0)
    def _():
        for copy in copies:
            copy.start()
        table_out[...] = table_ref[...]

    length = table_ref.shape[1] // 2
    freq = lax.broadcasted_iota(jnp.int32, (length, 1), 0)
    sign = jnp.where(freq % 2 == 0, 1.0, -1.0).astype(F32)
    lanes = lanes_at(step)
    before = None
    for part in range(REACH + 1):
        if part < REACH:
            values = taps_ref[part * length : (part + 1) * length, :]
            high = values.astype(BF16)
            low = (values - high.astype(F32)).astype(BF16)
            full = nn(table_ref[...], jnp.concatenate([high, high], axis=0))
            full = full + nn(table_ref[:, :length], low)
            now = (full[:length], -full[length:])
        else:
            now = None
        if before is None:
            real, imag = now
        else:
            real, imag = sign * before[1], -sign * before[0]
            if now is not None:
                real, imag = now[0] + real, now[1] + imag
        spec_out[part, :length, lanes] = real
        spec_out[part, length:, lanes] = imag
        before = now

    @pl.when(step == pl.num_programs(0) - 1)
    def _():
        for copy in copies:
            copy.wait()


def prepare(table, back, taps, weight, gate, after):
    count, width = taps.shape
    length = count // REACH
    return pl.pallas_call(
        prepare_kernel,
        grid=(width // LANES,),
        out_shape=(
            pltpu.VMEM((REACH + 1, 2 * length, width), F32),
            pltpu.VMEM(weight.shape, BF16),
            pltpu.VMEM(gate.shape, BF16),
            pltpu.VMEM(table.shape, BF16),
            pltpu.VMEM(back.shape, BF16),
            jax.ShapeDtypeStruct((8, 128), F32),
        ),
        in_specs=[
            pl.BlockSpec((2 * length, 2 * length), lambda c: (0, 0)),
            OUTSIDE,
            pl.BlockSpec((count, LANES), lambda c: (0, c)),
            OUTSIDE,
            OUTSIDE,
        ]
        + [ANYWHERE] * len(after),
        out_specs=(WHOLE,) * 5 + (TOKEN,),
        scratch_shapes=[pltpu.SemaphoreType.DMA((3,))],
        compiler_params=params(2 * VMEM),
        cost_estimate=pl.CostEstimate(
            flops=2 * 3 * 2 * count * length * width,
            bytes_accessed=4 * (count * width + 8 * length * width),
            transcendentals=0,
        ),
    )(table, back, taps, weight, gate, *after)


def project_kernel(steps, slot, start, first, last, place_ref, *refs):
    shards, refs = refs[: len(steps)], refs[len(steps) :]
    weight_ref, gate_ref, out_ref = refs[0], refs[1], refs[-1]
    before_ref = None if first else refs[2]
    rows, depth = shards[0].shape
    count = weight_ref.shape[1] // depth
    for tile in range(weight_ref.shape[0] // LANES):
        lanes = pl.ds(tile * LANES, LANES)
        total = None if first else before_ref[:, lanes]
        for shard, step in zip(shards, steps):
            at = lax.rem(place_ref[0] + count - step, count)
            features = pl.ds(pl.multiple_of(at * depth, depth), depth)
            part = nt(shard[...], weight_ref[lanes, features])
            total = part if total is None else total + part
        if last:
            gate = gate_ref[0, slot, start : start + rows, lanes].astype(F32)
            out_ref[:, lanes] = (total * gate).astype(BF16)
        else:
            out_ref[:, lanes] = total


def project(place, shards, steps, weight, gate, slot, start, before=None, last=True, after=()):
    rows, depth = shards[0].shape
    width = weight.shape[0]
    operands = [place, *shards, weight, gate]
    if before is not None:
        operands.append(before)
    body = functools.partial(project_kernel, steps, slot, start, before is None, last)
    return pl.pallas_call(
        body,
        out_shape=pltpu.VMEM((rows, width), BF16 if last else F32),
        in_specs=[SCALARS] + [WHOLE] * (len(operands) - 1) + [ANYWHERE] * len(after),
        out_specs=WHOLE,
        compiler_params=params(),
        cost_estimate=pl.CostEstimate(
            flops=2 * rows * depth * len(shards) * width,
            bytes_accessed=2 * (rows + width) * depth * len(shards),
            transcendentals=0,
        ),
    )(*operands, *after)


class Conv:
    def __init__(self, facts, table, back, spectra):
        self.facts, self.table, self.back, self.spectra = facts, table, back, spectra
        self.length = table.shape[0] // 2
        self.lanes = lanes_at(pl.program_id(0))
        self.row = lax.broadcasted_iota(jnp.int32, (self.length, LANES), 0)

    def joined(self, pieces):
        tiles = [piece[:, self.lanes] for piece in pieces]
        return tiles[0] if len(tiles) == 1 else jnp.concatenate(tiles, axis=0)

    def within(self, low, high):
        return (self.row >= low) & (self.row < high)

    def term(self, values, low, high, distance):
        length = self.length
        kept = jnp.where(self.within(low, high), values.astype(F32), 0.0).astype(BF16)
        full = nn(self.table[...], jnp.concatenate([kept, kept], axis=0))
        real, imag = full[:length], full[length:]
        k_real = self.spectra[distance, :length, self.lanes]
        k_imag = self.spectra[distance, length:, self.lanes]
        return k_real * real - k_imag * imag, k_real * imag + k_imag * real

    def signal(self, real, imag):
        real, imag = real.astype(BF16), imag.astype(BF16)
        return nn(self.back[...], jnp.concatenate([real, imag, real, imag], axis=0))

    def far_terms(self, acc, values_of):
        for distance in range(1, REACH + 1):
            reach = self.facts[1 + distance]

            @pl.when(reach > 0)
            def _(distance=distance, reach=reach):
                real, imag = self.term(values_of(distance), 0, reach, distance)
                acc[: self.length, :] += real
                acc[self.length :, :] += imag

    def inner_documents(self, own, read, write):
        first_end, last_start = self.facts[0], self.facts[1]

        @pl.when(last_start > 0)
        def _():
            signal = self.signal(*self.term(own, 0, first_end, 0))
            write(jnp.where(self.row < first_end, signal, read()))

        @pl.when(last_start > first_end)
        def _():
            signal = self.signal(*self.term(own, first_end, last_start, 0))
            write(jnp.where(self.within(first_end, last_start), signal, read()))

    def halo(self, pieces, distance, mixed):
        sets = 3 if mixed else 4
        count = len(pieces) // sets
        kinds = [pieces[at * count : (at + 1) * count] for at in range(sets)]
        two, swapped, mate, far = kinds[0], kinds[1], kinds[2], kinds[-1]
        if distance == 2:
            return self.joined(two)
        inner = self.facts[5] == 1
        if distance == 1:
            return jnp.where(inner, self.joined(mate), self.joined(swapped))
        return jnp.where(inner, self.joined(swapped), self.joined(far))


def upper_kernel(facts_ref, table_ref, back_ref, spec_ref, own_ref, *refs):
    halos, (out_ref, token_ref, acc_ref) = refs[:4], refs[-3:]
    token_ref[...] = jnp.zeros_like(token_ref)
    conv = Conv(facts_ref, table_ref, back_ref, spec_ref)
    own = conv.joined([own_ref])
    real, imag = conv.term(own, facts_ref[1], conv.length, 0)
    acc_ref[: conv.length, :] = real
    acc_ref[conv.length :, :] = imag
    conv.far_terms(acc_ref, lambda distance: conv.halo(halos, distance, False))
    out_ref[0, 0] = conv.signal(acc_ref[: conv.length, :], acc_ref[conv.length :, :])

    def write(value):
        out_ref[0, 0] = value

    conv.inner_documents(own, lambda: out_ref[0, 0], write)


def own_kernel(pieces, facts_ref, table_ref, back_ref, spec_ref, *refs):
    own_refs, out_ref = refs[:pieces], refs[-1]
    conv = Conv(facts_ref, table_ref, back_ref, spec_ref)
    own = conv.joined(own_refs)
    out_ref[:, conv.lanes] = conv.signal(*conv.term(own, facts_ref[1], conv.length, 0))

    def write(value):
        out_ref[:, conv.lanes] = value

    conv.inner_documents(own, lambda: out_ref[:, conv.lanes], write)


def far_kernel(pieces, facts_ref, table_ref, back_ref, spec_ref, *refs):
    near_ref, upper_ref, mate_ref, two_ref, fold_ref = refs[:5]
    halos = refs[5 : 5 + 3 * pieces]
    out_ref, acc_ref = refs[-2:]
    conv = Conv(facts_ref, table_ref, back_ref, spec_ref)
    role = facts_ref[6]

    def values_of(distance):
        value = conv.halo(halos, distance, True)
        if distance == 1:
            return jnp.where(role == 1, conv.joined([upper_ref]), value)
        if distance == 2:
            return jnp.where((role == 1) | (role == 2), conv.joined([mate_ref]), value)
        value = jnp.where(role == 1, conv.joined([two_ref]), value)
        value = jnp.where(role == 2, conv.joined([upper_ref]), value)
        return jnp.where(role == 3, conv.joined([fold_ref]), value)

    reaches = facts_ref[2] > 0

    @pl.when(reaches)
    def _():
        acc_ref[...] = jnp.zeros_like(acc_ref)
        conv.far_terms(acc_ref, values_of)
        signal = conv.signal(acc_ref[: conv.length, :], acc_ref[conv.length :, :])
        kept = jnp.where(conv.row >= facts_ref[1], signal, 0.0)
        out_ref[0, 0] = near_ref[:, conv.lanes] + kept

    @pl.when(jnp.logical_not(reaches))
    def _():
        out_ref[0, 0] = near_ref[:, conv.lanes]


def conv_call(body, tabs, facts, arrays, out_shape, out_spec, scratch, terms, after=(), result=None):
    table, back, spectra = tabs
    length = table.shape[0] // 2
    width = spectra.shape[2]
    operands = [facts, table, back, spectra, *arrays]
    specs = [SCALARS] + [WHOLE] * (len(operands) - 1)
    operands.extend(after)
    specs += [ANYWHERE] * len(after)
    aliases = {}
    if result is not None:
        aliases = {len(operands): 0}
        operands.append(result)
        specs.append(ANYWHERE)
    return pl.pallas_call(
        body,
        grid=(width // LANES,),
        out_shape=out_shape,
        in_specs=specs,
        out_specs=out_spec,
        scratch_shapes=[pltpu.VMEM((2 * length, LANES), F32)] * scratch,
        input_output_aliases=aliases,
        compiler_params=params(),
        cost_estimate=pl.CostEstimate(
            flops=8 * terms * length * length * width,
            bytes_accessed=4 * length * width,
            transcendentals=0,
        ),
    )(*operands)


def ordered(value, *earlier):
    return pl.pallas_call(
        lambda *refs: None,
        out_shape=jax.ShapeDtypeStruct(value.shape, value.dtype),
        in_specs=[ANYWHERE] * (1 + len(earlier)),
        out_specs=ANYWHERE,
        input_output_aliases={0: 0},
    )(value, *earlier)


def shifted(value, steps):
    count = lax.axis_size("ctx")
    initial, last = (max(0, -steps), min(count, count - steps))
    return lax.ppermute(value, "ctx", [(source, source + steps) for source in range(initial, last)])


def core_swapped(value):
    count = lax.axis_size("ctx")
    return lax.ppermute(value, "ctx", [(source, source ^ 1) for source in range(count)])


def upper_halo_of(value):
    count = lax.axis_size("ctx")
    far = [(source, source + 3) for source in range(1, count - 3, 2)] + [(count - 1, count - 3)]
    two = shifted(value, 2)
    mate, far = core_swapped(value), lax.ppermute(value, "ctx", far)
    return [two, core_swapped(two), mate, far]


def lower_halo_of(value):
    count = lax.axis_size("ctx")
    mixed = [(source, source - 1) for source in range(1, count, 2)]
    mixed += [(source, source - 3) for source in range(4, count, 2)]
    two = shifted(value, -2)
    mixed = lax.ppermute(value, "ctx", mixed)
    return [two, core_swapped(two), mixed]


def block_facts(doc_starts, block, length, end, inner, role):
    start = block * length

    def after(where):
        return jnp.min(jnp.where(doc_starts > where, doc_starts, end))

    first_end = jnp.clip(after(start) - start, 0, length)
    last_start = jnp.max(jnp.where(doc_starts <= start + length - 1, doc_starts, 0)) - start
    last_start = jnp.clip(last_start, 0, length)
    reaches = after(start + length - 1) - start
    facts = [first_end, last_start]
    facts += [jnp.clip(reaches - distance * length, 0, length) for distance in range(1, REACH + 1)]
    facts += [inner, role]
    return jnp.stack(facts).astype(jnp.int32)


def on_device(grad_out, out_weight, gate, filter_taps, doc_starts):
    pairs = lax.axis_size("ctx")
    place = lax.axis_index("ctx")
    length = grad_out.shape[2]
    width = out_weight.shape[0]
    blocks = 2 * pairs
    half = length // 2
    count = lax.axis_size("ch")
    lane = lax.axis_index("ch").astype(jnp.int32)[None]
    around = [(source, (source + 1) % count) for source in range(count)]
    everything = tuple(range(count))

    def turned(piece):
        return lax.ppermute(piece, "ch", around)

    def ring(piece):
        shards = [piece]
        for _ in range(1, count):
            shards.append(turned(shards[-1]))
        return shards

    slices = [grad_out[0, 0, :half], grad_out[0, 0, half:]]
    upper_in = [grad_out[0, 1]]
    upper_in.append(turned(upper_in[0]))

    odd = place % 2
    role = jnp.where(place >= pairs - 3, pairs - place, 0)
    end = blocks * length
    lower_facts = block_facts(doc_starts, place, length, end, 1 - odd, role)
    upper_facts = block_facts(doc_starts, blocks - 1 - place, length, end, odd, role)
    table, back = (jnp.asarray(one) for one in tables(length))
    spectra, weight, gates, table, back, prepared = prepare(
        table, back, filter_taps, out_weight, gate, [lower_facts, upper_facts, *slices]
    )
    tabs = (table, back, spectra)

    upper_in[1] = ordered(upper_in[1], prepared)
    for step in range(2, count):
        upper_in.append(turned(upper_in[-1]))
    first_in = ring(ordered(slices[0], upper_in[-2]))
    second_in = ring(ordered(slices[1], upper_in[-1]))

    upper = project(lane, upper_in, everything, weight, gates, 1, 0, after=[first_in[1]])
    upper_halo = upper_halo_of(upper)
    out_shape = jax.ShapeDtypeStruct((1, 2, length, width), F32)
    result, convolved = conv_call(
        upper_kernel,
        tabs,
        upper_facts,
        [upper, *upper_halo],
        (out_shape, jax.ShapeDtypeStruct((8, 128), F32)),
        (pl.BlockSpec((1, 1, length, LANES), lambda c: (0, 1, 0, c)), TOKEN),
        1,
        6,
    )

    first = project(lane, first_in, everything, weight, gates, 0, 0)
    first_halo = lower_halo_of(first)
    partial = project(
        lane, second_in[:-1], everything[:-1], weight, gates, 0, half, last=False
    )
    second = project(
        lane, second_in[-1:], everything[-1:], weight, gates, 0, half, partial, after=[convolved]
    )
    second_halo = lower_halo_of(second)
    near = conv_call(
        functools.partial(own_kernel, 2),
        tabs,
        lower_facts,
        [first, second],
        pltpu.VMEM((length, width), F32),
        WHOLE,
        0,
        4,
    )
    two, _, mate, fold = upper_halo
    halos = [piece for both in zip(first_halo, second_halo) for piece in both]
    return conv_call(
        functools.partial(far_kernel, 2),
        tabs,
        lower_facts,
        [near, upper, mate, two, fold, *halos],
        out_shape,
        pl.BlockSpec((1, 1, length, LANES), lambda c: (0, 0, 0, c)),
        1,
        4,
        result=result,
    )


def solution(mesh):
    in_specs = (
        P("ctx", None, None, "ch"),
        P("ch", None),
        P("ctx", None, None, "ch"),
        P(None, "ch"),
        P(),
    )
    out_specs = P("ctx", None, None, "ch")
    return jax.shard_map(
        on_device, mesh=mesh, in_specs=in_specs, out_specs=out_specs, check_vma=False
    )
```

```python
import functools
import math

import jax
import jax.numpy as jnp
import ml_dtypes
import numpy as np
from jax import lax
from jax.experimental import pallas as pl
from jax.experimental.pallas import tpu as pltpu
from jax.sharding import PartitionSpec as P

REACH = 3
LANES = 256
VMEM = 20 * 1024 * 1024
F32 = jnp.float32
BF16 = jnp.bfloat16
WHOLE = pl.BlockSpec(memory_space=pltpu.VMEM)
ANYWHERE = pl.BlockSpec(memory_space=pl.ANY)
OUTSIDE = pl.BlockSpec(memory_space=pltpu.HBM)
TOKEN = pl.BlockSpec((8, 128), lambda *at: (0, 0))
SCALARS = pl.BlockSpec(memory_space=pltpu.SMEM)


def parts_of(table):
    high = table.astype(np.float32).astype(ml_dtypes.bfloat16)
    low = (table - high.astype(np.float64)).astype(np.float32).astype(ml_dtypes.bfloat16)
    return high, low


@functools.lru_cache(maxsize=None)
def tables(length):
    angle = np.outer(2 * np.arange(length) + 1, np.arange(length)) % (4 * length)
    angle = angle.astype(np.float64) * (math.pi / (2 * length))
    forward = np.concatenate([np.cos(angle), -np.sin(angle)], axis=0)
    high, low = parts_of(forward)
    back_high, back_low = parts_of(forward.T / length)
    return np.concatenate([high, low], axis=1), np.concatenate([back_high, back_low], axis=1)


def nn(a, b):
    return lax.dot_general(a, b, (((1,), (0,)), ((), ())), preferred_element_type=F32)


def nt(a, b):
    return lax.dot_general(a, b, (((1,), (1,)), ((), ())), preferred_element_type=F32)


def params():
    return pltpu.CompilerParams(vmem_limit_bytes=VMEM)


def lanes_at(tile):
    return pl.ds(pl.multiple_of(tile * LANES, LANES), LANES)


def write_facts(facts_ref, slot, docs_ref, block, length, end, inner, role):
    start = block * length
    stop = start + length - 1

    def visit(at, found):
        first, following, last = found
        here = docs_ref[at]
        first = jnp.minimum(first, jnp.where(here > start, here, end))
        following = jnp.minimum(following, jnp.where(here > stop, here, end))
        last = jnp.maximum(last, jnp.where(here <= stop, here, 0))
        return first, following, last

    whole = jnp.int32(end)
    first, following, last = lax.fori_loop(
        0, docs_ref.shape[0], visit, (whole, whole, jnp.int32(0))
    )
    facts_ref[slot, 0] = jnp.clip(first - start, 0, length)
    facts_ref[slot, 1] = jnp.clip(last - start, 0, length)
    for distance in range(1, REACH + 1):
        facts_ref[slot, 1 + distance] = jnp.clip(following - start - distance * length, 0, length)
    facts_ref[slot, 2 + REACH] = inner
    facts_ref[slot, 3 + REACH] = role


def prepare_kernel(pairs, *refs):
    place_ref, docs_ref, table_ref, back_ref, taps_ref, weight_ref, gate_ref = refs[:7]
    spec_out, weight_out, gate_out, table_out, back_out, facts_out, token_out, sems = refs[-8:]
    token_out[...] = jnp.zeros_like(token_out)
    copies = [
        pltpu.make_async_copy(source, target, sems.at[at])
        for at, (source, target) in enumerate(
            [(weight_ref, weight_out), (gate_ref, gate_out), (back_ref, back_out)]
        )
    ]
    step = pl.program_id(0)
    length = table_ref.shape[1] // 2

    @pl.when(step == 0)
    def _():
        for copy in copies:
            copy.start()
        table_out[...] = table_ref[:, :length]
        place = place_ref[0]
        odd = lax.rem(place, 2)
        role = jnp.where(place >= pairs - 3, pairs - place, 0)
        end = 2 * pairs * length
        write_facts(facts_out, 0, docs_ref, place, length, end, 1 - odd, role)
        write_facts(facts_out, 1, docs_ref, 2 * pairs - 1 - place, length, end, odd, role)

    freq = lax.broadcasted_iota(jnp.int32, (length, 1), 0)
    sign = jnp.where(freq % 2 == 0, 1.0, -1.0).astype(F32)
    lanes = lanes_at(step)
    before = None
    for part in range(REACH + 1):
        if part < REACH:
            values = taps_ref[part * length : (part + 1) * length, :]
            high = values.astype(BF16)
            low = (values - high.astype(F32)).astype(BF16)
            full = nn(table_ref[...], jnp.concatenate([high, high], axis=0))
            full = full + nn(table_ref[:, :length], low)
            now = (full[:length], -full[length:])
        else:
            now = None
        if before is None:
            real, imag = now
        else:
            real, imag = sign * before[1], -sign * before[0]
            if now is not None:
                real, imag = now[0] + real, now[1] + imag
        spec_out[part, :length, lanes] = real
        spec_out[part, length:, lanes] = imag
        before = now

    @pl.when(step == pl.num_programs(0) - 1)
    def _():
        for copy in copies:
            copy.wait()


def prepare(pairs, place, docs, table, back, taps, weight, gate, after):
    count, width = taps.shape
    length = count // REACH
    return pl.pallas_call(
        functools.partial(prepare_kernel, pairs),
        grid=(width // LANES,),
        out_shape=(
            pltpu.VMEM((REACH + 1, 2 * length, width), F32),
            pltpu.VMEM(weight.shape, BF16),
            pltpu.VMEM(gate.shape, BF16),
            pltpu.VMEM((2 * length, length), BF16),
            pltpu.VMEM(back.shape, BF16),
            jax.ShapeDtypeStruct((2, 8), jnp.int32),
            jax.ShapeDtypeStruct((8, 128), F32),
        ),
        in_specs=[
            SCALARS,
            SCALARS,
            pl.BlockSpec((2 * length, 2 * length), lambda c: (0, 0)),
            OUTSIDE,
            pl.BlockSpec((count, LANES), lambda c: (0, c)),
            OUTSIDE,
            OUTSIDE,
        ]
        + [ANYWHERE] * len(after),
        out_specs=(WHOLE,) * 5 + (SCALARS, TOKEN),
        scratch_shapes=[pltpu.SemaphoreType.DMA((3,))],
        compiler_params=params(),
        cost_estimate=pl.CostEstimate(
            flops=2 * 3 * 2 * count * length * width,
            bytes_accessed=4 * (count * width + 8 * length * width),
            transcendentals=0,
        ),
    )(place, docs, table, back, taps, weight, gate, *after)


def project_kernel(steps, slot, start, first, last, place_ref, *refs):
    shards, refs = refs[: len(steps)], refs[len(steps) :]
    weight_ref, gate_ref, out_ref = refs[0], refs[1], refs[-1]
    before_ref = None if first else refs[2]
    rows, depth = shards[0].shape
    count = weight_ref.shape[1] // depth
    for tile in range(weight_ref.shape[0] // LANES):
        lanes = pl.ds(tile * LANES, LANES)
        total = None if first else before_ref[:, lanes]
        for shard, step in zip(shards, steps):
            at = lax.rem(place_ref[0] + count - step, count)
            features = pl.ds(pl.multiple_of(at * depth, depth), depth)
            part = nt(shard[...], weight_ref[lanes, features])
            total = part if total is None else total + part
        if last:
            gate = gate_ref[0, slot, start : start + rows, lanes].astype(F32)
            out_ref[:, lanes] = (total * gate).astype(BF16)
        else:
            out_ref[:, lanes] = total


def project(place, shards, steps, weight, gate, slot, start, before=None, last=True, after=()):
    rows, depth = shards[0].shape
    width = weight.shape[0]
    operands = [place, *shards, weight, gate]
    if before is not None:
        operands.append(before)
    body = functools.partial(project_kernel, steps, slot, start, before is None, last)
    return pl.pallas_call(
        body,
        out_shape=pltpu.VMEM((rows, width), BF16 if last else F32),
        in_specs=[SCALARS] + [WHOLE] * (len(operands) - 1) + [ANYWHERE] * len(after),
        out_specs=WHOLE,
        compiler_params=params(),
        cost_estimate=pl.CostEstimate(
            flops=2 * rows * depth * len(shards) * width,
            bytes_accessed=2 * (rows + width) * depth * len(shards),
            transcendentals=0,
        ),
    )(*operands, *after)


class Conv:
    def __init__(self, slot, facts, table, back, spectra):
        self.facts = [facts[slot, at] for at in range(4 + REACH)]
        self.table, self.back, self.spectra = table, back, spectra
        self.length = table.shape[0] // 2
        self.lanes = lanes_at(pl.program_id(0))
        self.row = lax.broadcasted_iota(jnp.int32, (self.length, LANES), 0)

    def joined(self, pieces):
        tiles = [piece[:, self.lanes] for piece in pieces]
        return tiles[0] if len(tiles) == 1 else jnp.concatenate(tiles, axis=0)

    def within(self, low, high):
        return (self.row >= low) & (self.row < high)

    def term(self, values, low, high, distance):
        length = self.length
        kept = jnp.where(self.within(low, high), values.astype(F32), 0.0).astype(BF16)
        full = nn(self.table[...], kept)
        real, imag = full[:length], full[length:]
        k_real = self.spectra[distance, :length, self.lanes]
        k_imag = self.spectra[distance, length:, self.lanes]
        return k_real * real - k_imag * imag, k_real * imag + k_imag * real

    def signal(self, real, imag):
        real, imag = real.astype(BF16), imag.astype(BF16)
        return nn(self.back[...], jnp.concatenate([real, imag, real, imag], axis=0))

    def far_terms(self, acc, values_of):
        for distance in range(1, REACH + 1):
            reach = self.facts[1 + distance]

            @pl.when(reach > 0)
            def _(distance=distance, reach=reach):
                real, imag = self.term(values_of(distance), 0, reach, distance)
                acc[: self.length, :] += real
                acc[self.length :, :] += imag

    def inner_documents(self, own, read, write):
        first_end, last_start = self.facts[0], self.facts[1]

        @pl.when(last_start > 0)
        def _():
            signal = self.signal(*self.term(own, 0, first_end, 0))
            write(jnp.where(self.row < first_end, signal, read()))

        @pl.when(last_start > first_end)
        def _():
            signal = self.signal(*self.term(own, first_end, last_start, 0))
            write(jnp.where(self.within(first_end, last_start), signal, read()))

    def halo(self, pieces, distance, mixed):
        sets = 3 if mixed else 4
        count = len(pieces) // sets
        kinds = [pieces[at * count : (at + 1) * count] for at in range(sets)]
        two, swapped, mate, far = kinds[0], kinds[1], kinds[2], kinds[-1]
        if distance == 2:
            return self.joined(two)
        inner = self.facts[5] == 1
        if distance == 1:
            return jnp.where(inner, self.joined(mate), self.joined(swapped))
        return jnp.where(inner, self.joined(swapped), self.joined(far))


def upper_kernel(facts_ref, table_ref, back_ref, spec_ref, own_ref, *refs):
    halos, (out_ref, token_ref, acc_ref) = refs[:4], refs[-3:]
    token_ref[...] = jnp.zeros_like(token_ref)
    conv = Conv(1, facts_ref, table_ref, back_ref, spec_ref)
    own = conv.joined([own_ref])
    real, imag = conv.term(own, conv.facts[1], conv.length, 0)
    acc_ref[: conv.length, :] = real
    acc_ref[conv.length :, :] = imag
    conv.far_terms(acc_ref, lambda distance: conv.halo(halos, distance, False))
    out_ref[0, 0] = conv.signal(acc_ref[: conv.length, :], acc_ref[conv.length :, :])

    def write(value):
        out_ref[0, 0] = value

    conv.inner_documents(own, lambda: out_ref[0, 0], write)


def own_kernel(pieces, facts_ref, table_ref, back_ref, spec_ref, *refs):
    own_refs, out_ref = refs[:pieces], refs[-1]
    conv = Conv(0, facts_ref, table_ref, back_ref, spec_ref)
    own = conv.joined(own_refs)
    out_ref[:, conv.lanes] = conv.signal(*conv.term(own, conv.facts[1], conv.length, 0))

    def write(value):
        out_ref[:, conv.lanes] = value

    conv.inner_documents(own, lambda: out_ref[:, conv.lanes], write)


def far_kernel(pieces, facts_ref, table_ref, back_ref, spec_ref, *refs):
    near_ref, upper_ref, mate_ref, two_ref, fold_ref = refs[:5]
    halos = refs[5 : 5 + 3 * pieces]
    out_ref, acc_ref = refs[-2:]
    conv = Conv(0, facts_ref, table_ref, back_ref, spec_ref)
    role = conv.facts[6]

    def values_of(distance):
        value = conv.halo(halos, distance, True)
        if distance == 1:
            return jnp.where(role == 1, conv.joined([upper_ref]), value)
        if distance == 2:
            return jnp.where((role == 1) | (role == 2), conv.joined([mate_ref]), value)
        value = jnp.where(role == 1, conv.joined([two_ref]), value)
        value = jnp.where(role == 2, conv.joined([upper_ref]), value)
        return jnp.where(role == 3, conv.joined([fold_ref]), value)

    reaches = conv.facts[2] > 0

    @pl.when(reaches)
    def _():
        acc_ref[...] = jnp.zeros_like(acc_ref)
        conv.far_terms(acc_ref, values_of)
        signal = conv.signal(acc_ref[: conv.length, :], acc_ref[conv.length :, :])
        kept = jnp.where(conv.row >= conv.facts[1], signal, 0.0)
        out_ref[0, 0] = near_ref[:, conv.lanes] + kept

    @pl.when(jnp.logical_not(reaches))
    def _():
        out_ref[0, 0] = near_ref[:, conv.lanes]


def conv_call(body, tabs, facts, arrays, out_shape, out_spec, scratch, terms, after=(), result=None):
    table, back, spectra = tabs
    length = table.shape[0] // 2
    width = spectra.shape[2]
    operands = [facts, table, back, spectra, *arrays]
    specs = [SCALARS] + [WHOLE] * (len(operands) - 1)
    operands.extend(after)
    specs += [ANYWHERE] * len(after)
    aliases = {}
    if result is not None:
        aliases = {len(operands): 0}
        operands.append(result)
        specs.append(ANYWHERE)
    return pl.pallas_call(
        body,
        grid=(width // LANES,),
        out_shape=out_shape,
        in_specs=specs,
        out_specs=out_spec,
        scratch_shapes=[pltpu.VMEM((2 * length, LANES), F32)] * scratch,
        input_output_aliases=aliases,
        compiler_params=params(),
        cost_estimate=pl.CostEstimate(
            flops=8 * terms * length * length * width,
            bytes_accessed=4 * length * width,
            transcendentals=0,
        ),
    )(*operands)


def ordered(value, *earlier):
    return pl.pallas_call(
        lambda *refs: None,
        out_shape=jax.ShapeDtypeStruct(value.shape, value.dtype),
        in_specs=[ANYWHERE] * (1 + len(earlier)),
        out_specs=ANYWHERE,
        input_output_aliases={0: 0},
    )(value, *earlier)


def shifted(value, steps):
    count = lax.axis_size("ctx")
    initial, last = (max(0, -steps), min(count, count - steps))
    return lax.ppermute(value, "ctx", [(source, source + steps) for source in range(initial, last)])


def core_swapped(value):
    count = lax.axis_size("ctx")
    return lax.ppermute(value, "ctx", [(source, source ^ 1) for source in range(count)])


def upper_halo_of(value):
    count = lax.axis_size("ctx")
    far = [(source, source + 3) for source in range(1, count - 3, 2)] + [(count - 1, count - 3)]
    two = shifted(value, 2)
    mate, far = core_swapped(value), lax.ppermute(value, "ctx", far)
    return [two, core_swapped(two), mate, far]


def lower_halo_of(value):
    count = lax.axis_size("ctx")
    mixed = [(source, source - 1) for source in range(1, count, 2)]
    mixed += [(source, source - 3) for source in range(4, count, 2)]
    two = shifted(value, -2)
    mixed = lax.ppermute(value, "ctx", mixed)
    return [two, core_swapped(two), mixed]


def on_device(grad_out, out_weight, gate, filter_taps, doc_starts):
    pairs = lax.axis_size("ctx")
    place = lax.axis_index("ctx")
    length = grad_out.shape[2]
    width = out_weight.shape[0]
    cut = length * 5 // 8
    count = lax.axis_size("ch")
    lane = lax.axis_index("ch").astype(jnp.int32)[None]
    around = [(source, (source + 1) % count) for source in range(count)]
    everything = tuple(range(count))

    def turned(piece):
        return lax.ppermute(piece, "ch", around)

    slices = [grad_out[0, 0, :cut], grad_out[0, 0, cut:]]
    upper_in = [grad_out[0, 1]]
    upper_in.append(turned(upper_in[0]))

    table, back = (jnp.asarray(one) for one in tables(length))
    spectra, weight, gates, table, back, facts, prepared = prepare(
        pairs,
        place.astype(jnp.int32)[None],
        doc_starts,
        table,
        back,
        filter_taps,
        out_weight,
        gate,
        slices,
    )
    tabs = (table, back, spectra)

    upper_in[1] = ordered(upper_in[1], prepared)
    for step in range(2, count):
        upper_in.append(turned(upper_in[-1]))
    first_in = [ordered(slices[0], upper_in[-2])]
    for step in range(1, count):
        first_in.append(turned(first_in[-1]))
    second_in = [ordered(slices[1], upper_in[-1])]
    second_in.append(ordered(turned(second_in[0]), first_in[-1]))
    for step in range(2, count):
        second_in.append(turned(second_in[-1]))

    upper = project(lane, upper_in, everything, weight, gates, 1, 0, after=[first_in[1]])
    upper_halo = upper_halo_of(upper)
    out_shape = jax.ShapeDtypeStruct((1, 2, length, width), F32)
    result, convolved = conv_call(
        upper_kernel,
        tabs,
        facts,
        [upper, *upper_halo],
        (out_shape, jax.ShapeDtypeStruct((8, 128), F32)),
        (pl.BlockSpec((1, 1, length, LANES), lambda c: (0, 1, 0, c)), TOKEN),
        1,
        6,
    )

    first = project(lane, first_in, everything, weight, gates, 0, 0)
    first_halo = lower_halo_of(first)
    partial = project(
        lane, second_in[:-1], everything[:-1], weight, gates, 0, cut, last=False
    )
    second = project(
        lane, second_in[-1:], everything[-1:], weight, gates, 0, cut, partial, after=[convolved]
    )
    second_halo = lower_halo_of(second)
    near = conv_call(
        functools.partial(own_kernel, 2),
        tabs,
        facts,
        [first, second],
        pltpu.VMEM((length, width), F32),
        WHOLE,
        0,
        4,
    )
    two, _, mate, fold = upper_halo
    halos = [piece for both in zip(first_halo, second_halo) for piece in both]
    return conv_call(
        functools.partial(far_kernel, 2),
        tabs,
        facts,
        [near, upper, mate, two, fold, *halos],
        out_shape,
        pl.BlockSpec((1, 1, length, LANES), lambda c: (0, 0, 0, c)),
        1,
        4,
        result=result,
    )


def solution(mesh):
    in_specs = (
        P("ctx", None, None, "ch"),
        P("ch", None),
        P("ctx", None, None, "ch"),
        P(None, "ch"),
        P(),
    )
    out_specs = P("ctx", None, None, "ch")
    return jax.shard_map(
        on_device, mesh=mesh, in_specs=in_specs, out_specs=out_specs, check_vma=False
    )
```

```python
import functools
import math

import jax
import jax.numpy as jnp
import ml_dtypes
import numpy as np
from jax import lax
from jax.experimental import pallas as pl
from jax.experimental.pallas import tpu as pltpu
from jax.sharding import PartitionSpec as P

REACH = 3
LANES = 256
VMEM = 20 * 1024 * 1024
F32 = jnp.float32
BF16 = jnp.bfloat16
WHOLE = pl.BlockSpec(memory_space=pltpu.VMEM)
ANYWHERE = pl.BlockSpec(memory_space=pl.ANY)
OUTSIDE = pl.BlockSpec(memory_space=pltpu.HBM)
TOKEN = pl.BlockSpec((8, 128), lambda *at: (0, 0))
SCALARS = pl.BlockSpec(memory_space=pltpu.SMEM)


def parts_of(table):
    high = table.astype(np.float32).astype(ml_dtypes.bfloat16)
    low = (table - high.astype(np.float64)).astype(np.float32).astype(ml_dtypes.bfloat16)
    return high, low


@functools.lru_cache(maxsize=None)
def tables(length):
    angle = np.outer(2 * np.arange(length) + 1, np.arange(length)) % (4 * length)
    angle = angle.astype(np.float64) * (math.pi / (2 * length))
    forward = np.concatenate([np.cos(angle), -np.sin(angle)], axis=0)
    high, low = parts_of(forward)
    back_high, back_low = parts_of(forward.T / length)
    return np.concatenate([high, low], axis=1), np.concatenate([back_high, back_low], axis=1)


def nn(a, b):
    return lax.dot_general(a, b, (((1,), (0,)), ((), ())), preferred_element_type=F32)


def nt(a, b):
    return lax.dot_general(a, b, (((1,), (1,)), ((), ())), preferred_element_type=F32)


def params(limit=VMEM):
    return pltpu.CompilerParams(vmem_limit_bytes=limit)


def lanes_at(tile):
    return pl.ds(pl.multiple_of(tile * LANES, LANES), LANES)


def write_facts(facts_ref, slot, docs_ref, block, length, end, inner, role):
    start = block * length
    stop = start + length - 1

    def visit(at, found):
        first, following, last = found
        here = docs_ref[at]
        first = jnp.minimum(first, jnp.where(here > start, here, end))
        following = jnp.minimum(following, jnp.where(here > stop, here, end))
        last = jnp.maximum(last, jnp.where(here <= stop, here, 0))
        return first, following, last

    whole = jnp.int32(end)
    first, following, last = lax.fori_loop(
        0, docs_ref.shape[0], visit, (whole, whole, jnp.int32(0))
    )
    facts_ref[slot, 0] = jnp.clip(first - start, 0, length)
    facts_ref[slot, 1] = jnp.clip(last - start, 0, length)
    for distance in range(1, REACH + 1):
        facts_ref[slot, 1 + distance] = jnp.clip(following - start - distance * length, 0, length)
    facts_ref[slot, 2 + REACH] = inner
    facts_ref[slot, 3 + REACH] = role


def prepare_kernel(pairs, *refs):
    place_ref, docs_ref, table_ref, back_ref, taps_ref, weight_ref, gate_ref = refs[:7]
    spec_out, weight_out, gate_out, table_out, back_out, facts_out, token_out, sems = refs[-8:]
    token_out[...] = jnp.zeros_like(token_out)
    copies = [
        pltpu.make_async_copy(source, target, sems.at[at])
        for at, (source, target) in enumerate(
            [(weight_ref, weight_out), (gate_ref, gate_out), (back_ref, back_out)]
        )
    ]
    step = pl.program_id(0)
    length = table_ref.shape[1] // 2

    @pl.when(step == 0)
    def _():
        for copy in copies:
            copy.start()
        table_out[...] = table_ref[:, :length]
        place = place_ref[0]
        odd = lax.rem(place, 2)
        role = jnp.where(place >= pairs - 3, pairs - place, 0)
        end = 2 * pairs * length
        write_facts(facts_out, 0, docs_ref, place, length, end, 1 - odd, role)
        write_facts(facts_out, 1, docs_ref, 2 * pairs - 1 - place, length, end, odd, role)

    freq = lax.broadcasted_iota(jnp.int32, (length, 1), 0)
    sign = jnp.where(freq % 2 == 0, 1.0, -1.0).astype(F32)
    lanes = lanes_at(step)
    before = None
    for part in range(REACH + 1):
        if part < REACH:
            values = taps_ref[part * length : (part + 1) * length, :]
            high = values.astype(BF16)
            low = (values - high.astype(F32)).astype(BF16)
            full = nn(table_ref[...], jnp.concatenate([high, high], axis=0))
            full = full + nn(table_ref[:, :length], low)
            now = (full[:length], -full[length:])
        else:
            now = None
        if before is None:
            real, imag = now
        else:
            real, imag = sign * before[1], -sign * before[0]
            if now is not None:
                real, imag = now[0] + real, now[1] + imag
        spec_out[part, :length, lanes] = real
        spec_out[part, length:, lanes] = imag
        before = now

    @pl.when(step == pl.num_programs(0) - 1)
    def _():
        for copy in copies:
            copy.wait()


def prepare(pairs, place, docs, table, back, taps, weight, gate, after):
    count, width = taps.shape
    length = count // REACH
    return pl.pallas_call(
        functools.partial(prepare_kernel, pairs),
        grid=(width // LANES,),
        out_shape=(
            pltpu.VMEM((REACH + 1, 2 * length, width), F32),
            pltpu.VMEM(weight.shape, BF16),
            pltpu.VMEM(gate.shape, BF16),
            pltpu.VMEM((2 * length, length), BF16),
            pltpu.VMEM(back.shape, BF16),
            jax.ShapeDtypeStruct((2, 8), jnp.int32),
            jax.ShapeDtypeStruct((8, 128), F32),
        ),
        in_specs=[
            SCALARS,
            SCALARS,
            pl.BlockSpec((2 * length, 2 * length), lambda c: (0, 0)),
            OUTSIDE,
            pl.BlockSpec((count, LANES), lambda c: (0, c)),
            OUTSIDE,
            OUTSIDE,
        ]
        + [ANYWHERE] * len(after),
        out_specs=(WHOLE,) * 5 + (SCALARS, TOKEN),
        scratch_shapes=[pltpu.SemaphoreType.DMA((3,))],
        compiler_params=params(2 * VMEM),
        cost_estimate=pl.CostEstimate(
            flops=2 * 3 * 2 * count * length * width,
            bytes_accessed=4 * (count * width + 8 * length * width),
            transcendentals=0,
        ),
    )(place, docs, table, back, taps, weight, gate, *after)


def project_kernel(steps, slot, start, first, last, place_ref, *refs):
    shards, refs = refs[: len(steps)], refs[len(steps) :]
    weight_ref, gate_ref, out_ref = refs[0], refs[1], refs[-1]
    before_ref = None if first else refs[2]
    rows, depth = shards[0].shape
    count = weight_ref.shape[1] // depth
    for tile in range(weight_ref.shape[0] // LANES):
        lanes = pl.ds(tile * LANES, LANES)
        total = None if first else before_ref[:, lanes]
        for shard, step in zip(shards, steps):
            at = lax.rem(place_ref[0] + count - step, count)
            features = pl.ds(pl.multiple_of(at * depth, depth), depth)
            part = nt(shard[...], weight_ref[lanes, features])
            total = part if total is None else total + part
        if last:
            gate = gate_ref[0, slot, start : start + rows, lanes].astype(F32)
            out_ref[:, lanes] = (total * gate).astype(BF16)
        else:
            out_ref[:, lanes] = total


def project(place, shards, steps, weight, gate, slot, start, before=None, last=True, after=()):
    rows, depth = shards[0].shape
    width = weight.shape[0]
    operands = [place, *shards, weight, gate]
    if before is not None:
        operands.append(before)
    body = functools.partial(project_kernel, steps, slot, start, before is None, last)
    return pl.pallas_call(
        body,
        out_shape=pltpu.VMEM((rows, width), BF16 if last else F32),
        in_specs=[SCALARS] + [WHOLE] * (len(operands) - 1) + [ANYWHERE] * len(after),
        out_specs=WHOLE,
        compiler_params=params(),
        cost_estimate=pl.CostEstimate(
            flops=2 * rows * depth * len(shards) * width,
            bytes_accessed=2 * (rows + width) * depth * len(shards),
            transcendentals=0,
        ),
    )(*operands, *after)


class Conv:
    def __init__(self, slot, facts, table, back, spectra):
        self.facts = [facts[slot, at] for at in range(4 + REACH)]
        self.table, self.back, self.spectra = table, back, spectra
        self.length = table.shape[0] // 2
        self.lanes = lanes_at(pl.program_id(0))
        self.row = lax.broadcasted_iota(jnp.int32, (self.length, LANES), 0)

    def joined(self, pieces):
        tiles = [piece[:, self.lanes] for piece in pieces]
        return tiles[0] if len(tiles) == 1 else jnp.concatenate(tiles, axis=0)

    def within(self, low, high):
        return (self.row >= low) & (self.row < high)

    def term(self, values, low, high, distance):
        length = self.length
        kept = jnp.where(self.within(low, high), values.astype(F32), 0.0).astype(BF16)
        full = nn(self.table[...], kept)
        real, imag = full[:length], full[length:]
        k_real = self.spectra[distance, :length, self.lanes]
        k_imag = self.spectra[distance, length:, self.lanes]
        return k_real * real - k_imag * imag, k_real * imag + k_imag * real

    def signal(self, real, imag):
        real, imag = real.astype(BF16), imag.astype(BF16)
        return nn(self.back[...], jnp.concatenate([real, imag, real, imag], axis=0))

    def far_terms(self, acc, chosen, choices):
        for distance in range(1, REACH + 1):
            reach = self.facts[1 + distance]

            @pl.when(reach > 0)
            def _(distance=distance, reach=reach):
                for pieces, holds in choices(distance):

                    @pl.when(holds)
                    def _(pieces=pieces):
                        chosen[...] = self.joined(pieces)

                real, imag = self.term(chosen[...], 0, reach, distance)
                acc[: self.length, :] += real
                acc[self.length :, :] += imag

    def inner_documents(self, own, read, write):
        first_end, last_start = self.facts[0], self.facts[1]

        @pl.when(last_start > 0)
        def _():
            signal = self.signal(*self.term(own, 0, first_end, 0))
            write(jnp.where(self.row < first_end, signal, read()))

        @pl.when(last_start > first_end)
        def _():
            signal = self.signal(*self.term(own, first_end, last_start, 0))
            write(jnp.where(self.within(first_end, last_start), signal, read()))

    def halo(self, pieces, distance, mixed):
        sets = 3 if mixed else 4
        count = len(pieces) // sets
        kinds = [pieces[at * count : (at + 1) * count] for at in range(sets)]
        two, swapped, mate, far = kinds[0], kinds[1], kinds[2], kinds[-1]
        inner = self.facts[5]
        if distance == 2:
            return [(two, inner >= 0)]
        if distance == 1:
            return [(mate, inner == 1), (swapped, inner == 0)]
        return [(swapped, inner == 1), (far, inner == 0)]


def own_kernel(slot, pieces, facts_ref, table_ref, back_ref, spec_ref, *refs):
    own_refs, out_ref = refs[:pieces], refs[-1]
    conv = Conv(slot, facts_ref, table_ref, back_ref, spec_ref)
    own = conv.joined(own_refs)
    out_ref[:, conv.lanes] = conv.signal(*conv.term(own, conv.facts[1], conv.length, 0))

    def write(value):
        out_ref[:, conv.lanes] = value

    conv.inner_documents(own, lambda: out_ref[:, conv.lanes], write)


def far_kernel(slot, pieces, facts_ref, table_ref, back_ref, spec_ref, *refs):
    near_ref, refs = refs[0], refs[1:]
    if slot == 0:
        upper_ref, mate_ref, two_ref, fold_ref = refs[:4]
        halos = refs[4 : 4 + 3 * pieces]
    else:
        halos = refs[: 4 * pieces]
    out_ref, acc_ref, chosen_ref = refs[-3:]
    conv = Conv(slot, facts_ref, table_ref, back_ref, spec_ref)
    role = conv.facts[6]

    def choices(distance):
        found = conv.halo(halos, distance, slot == 0)
        if slot == 0:
            folded = {
                1: [([upper_ref], role == 1)],
                2: [([mate_ref], (role == 1) | (role == 2))],
                3: [([two_ref], role == 1), ([upper_ref], role == 2), ([fold_ref], role == 3)],
            }
            found = found + folded[distance]
        return found

    reaches = conv.facts[2] > 0

    @pl.when(reaches)
    def _():
        acc_ref[...] = jnp.zeros_like(acc_ref)
        conv.far_terms(acc_ref, chosen_ref, choices)
        signal = conv.signal(acc_ref[: conv.length, :], acc_ref[conv.length :, :])
        kept = jnp.where(conv.row >= conv.facts[1], signal, 0.0)
        out_ref[0, 0] = near_ref[:, conv.lanes] + kept

    @pl.when(jnp.logical_not(reaches))
    def _():
        out_ref[0, 0] = near_ref[:, conv.lanes]


def conv_call(body, tabs, facts, arrays, out_shape, out_spec, scratch, terms, result=None):
    table, back, spectra = tabs
    length = table.shape[0] // 2
    width = spectra.shape[2]
    operands = [facts, table, back, spectra, *arrays]
    specs = [SCALARS] + [WHOLE] * (len(operands) - 1)
    aliases = {}
    if result is not None:
        aliases = {len(operands): 0}
        operands.append(result)
        specs.append(ANYWHERE)
    return pl.pallas_call(
        body,
        grid=(width // LANES,),
        out_shape=out_shape,
        in_specs=specs,
        out_specs=out_spec,
        scratch_shapes=scratch,
        input_output_aliases=aliases,
        compiler_params=params(),
        cost_estimate=pl.CostEstimate(
            flops=4 * terms * length * length * width,
            bytes_accessed=4 * length * width,
            transcendentals=0,
        ),
    )(*operands)


def own_terms(slot, tabs, facts, pieces):
    _, back, spectra = tabs
    shape = pltpu.VMEM((back.shape[0], spectra.shape[2]), F32)
    body = functools.partial(own_kernel, slot, len(pieces))
    return conv_call(body, tabs, facts, pieces, shape, WHOLE, [], 8)


def far_terms(slot, count, tabs, facts, arrays, result=None):
    _, back, spectra = tabs
    length, width = back.shape[0], spectra.shape[2]
    shape = jax.ShapeDtypeStruct((1, 2, length, width), F32)
    spec = pl.BlockSpec((1, 1, length, LANES), lambda c: (0, slot, 0, c))
    scratch = [pltpu.VMEM((2 * length, LANES), F32), pltpu.VMEM((length, LANES), BF16)]
    body = functools.partial(far_kernel, slot, count)
    return conv_call(body, tabs, facts, arrays, shape, spec, scratch, 8, result)


def ordered(value, *earlier):
    return pl.pallas_call(
        lambda *refs: None,
        out_shape=jax.ShapeDtypeStruct(value.shape, value.dtype),
        in_specs=[ANYWHERE] * (1 + len(earlier)),
        out_specs=ANYWHERE,
        input_output_aliases={0: 0},
        compiler_params=params(VMEM // 20),
    )(value, *earlier)


def shifted(value, steps):
    count = lax.axis_size("ctx")
    initial, last = (max(0, -steps), min(count, count - steps))
    return lax.ppermute(value, "ctx", [(source, source + steps) for source in range(initial, last)])


def core_swapped(value):
    count = lax.axis_size("ctx")
    return lax.ppermute(value, "ctx", [(source, source ^ 1) for source in range(count)])


def upper_halo_of(value):
    count = lax.axis_size("ctx")
    far = [(source, source + 3) for source in range(1, count - 3, 2)] + [(count - 1, count - 3)]
    two = shifted(value, 2)
    mate, far = core_swapped(value), lax.ppermute(value, "ctx", far)
    return [two, core_swapped(two), mate, far]


def lower_halo_of(value):
    count = lax.axis_size("ctx")
    mixed = [(source, source - 1) for source in range(1, count, 2)]
    mixed += [(source, source - 3) for source in range(4, count, 2)]
    two = shifted(value, -2)
    mixed = lax.ppermute(value, "ctx", mixed)
    return [two, core_swapped(two), mixed]


def on_device(grad_out, out_weight, gate, filter_taps, doc_starts):
    pairs = lax.axis_size("ctx")
    place = lax.axis_index("ctx")
    length = grad_out.shape[2]
    width = out_weight.shape[0]
    cut = length * 5 // 8
    count = lax.axis_size("ch")
    lane = lax.axis_index("ch").astype(jnp.int32)[None]
    around = [(source, (source + 1) % count) for source in range(count)]
    everything = tuple(range(count))

    def turned(piece):
        return lax.ppermute(piece, "ch", around)

    slices = [grad_out[0, 0, :cut], grad_out[0, 0, cut:]]
    upper_in = [grad_out[0, 1]]
    upper_in.append(turned(upper_in[0]))

    table, back = (jnp.asarray(one) for one in tables(length))
    spectra, weight, gates, table, back, facts, prepared = prepare(
        pairs,
        place.astype(jnp.int32)[None],
        doc_starts,
        table,
        back,
        filter_taps,
        out_weight,
        gate,
        slices,
    )
    tabs = (table, back, spectra)

    upper_in[1] = ordered(upper_in[1], prepared)
    for step in range(2, count):
        upper_in.append(turned(upper_in[-1]))
    first_in = [ordered(slices[0], upper_in[-2])]
    for step in range(1, count):
        first_in.append(turned(first_in[-1]))
    second_in = [ordered(slices[1], upper_in[-1])]
    second_in.append(ordered(turned(second_in[0]), first_in[-1]))
    for step in range(2, count):
        second_in.append(turned(second_in[-1]))

    upper = project(lane, upper_in, everything, weight, gates, 1, 0, after=[first_in[1]])
    upper_halo = upper_halo_of(upper)
    near = own_terms(1, tabs, facts, [upper])
    result = far_terms(1, 1, tabs, facts, [near, *upper_halo])

    first = project(lane, first_in, everything, weight, gates, 0, 0)
    first_halo = lower_halo_of(first)
    partial = project(lane, second_in[:-1], everything[:-1], weight, gates, 0, cut, last=False)
    second = project(lane, second_in[-1:], everything[-1:], weight, gates, 0, cut, partial)
    second_halo = lower_halo_of(second)
    near = own_terms(0, tabs, facts, [first, second])
    two, _, mate, fold = upper_halo
    halos = [piece for both in zip(first_halo, second_halo) for piece in both]
    return far_terms(0, 2, tabs, facts, [near, upper, mate, two, fold, *halos], result)


def solution(mesh):
    in_specs = (
        P("ctx", None, None, "ch"),
        P("ch", None),
        P("ctx", None, None, "ch"),
        P(None, "ch"),
        P(),
    )
    out_specs = P("ctx", None, None, "ch")
    return jax.shard_map(
        on_device, mesh=mesh, in_specs=in_specs, out_specs=out_specs, check_vma=False
    )
```

```python
import functools
import math

import jax
import jax.numpy as jnp
import ml_dtypes
import numpy as np
from jax import lax
from jax.experimental import pallas as pl
from jax.experimental.pallas import tpu as pltpu
from jax.sharding import PartitionSpec as P

REACH = 3
LANES = 256
VMEM = 20 * 1024 * 1024
F32 = jnp.float32
BF16 = jnp.bfloat16
WHOLE = pl.BlockSpec(memory_space=pltpu.VMEM)
ANYWHERE = pl.BlockSpec(memory_space=pl.ANY)
OUTSIDE = pl.BlockSpec(memory_space=pltpu.HBM)
TOKEN = pl.BlockSpec((8, 128), lambda *at: (0, 0))
SCALARS = pl.BlockSpec(memory_space=pltpu.SMEM)


def parts_of(table):
    high = table.astype(np.float32).astype(ml_dtypes.bfloat16)
    low = (table - high.astype(np.float64)).astype(np.float32).astype(ml_dtypes.bfloat16)
    return high, low


@functools.lru_cache(maxsize=None)
def tables(length):
    angle = np.outer(2 * np.arange(length) + 1, np.arange(length)) % (4 * length)
    angle = angle.astype(np.float64) * (math.pi / (2 * length))
    forward = np.concatenate([np.cos(angle), -np.sin(angle)], axis=0)
    high, low = parts_of(forward)
    back_high, back_low = parts_of(forward.T / length)
    return np.concatenate([high, low], axis=1), np.concatenate([back_high, back_low], axis=1)


def nn(a, b):
    return lax.dot_general(a, b, (((1,), (0,)), ((), ())), preferred_element_type=F32)


def nt(a, b):
    return lax.dot_general(a, b, (((1,), (1,)), ((), ())), preferred_element_type=F32)


def params(limit=VMEM):
    return pltpu.CompilerParams(vmem_limit_bytes=limit)


def lanes_at(tile):
    return pl.ds(pl.multiple_of(tile * LANES, LANES), LANES)


def write_facts(facts_ref, slot, docs_ref, block, length, end, inner, role):
    start = block * length
    stop = start + length - 1

    def visit(at, found):
        first, following, last = found
        here = docs_ref[at]
        first = jnp.minimum(first, jnp.where(here > start, here, end))
        following = jnp.minimum(following, jnp.where(here > stop, here, end))
        last = jnp.maximum(last, jnp.where(here <= stop, here, 0))
        return first, following, last

    whole = jnp.int32(end)
    first, following, last = lax.fori_loop(
        0, docs_ref.shape[0], visit, (whole, whole, jnp.int32(0))
    )
    facts_ref[slot, 0] = jnp.clip(first - start, 0, length)
    facts_ref[slot, 1] = jnp.clip(last - start, 0, length)
    for distance in range(1, REACH + 1):
        facts_ref[slot, 1 + distance] = jnp.clip(following - start - distance * length, 0, length)
    facts_ref[slot, 2 + REACH] = inner
    facts_ref[slot, 3 + REACH] = role


def prepare_kernel(pairs, *refs):
    place_ref, docs_ref, table_ref, back_ref, taps_ref, weight_ref, gate_ref = refs[:7]
    spec_out, weight_out, gate_out, table_out, back_out, facts_out, token_out, sems = refs[-8:]
    token_out[...] = jnp.zeros_like(token_out)
    copies = [
        pltpu.make_async_copy(source, target, sems.at[at])
        for at, (source, target) in enumerate(
            [(weight_ref, weight_out), (gate_ref, gate_out), (back_ref, back_out)]
        )
    ]
    step = pl.program_id(0)
    length = table_ref.shape[1] // 2

    @pl.when(step == 0)
    def _():
        for copy in copies:
            copy.start()
        table_out[...] = table_ref[:, :length]
        place = place_ref[0]
        odd = lax.rem(place, 2)
        role = jnp.where(place >= pairs - 3, pairs - place, 0)
        end = 2 * pairs * length
        write_facts(facts_out, 0, docs_ref, place, length, end, 1 - odd, role)
        write_facts(facts_out, 1, docs_ref, 2 * pairs - 1 - place, length, end, odd, role)

    freq = lax.broadcasted_iota(jnp.int32, (length, 1), 0)
    sign = jnp.where(freq % 2 == 0, 1.0, -1.0).astype(F32)
    lanes = lanes_at(step)
    before = None
    for part in range(REACH + 1):
        if part < REACH:
            values = taps_ref[part * length : (part + 1) * length, :]
            high = values.astype(BF16)
            low = (values - high.astype(F32)).astype(BF16)
            full = nn(table_ref[...], jnp.concatenate([high, high], axis=0))
            full = full + nn(table_ref[:, :length], low)
            now = (full[:length], -full[length:])
        else:
            now = None
        if before is None:
            real, imag = now
        else:
            real, imag = sign * before[1], -sign * before[0]
            if now is not None:
                real, imag = now[0] + real, now[1] + imag
        spec_out[part, :length, lanes] = real
        spec_out[part, length:, lanes] = imag
        before = now

    @pl.when(step == pl.num_programs(0) - 1)
    def _():
        for copy in copies:
            copy.wait()


def prepare(pairs, place, docs, table, back, taps, weight, gate, after):
    count, width = taps.shape
    length = count // REACH
    return pl.pallas_call(
        functools.partial(prepare_kernel, pairs),
        grid=(width // LANES,),
        out_shape=(
            pltpu.VMEM((REACH + 1, 2 * length, width), F32),
            pltpu.VMEM(weight.shape, BF16),
            pltpu.VMEM(gate.shape, BF16),
            pltpu.VMEM((2 * length, length), BF16),
            pltpu.VMEM(back.shape, BF16),
            jax.ShapeDtypeStruct((2, 8), jnp.int32),
            jax.ShapeDtypeStruct((8, 128), F32),
        ),
        in_specs=[
            SCALARS,
            SCALARS,
            pl.BlockSpec((2 * length, 2 * length), lambda c: (0, 0)),
            OUTSIDE,
            pl.BlockSpec((count, LANES), lambda c: (0, c)),
            OUTSIDE,
            OUTSIDE,
        ]
        + [ANYWHERE] * len(after),
        out_specs=(WHOLE,) * 5 + (SCALARS, TOKEN),
        scratch_shapes=[pltpu.SemaphoreType.DMA((3,))],
        compiler_params=params(),
        cost_estimate=pl.CostEstimate(
            flops=2 * 3 * 2 * count * length * width,
            bytes_accessed=4 * (count * width + 8 * length * width),
            transcendentals=0,
        ),
    )(place, docs, table, back, taps, weight, gate, *after)


def project_kernel(steps, slot, start, first, last, place_ref, *refs):
    shards, refs = refs[: len(steps)], refs[len(steps) :]
    weight_ref, gate_ref, out_ref = refs[0], refs[1], refs[-1]
    before_ref = None if first else refs[2]
    rows, depth = shards[0].shape
    count = weight_ref.shape[1] // depth
    for tile in range(weight_ref.shape[0] // LANES):
        lanes = pl.ds(tile * LANES, LANES)
        total = None if first else before_ref[:, lanes]
        for shard, step in zip(shards, steps):
            at = lax.rem(place_ref[0] + count - step, count)
            features = pl.ds(pl.multiple_of(at * depth, depth), depth)
            part = nt(shard[...], weight_ref[lanes, features])
            total = part if total is None else total + part
        if last:
            gate = gate_ref[0, slot, start : start + rows, lanes].astype(F32)
            out_ref[:, lanes] = (total * gate).astype(BF16)
        else:
            out_ref[:, lanes] = total


def project(place, shards, steps, weight, gate, slot, start, before=None, last=True, after=()):
    rows, depth = shards[0].shape
    width = weight.shape[0]
    operands = [place, *shards, weight, gate]
    if before is not None:
        operands.append(before)
    body = functools.partial(project_kernel, steps, slot, start, before is None, last)
    return pl.pallas_call(
        body,
        out_shape=pltpu.VMEM((rows, width), BF16 if last else F32),
        in_specs=[SCALARS] + [WHOLE] * (len(operands) - 1) + [ANYWHERE] * len(after),
        out_specs=WHOLE,
        compiler_params=params(),
        cost_estimate=pl.CostEstimate(
            flops=2 * rows * depth * len(shards) * width,
            bytes_accessed=2 * (rows + width) * depth * len(shards),
            transcendentals=0,
        ),
    )(*operands, *after)


class Conv:
    def __init__(self, slot, facts, table, back, spectra):
        self.facts = [facts[slot, at] for at in range(4 + REACH)]
        self.table, self.back, self.spectra = table, back, spectra
        self.length = table.shape[0] // 2
        self.lanes = lanes_at(pl.program_id(0))
        self.row = lax.broadcasted_iota(jnp.int32, (self.length, LANES), 0)

    def joined(self, pieces):
        tiles = [piece[:, self.lanes] for piece in pieces]
        return tiles[0] if len(tiles) == 1 else jnp.concatenate(tiles, axis=0)

    def within(self, low, high):
        return (self.row >= low) & (self.row < high)

    def term(self, values, low, high, distance):
        length = self.length
        kept = jnp.where(self.within(low, high), values.astype(F32), 0.0).astype(BF16)
        full = nn(self.table[...], kept)
        real, imag = full[:length], full[length:]
        k_real = self.spectra[distance, :length, self.lanes]
        k_imag = self.spectra[distance, length:, self.lanes]
        return k_real * real - k_imag * imag, k_real * imag + k_imag * real

    def signal(self, real, imag):
        real, imag = real.astype(BF16), imag.astype(BF16)
        return nn(self.back[...], jnp.concatenate([real, imag, real, imag], axis=0))

    def far_terms(self, acc, chosen, choices):
        for distance in range(1, REACH + 1):
            reach = self.facts[1 + distance]

            @pl.when(reach > 0)
            def _(distance=distance, reach=reach):
                for pieces, holds in choices(distance):

                    @pl.when(holds)
                    def _(pieces=pieces):
                        chosen[...] = self.joined(pieces)

                real, imag = self.term(chosen[...], 0, reach, distance)
                acc[: self.length, :] += real
                acc[self.length :, :] += imag

    def inner_documents(self, own, read, write):
        first_end, last_start = self.facts[0], self.facts[1]

        @pl.when(last_start > 0)
        def _():
            signal = self.signal(*self.term(own, 0, first_end, 0))
            write(jnp.where(self.row < first_end, signal, read()))

        @pl.when(last_start > first_end)
        def _():
            signal = self.signal(*self.term(own, first_end, last_start, 0))
            write(jnp.where(self.within(first_end, last_start), signal, read()))

    def halo(self, pieces, distance, mixed):
        sets = 3 if mixed else 4
        count = len(pieces) // sets
        kinds = [pieces[at * count : (at + 1) * count] for at in range(sets)]
        two, swapped, mate, far = kinds[0], kinds[1], kinds[2], kinds[-1]
        inner = self.facts[5]
        if distance == 2:
            return [(two, inner >= 0)]
        if distance == 1:
            return [(mate, inner == 1), (swapped, inner == 0)]
        return [(swapped, inner == 1), (far, inner == 0)]


def own_kernel(slot, pieces, facts_ref, table_ref, back_ref, spec_ref, *refs):
    own_refs, out_ref = refs[:pieces], refs[-1]
    conv = Conv(slot, facts_ref, table_ref, back_ref, spec_ref)
    own = conv.joined(own_refs)
    out_ref[:, conv.lanes] = conv.signal(*conv.term(own, conv.facts[1], conv.length, 0))

    def write(value):
        out_ref[:, conv.lanes] = value

    conv.inner_documents(own, lambda: out_ref[:, conv.lanes], write)


def far_kernel(slot, pieces, facts_ref, table_ref, back_ref, spec_ref, *refs):
    near_ref, refs = refs[0], refs[1:]
    if slot == 0:
        upper_ref, mate_ref, two_ref, fold_ref = refs[:4]
        halos = refs[4 : 4 + 3 * pieces]
    else:
        halos = refs[: 4 * pieces]
    out_ref, acc_ref, chosen_ref = refs[-3:]
    conv = Conv(slot, facts_ref, table_ref, back_ref, spec_ref)
    role = conv.facts[6]

    def choices(distance):
        found = conv.halo(halos, distance, slot == 0)
        if slot == 0:
            folded = {
                1: [([upper_ref], role == 1)],
                2: [([mate_ref], (role == 1) | (role == 2))],
                3: [([two_ref], role == 1), ([upper_ref], role == 2), ([fold_ref], role == 3)],
            }
            found = found + folded[distance]
        return found

    reaches = conv.facts[2] > 0

    @pl.when(reaches)
    def _():
        acc_ref[...] = jnp.zeros_like(acc_ref)
        conv.far_terms(acc_ref, chosen_ref, choices)
        signal = conv.signal(acc_ref[: conv.length, :], acc_ref[conv.length :, :])
        kept = jnp.where(conv.row >= conv.facts[1], signal, 0.0)
        out_ref[0, 0] = near_ref[:, conv.lanes] + kept

    @pl.when(jnp.logical_not(reaches))
    def _():
        out_ref[0, 0] = near_ref[:, conv.lanes]


def conv_call(body, tabs, facts, arrays, out_shape, out_spec, scratch, terms, result=None):
    table, back, spectra = tabs
    length = table.shape[0] // 2
    width = spectra.shape[2]
    operands = [facts, table, back, spectra, *arrays]
    specs = [SCALARS] + [WHOLE] * (len(operands) - 1)
    aliases = {}
    if result is not None:
        aliases = {len(operands): 0}
        operands.append(result)
        specs.append(ANYWHERE)
    return pl.pallas_call(
        body,
        grid=(width // LANES,),
        out_shape=out_shape,
        in_specs=specs,
        out_specs=out_spec,
        scratch_shapes=scratch,
        input_output_aliases=aliases,
        compiler_params=params(),
        cost_estimate=pl.CostEstimate(
            flops=4 * terms * length * length * width,
            bytes_accessed=4 * length * width,
            transcendentals=0,
        ),
    )(*operands)


def own_terms(slot, tabs, facts, pieces):
    _, back, spectra = tabs
    shape = pltpu.VMEM((back.shape[0], spectra.shape[2]), F32)
    body = functools.partial(own_kernel, slot, len(pieces))
    return conv_call(body, tabs, facts, pieces, shape, WHOLE, [], 8)


def far_terms(slot, count, tabs, facts, arrays, result=None):
    _, back, spectra = tabs
    length, width = back.shape[0], spectra.shape[2]
    shape = jax.ShapeDtypeStruct((1, 2, length, width), F32)
    spec = pl.BlockSpec((1, 1, length, LANES), lambda c: (0, slot, 0, c))
    scratch = [pltpu.VMEM((2 * length, LANES), F32), pltpu.VMEM((length, LANES), BF16)]
    body = functools.partial(far_kernel, slot, count)
    return conv_call(body, tabs, facts, arrays, shape, spec, scratch, 8, result)


def ordered(value, *earlier):
    return pl.pallas_call(
        lambda *refs: None,
        out_shape=jax.ShapeDtypeStruct(value.shape, value.dtype),
        in_specs=[ANYWHERE] * (1 + len(earlier)),
        out_specs=ANYWHERE,
        input_output_aliases={0: 0},
        compiler_params=params(VMEM // 20),
    )(value, *earlier)


def shifted(value, steps):
    count = lax.axis_size("ctx")
    initial, last = (max(0, -steps), min(count, count - steps))
    return lax.ppermute(value, "ctx", [(source, source + steps) for source in range(initial, last)])


def core_swapped(value):
    count = lax.axis_size("ctx")
    return lax.ppermute(value, "ctx", [(source, source ^ 1) for source in range(count)])


def upper_halo_of(value):
    count = lax.axis_size("ctx")
    far = [(source, source + 3) for source in range(1, count - 3, 2)] + [(count - 1, count - 3)]
    two = shifted(value, 2)
    mate, far = core_swapped(value), lax.ppermute(value, "ctx", far)
    return [two, core_swapped(two), mate, far]


def lower_halo_of(value):
    count = lax.axis_size("ctx")
    mixed = [(source, source - 1) for source in range(1, count, 2)]
    mixed += [(source, source - 3) for source in range(4, count, 2)]
    two = shifted(value, -2)
    mixed = lax.ppermute(value, "ctx", mixed)
    return [two, core_swapped(two), mixed]


def on_device(grad_out, out_weight, gate, filter_taps, doc_starts):
    pairs = lax.axis_size("ctx")
    place = lax.axis_index("ctx")
    length = grad_out.shape[2]
    width = out_weight.shape[0]
    cut = length * 5 // 8
    count = lax.axis_size("ch")
    lane = lax.axis_index("ch").astype(jnp.int32)[None]
    around = [(source, (source + 1) % count) for source in range(count)]
    everything = tuple(range(count))

    def turned(piece):
        return lax.ppermute(piece, "ch", around)

    slices = [grad_out[0, 0, :cut], grad_out[0, 0, cut:]]
    upper_in = [grad_out[0, 1]]
    upper_in.append(turned(upper_in[0]))

    table, back = (jnp.asarray(one) for one in tables(length))
    spectra, weight, gates, table, back, facts, prepared = prepare(
        pairs,
        place.astype(jnp.int32)[None],
        doc_starts,
        table,
        back,
        filter_taps,
        out_weight,
        gate,
        slices,
    )
    tabs = (table, back, spectra)

    for step in range(2, count):
        upper_in.append(turned(upper_in[-1]))
    upper_in[-2] = ordered(upper_in[-2], prepared)
    upper_in[-1] = turned(upper_in[-2])
    first_in = [ordered(slices[0], upper_in[-2])]
    for step in range(1, count):
        first_in.append(turned(first_in[-1]))
    second_in = [ordered(slices[1], upper_in[-1])]
    second_in.append(ordered(turned(second_in[0]), first_in[-1]))
    for step in range(2, count):
        second_in.append(turned(second_in[-1]))

    upper = project(lane, upper_in, everything, weight, gates, 1, 0, after=[first_in[1]])
    upper_halo = upper_halo_of(upper)
    near = own_terms(1, tabs, facts, [upper])
    result = far_terms(1, 1, tabs, facts, [near, *upper_halo])

    first = project(lane, first_in, everything, weight, gates, 0, 0)
    first_halo = lower_halo_of(first)
    partial = project(lane, second_in[:-1], everything[:-1], weight, gates, 0, cut, last=False)
    second = project(lane, second_in[-1:], everything[-1:], weight, gates, 0, cut, partial)
    second_halo = lower_halo_of(second)
    near = own_terms(0, tabs, facts, [first, second])
    two, _, mate, fold = upper_halo
    halos = [piece for both in zip(first_halo, second_halo) for piece in both]
    return far_terms(0, 2, tabs, facts, [near, upper, mate, two, fold, *halos], result)


def solution(mesh):
    in_specs = (
        P("ctx", None, None, "ch"),
        P("ch", None),
        P("ctx", None, None, "ch"),
        P(None, "ch"),
        P(),
    )
    out_specs = P("ctx", None, None, "ch")
    return jax.shard_map(
        on_device, mesh=mesh, in_specs=in_specs, out_specs=out_specs, check_vma=False
    )
```

```python
import functools
import math

import jax
import jax.numpy as jnp
import ml_dtypes
import numpy as np
from jax import lax
from jax.experimental import pallas as pl
from jax.experimental.pallas import tpu as pltpu
from jax.sharding import PartitionSpec as P

REACH = 3
LANES = 256
VMEM = 20 * 1024 * 1024
F32 = jnp.float32
BF16 = jnp.bfloat16
WHOLE = pl.BlockSpec(memory_space=pltpu.VMEM)
ANYWHERE = pl.BlockSpec(memory_space=pl.ANY)
OUTSIDE = pl.BlockSpec(memory_space=pltpu.HBM)
TOKEN = pl.BlockSpec((8, 128), lambda *at: (0, 0))
SCALARS = pl.BlockSpec(memory_space=pltpu.SMEM)


def parts_of(table):
    high = table.astype(np.float32).astype(ml_dtypes.bfloat16)
    low = (table - high.astype(np.float64)).astype(np.float32).astype(ml_dtypes.bfloat16)
    return high, low


@functools.lru_cache(maxsize=None)
def tables(length):
    angle = np.outer(2 * np.arange(length) + 1, np.arange(length)) % (4 * length)
    angle = angle.astype(np.float64) * (math.pi / (2 * length))
    forward = np.concatenate([np.cos(angle), -np.sin(angle)], axis=0)
    high, low = parts_of(forward)
    back_high, back_low = parts_of(forward.T / length)
    return np.concatenate([high, low], axis=1), np.concatenate([back_high, back_low], axis=1)


def nn(a, b):
    return lax.dot_general(a, b, (((1,), (0,)), ((), ())), preferred_element_type=F32)


def nt(a, b):
    return lax.dot_general(a, b, (((1,), (1,)), ((), ())), preferred_element_type=F32)


def params(limit=VMEM):
    return pltpu.CompilerParams(vmem_limit_bytes=limit)


def lanes_at(tile):
    return pl.ds(pl.multiple_of(tile * LANES, LANES), LANES)


def write_facts(facts_ref, slot, docs_ref, block, length, end, inner, role):
    start = block * length
    stop = start + length - 1

    def visit(at, found):
        first, following, last = found
        here = docs_ref[at]
        first = jnp.minimum(first, jnp.where(here > start, here, end))
        following = jnp.minimum(following, jnp.where(here > stop, here, end))
        last = jnp.maximum(last, jnp.where(here <= stop, here, 0))
        return first, following, last

    whole = jnp.int32(end)
    first, following, last = lax.fori_loop(
        0, docs_ref.shape[0], visit, (whole, whole, jnp.int32(0))
    )
    facts_ref[slot, 0] = jnp.clip(first - start, 0, length)
    facts_ref[slot, 1] = jnp.clip(last - start, 0, length)
    for distance in range(1, REACH + 1):
        facts_ref[slot, 1 + distance] = jnp.clip(following - start - distance * length, 0, length)
    facts_ref[slot, 2 + REACH] = inner
    facts_ref[slot, 3 + REACH] = role


def prepare_kernel(pairs, *refs):
    place_ref, lane_ref, docs_ref, table_ref, back_ref, taps_ref, weight_ref, gate_ref = refs[:8]
    spec_out, weight_out, gate_out, table_out, back_out, facts_out, token_out, sems = refs[-8:]
    token_out[...] = jnp.zeros_like(token_out)
    copies = [
        pltpu.make_async_copy(source, target, sems.at[at])
        for at, (source, target) in enumerate(
            [(weight_ref, weight_out), (gate_ref, gate_out), (back_ref, back_out)]
        )
    ]
    step = pl.program_id(0)
    length = table_ref.shape[1] // 2

    @pl.when(step == 0)
    def _():
        for copy in copies:
            copy.start()
        table_out[...] = table_ref[:, :length]
        place = place_ref[0]
        odd = lax.rem(place, 2)
        role = jnp.where(place >= pairs - 3, pairs - place, 0)
        end = 2 * pairs * length
        for slot in range(2):
            facts_out[slot, 4 + REACH] = lane_ref[0]
        write_facts(facts_out, 0, docs_ref, place, length, end, 1 - odd, role)
        write_facts(facts_out, 1, docs_ref, 2 * pairs - 1 - place, length, end, odd, role)

    freq = lax.broadcasted_iota(jnp.int32, (length, 1), 0)
    sign = jnp.where(freq % 2 == 0, 1.0, -1.0).astype(F32)
    lanes = lanes_at(step)
    before = None
    for part in range(REACH + 1):
        if part < REACH:
            values = taps_ref[part * length : (part + 1) * length, :]
            high = values.astype(BF16)
            low = (values - high.astype(F32)).astype(BF16)
            full = nn(table_ref[...], jnp.concatenate([high, high], axis=0))
            full = full + nn(table_ref[:, :length], low)
            now = (full[:length], -full[length:])
        else:
            now = None
        if before is None:
            real, imag = now
        else:
            real, imag = sign * before[1], -sign * before[0]
            if now is not None:
                real, imag = now[0] + real, now[1] + imag
        spec_out[part, :length, lanes] = real
        spec_out[part, length:, lanes] = imag
        before = now

    @pl.when(step == pl.num_programs(0) - 1)
    def _():
        for copy in copies:
            copy.wait()


def prepare(pairs, place, lane, docs, table, back, taps, weight, gate, after):
    count, width = taps.shape
    length = count // REACH
    return pl.pallas_call(
        functools.partial(prepare_kernel, pairs),
        grid=(width // LANES,),
        out_shape=(
            pltpu.VMEM((REACH + 1, 2 * length, width), F32),
            pltpu.VMEM(weight.shape, BF16),
            pltpu.VMEM(gate.shape, BF16),
            pltpu.VMEM((2 * length, length), BF16),
            pltpu.VMEM(back.shape, BF16),
            jax.ShapeDtypeStruct((2, 8), jnp.int32),
            jax.ShapeDtypeStruct((8, 128), F32),
        ),
        in_specs=[
            SCALARS,
            SCALARS,
            SCALARS,
            pl.BlockSpec((2 * length, 2 * length), lambda c: (0, 0)),
            OUTSIDE,
            pl.BlockSpec((count, LANES), lambda c: (0, c)),
            OUTSIDE,
            OUTSIDE,
        ]
        + [ANYWHERE] * len(after),
        out_specs=(WHOLE,) * 5 + (SCALARS, TOKEN),
        scratch_shapes=[pltpu.SemaphoreType.DMA((3,))],
        compiler_params=params(2 * VMEM),
        cost_estimate=pl.CostEstimate(
            flops=2 * 3 * 2 * count * length * width,
            bytes_accessed=4 * (count * width + 8 * length * width),
            transcendentals=0,
        ),
    )(place, lane, docs, table, back, taps, weight, gate, *after)


def project_kernel(steps, slot, start, first, last, facts_ref, *refs):
    shards, refs = refs[: len(steps)], refs[len(steps) :]
    weight_ref, gate_ref, out_ref = refs[0], refs[1], refs[-1]
    before_ref = None if first else refs[2]
    rows, depth = shards[0].shape
    count = weight_ref.shape[1] // depth
    for tile in range(weight_ref.shape[0] // LANES):
        lanes = pl.ds(tile * LANES, LANES)
        total = None if first else before_ref[:, lanes]
        for shard, step in zip(shards, steps):
            at = lax.rem(facts_ref[0, 4 + REACH] + count - step, count)
            features = pl.ds(pl.multiple_of(at * depth, depth), depth)
            part = nt(shard[...], weight_ref[lanes, features])
            total = part if total is None else total + part
        if last:
            gate = gate_ref[0, slot, start : start + rows, lanes].astype(F32)
            out_ref[:, lanes] = (total * gate).astype(BF16)
        else:
            out_ref[:, lanes] = total


def project(facts, shards, steps, weight, gate, slot, start, before=None, last=True, after=()):
    rows, depth = shards[0].shape
    width = weight.shape[0]
    operands = [facts, *shards, weight, gate]
    if before is not None:
        operands.append(before)
    body = functools.partial(project_kernel, steps, slot, start, before is None, last)
    return pl.pallas_call(
        body,
        out_shape=pltpu.VMEM((rows, width), BF16 if last else F32),
        in_specs=[SCALARS] + [WHOLE] * (len(operands) - 1) + [ANYWHERE] * len(after),
        out_specs=WHOLE,
        compiler_params=params(),
        cost_estimate=pl.CostEstimate(
            flops=2 * rows * depth * len(shards) * width,
            bytes_accessed=2 * (rows + width) * depth * len(shards),
            transcendentals=0,
        ),
    )(*operands, *after)


class Conv:
    def __init__(self, slot, facts, table, back, spectra):
        self.facts = [facts[slot, at] for at in range(4 + REACH)]
        self.table, self.back, self.spectra = table, back, spectra
        self.length = table.shape[0] // 2
        self.lanes = lanes_at(pl.program_id(0))
        self.row = lax.broadcasted_iota(jnp.int32, (self.length, LANES), 0)

    def joined(self, pieces):
        tiles = [piece[:, self.lanes] for piece in pieces]
        return tiles[0] if len(tiles) == 1 else jnp.concatenate(tiles, axis=0)

    def within(self, low, high):
        return (self.row >= low) & (self.row < high)

    def term(self, values, low, high, distance):
        length = self.length
        kept = jnp.where(self.within(low, high), values.astype(F32), 0.0).astype(BF16)
        full = nn(self.table[...], kept)
        real, imag = full[:length], full[length:]
        k_real = self.spectra[distance, :length, self.lanes]
        k_imag = self.spectra[distance, length:, self.lanes]
        return k_real * real - k_imag * imag, k_real * imag + k_imag * real

    def signal(self, real, imag):
        real, imag = real.astype(BF16), imag.astype(BF16)
        return nn(self.back[...], jnp.concatenate([real, imag, real, imag], axis=0))

    def far_terms(self, acc, chosen, choices):
        for distance in range(1, REACH + 1):
            reach = self.facts[1 + distance]

            @pl.when(reach > 0)
            def _(distance=distance, reach=reach):
                for pieces, holds in choices(distance):

                    @pl.when(holds)
                    def _(pieces=pieces):
                        chosen[...] = self.joined(pieces)

                real, imag = self.term(chosen[...], 0, reach, distance)
                acc[: self.length, :] += real
                acc[self.length :, :] += imag

    def inner_documents(self, own, read, write):
        first_end, last_start = self.facts[0], self.facts[1]

        @pl.when(last_start > 0)
        def _():
            signal = self.signal(*self.term(own, 0, first_end, 0))
            write(jnp.where(self.row < first_end, signal, read()))

        @pl.when(last_start > first_end)
        def _():
            signal = self.signal(*self.term(own, first_end, last_start, 0))
            write(jnp.where(self.within(first_end, last_start), signal, read()))

    def halo(self, pieces, distance, mixed):
        sets = 3 if mixed else 4
        count = len(pieces) // sets
        kinds = [pieces[at * count : (at + 1) * count] for at in range(sets)]
        two, swapped, mate, far = kinds[0], kinds[1], kinds[2], kinds[-1]
        inner = self.facts[5]
        if distance == 2:
            return [(two, inner >= 0)]
        if distance == 1:
            return [(mate, inner == 1), (swapped, inner == 0)]
        return [(swapped, inner == 1), (far, inner == 0)]


def own_kernel(slot, pieces, facts_ref, table_ref, back_ref, spec_ref, *refs):
    own_refs, out_ref = refs[:pieces], refs[-1]
    conv = Conv(slot, facts_ref, table_ref, back_ref, spec_ref)
    own = conv.joined(own_refs)
    out_ref[:, conv.lanes] = conv.signal(*conv.term(own, conv.facts[1], conv.length, 0))

    def write(value):
        out_ref[:, conv.lanes] = value

    conv.inner_documents(own, lambda: out_ref[:, conv.lanes], write)


def far_kernel(slot, pieces, facts_ref, table_ref, back_ref, spec_ref, *refs):
    near_ref, refs = refs[0], refs[1:]
    if slot == 0:
        upper_ref, mate_ref, two_ref, fold_ref = refs[:4]
        halos = refs[4 : 4 + 3 * pieces]
    else:
        halos = refs[: 4 * pieces]
    out_ref, acc_ref, chosen_ref = refs[-3:]
    conv = Conv(slot, facts_ref, table_ref, back_ref, spec_ref)
    role = conv.facts[6]

    def choices(distance):
        found = conv.halo(halos, distance, slot == 0)
        if slot == 0:
            folded = {
                1: [([upper_ref], role == 1)],
                2: [([mate_ref], (role == 1) | (role == 2))],
                3: [([two_ref], role == 1), ([upper_ref], role == 2), ([fold_ref], role == 3)],
            }
            found = found + folded[distance]
        return found

    reaches = conv.facts[2] > 0

    @pl.when(reaches)
    def _():
        acc_ref[...] = jnp.zeros_like(acc_ref)
        conv.far_terms(acc_ref, chosen_ref, choices)
        signal = conv.signal(acc_ref[: conv.length, :], acc_ref[conv.length :, :])
        kept = jnp.where(conv.row >= conv.facts[1], signal, 0.0)
        out_ref[0, 0] = near_ref[:, conv.lanes] + kept

    @pl.when(jnp.logical_not(reaches))
    def _():
        out_ref[0, 0] = near_ref[:, conv.lanes]


def conv_call(body, tabs, facts, arrays, out_shape, out_spec, scratch, terms, result=None):
    table, back, spectra = tabs
    length = table.shape[0] // 2
    width = spectra.shape[2]
    operands = [facts, table, back, spectra, *arrays]
    specs = [SCALARS] + [WHOLE] * (len(operands) - 1)
    aliases = {}
    if result is not None:
        aliases = {len(operands): 0}
        operands.append(result)
        specs.append(ANYWHERE)
    return pl.pallas_call(
        body,
        grid=(width // LANES,),
        out_shape=out_shape,
        in_specs=specs,
        out_specs=out_spec,
        scratch_shapes=scratch,
        input_output_aliases=aliases,
        compiler_params=params(),
        cost_estimate=pl.CostEstimate(
            flops=4 * terms * length * length * width,
            bytes_accessed=4 * length * width,
            transcendentals=0,
        ),
    )(*operands)


def own_terms(slot, tabs, facts, pieces):
    _, back, spectra = tabs
    shape = pltpu.VMEM((back.shape[0], spectra.shape[2]), F32)
    body = functools.partial(own_kernel, slot, len(pieces))
    return conv_call(body, tabs, facts, pieces, shape, WHOLE, [], 8)


def far_terms(slot, count, tabs, facts, arrays, result=None):
    _, back, spectra = tabs
    length, width = back.shape[0], spectra.shape[2]
    shape = jax.ShapeDtypeStruct((1, 2, length, width), F32)
    spec = pl.BlockSpec((1, 1, length, LANES), lambda c: (0, slot, 0, c))
    scratch = [pltpu.VMEM((2 * length, LANES), F32), pltpu.VMEM((length, LANES), BF16)]
    body = functools.partial(far_kernel, slot, count)
    return conv_call(body, tabs, facts, arrays, shape, spec, scratch, 8, result)


def ordered(value, *earlier):
    return pl.pallas_call(
        lambda *refs: None,
        out_shape=jax.ShapeDtypeStruct(value.shape, value.dtype),
        in_specs=[ANYWHERE] * (1 + len(earlier)),
        out_specs=ANYWHERE,
        input_output_aliases={0: 0},
        compiler_params=params(VMEM // 20),
    )(value, *earlier)


def shifted(value, steps):
    count = lax.axis_size("ctx")
    initial, last = (max(0, -steps), min(count, count - steps))
    return lax.ppermute(value, "ctx", [(source, source + steps) for source in range(initial, last)])


def core_swapped(value):
    count = lax.axis_size("ctx")
    return lax.ppermute(value, "ctx", [(source, source ^ 1) for source in range(count)])


def upper_halo_of(value):
    count = lax.axis_size("ctx")
    far = [(source, source + 3) for source in range(1, count - 3, 2)] + [(count - 1, count - 3)]
    two = shifted(value, 2)
    mate, far = core_swapped(value), lax.ppermute(value, "ctx", far)
    return [two, core_swapped(two), mate, far]


def lower_halo_of(value):
    count = lax.axis_size("ctx")
    mixed = [(source, source - 1) for source in range(1, count, 2)]
    mixed += [(source, source - 3) for source in range(4, count, 2)]
    two = shifted(value, -2)
    mixed = lax.ppermute(value, "ctx", mixed)
    return [two, core_swapped(two), mixed]


def on_device(grad_out, out_weight, gate, filter_taps, doc_starts):
    pairs = lax.axis_size("ctx")
    place = lax.axis_index("ctx")
    length = grad_out.shape[2]
    width = out_weight.shape[0]
    cut = length * 5 // 8
    count = lax.axis_size("ch")
    lane = lax.axis_index("ch").astype(jnp.int32)[None]
    around = [(source, (source + 1) % count) for source in range(count)]
    everything = tuple(range(count))

    def turned(piece):
        return lax.ppermute(piece, "ch", around)

    slices = [grad_out[0, 0, :cut], grad_out[0, 0, cut:]]
    upper_in = [grad_out[0, 1]]
    upper_in.append(turned(upper_in[0]))

    table, back = (jnp.asarray(one) for one in tables(length))
    spectra, weight, gates, table, back, facts, prepared = prepare(
        pairs,
        place.astype(jnp.int32)[None],
        lane,
        doc_starts,
        table,
        back,
        filter_taps,
        out_weight,
        gate,
        slices,
    )
    tabs = (table, back, spectra)

    upper_in[1] = ordered(upper_in[1], prepared)
    for step in range(2, count):
        upper_in.append(turned(upper_in[-1]))
    first_in = [ordered(slices[0], upper_in[-2])]
    for step in range(1, count):
        first_in.append(turned(first_in[-1]))
    second_in = [ordered(slices[1], upper_in[-1])]
    second_in.append(ordered(turned(second_in[0]), first_in[-1]))
    for step in range(2, count):
        second_in.append(turned(second_in[-1]))

    upper = project(facts, upper_in, everything, weight, gates, 1, 0, after=[first_in[1]])
    upper_halo = upper_halo_of(upper)
    near = own_terms(1, tabs, facts, [upper])
    result = far_terms(1, 1, tabs, facts, [near, *upper_halo])

    first = project(facts, first_in, everything, weight, gates, 0, 0)
    first_halo = lower_halo_of(first)
    partial = project(facts, second_in[:-1], everything[:-1], weight, gates, 0, cut, last=False)
    second = project(facts, second_in[-1:], everything[-1:], weight, gates, 0, cut, partial)
    second_halo = lower_halo_of(second)
    near = own_terms(0, tabs, facts, [first, second])
    two, _, mate, fold = upper_halo
    halos = [piece for both in zip(first_halo, second_halo) for piece in both]
    return far_terms(0, 2, tabs, facts, [near, upper, mate, two, fold, *halos], result)


def solution(mesh):
    in_specs = (
        P("ctx", None, None, "ch"),
        P("ch", None),
        P("ctx", None, None, "ch"),
        P(None, "ch"),
        P(),
    )
    out_specs = P("ctx", None, None, "ch")
    return jax.shard_map(
        on_device, mesh=mesh, in_specs=in_specs, out_specs=out_specs, check_vma=False
    )
```

```python
import functools
import math

import jax
import jax.numpy as jnp
import ml_dtypes
import numpy as np
from jax import lax
from jax.experimental import pallas as pl
from jax.experimental.pallas import tpu as pltpu
from jax.sharding import PartitionSpec as P

REACH = 3
LANES = 256
VMEM = 20 * 1024 * 1024
F32 = jnp.float32
BF16 = jnp.bfloat16
WHOLE = pl.BlockSpec(memory_space=pltpu.VMEM)
ANYWHERE = pl.BlockSpec(memory_space=pl.ANY)
OUTSIDE = pl.BlockSpec(memory_space=pltpu.HBM)
SCALARS = pl.BlockSpec(memory_space=pltpu.SMEM)


def parts_of(table):
    high = table.astype(np.float32).astype(ml_dtypes.bfloat16)
    low = (table - high.astype(np.float64)).astype(np.float32).astype(ml_dtypes.bfloat16)
    return high, low


@functools.lru_cache(maxsize=None)
def tables(length):
    angle = np.outer(2 * np.arange(length) + 1, np.arange(length)) % (4 * length)
    angle = angle.astype(np.float64) * (math.pi / (2 * length))
    forward = np.concatenate([np.cos(angle), -np.sin(angle)], axis=0)
    high, low = parts_of(forward)
    back_high, back_low = parts_of(forward.T / length)
    return np.concatenate([high, low], axis=1), np.concatenate([back_high, back_low], axis=1)


def nn(a, b):
    return lax.dot_general(a, b, (((1,), (0,)), ((), ())), preferred_element_type=F32)


def nt(a, b):
    return lax.dot_general(a, b, (((1,), (1,)), ((), ())), preferred_element_type=F32)


def params(limit=VMEM):
    return pltpu.CompilerParams(vmem_limit_bytes=limit)


def lanes_at(tile):
    return pl.ds(pl.multiple_of(tile * LANES, LANES), LANES)


def write_facts(facts_ref, slot, docs_ref, block, length, end, inner, role):
    start = block * length
    stop = start + length - 1

    def visit(at, found):
        first, following, last = found
        here = docs_ref[at]
        first = jnp.minimum(first, jnp.where(here > start, here, end))
        following = jnp.minimum(following, jnp.where(here > stop, here, end))
        last = jnp.maximum(last, jnp.where(here <= stop, here, 0))
        return first, following, last

    whole = jnp.int32(end)
    first, following, last = lax.fori_loop(
        0, docs_ref.shape[0], visit, (whole, whole, jnp.int32(0))
    )
    facts_ref[slot, 0] = jnp.clip(first - start, 0, length)
    facts_ref[slot, 1] = jnp.clip(last - start, 0, length)
    for distance in range(1, REACH + 1):
        facts_ref[slot, 1 + distance] = jnp.clip(following - start - distance * length, 0, length)
    facts_ref[slot, 2 + REACH] = inner
    facts_ref[slot, 3 + REACH] = role


def prepare_kernel(pairs, *refs):
    place_ref, lane_ref, docs_ref, table_ref, back_ref, taps_ref, weight_ref, gate_ref = refs[:8]
    spec_out, weight_out, gate_out, table_out, back_out, facts_out, token_out, sems = refs[-8:]
    token_out[...] = jnp.zeros_like(token_out)
    copies = [
        pltpu.make_async_copy(source, target, sems.at[at])
        for at, (source, target) in enumerate(
            [(weight_ref, weight_out), (gate_ref, gate_out), (back_ref, back_out)]
        )
    ]
    step = pl.program_id(0)
    length = table_ref.shape[1] // 2

    @pl.when(step == 0)
    def _():
        for copy in copies:
            copy.start()
        table_out[...] = table_ref[:, :length]
        place = place_ref[0]
        odd = lax.rem(place, 2)
        role = jnp.where(place >= pairs - 3, pairs - place, 0)
        end = 2 * pairs * length
        for slot in range(2):
            facts_out[slot, 4 + REACH] = lane_ref[0]
        write_facts(facts_out, 0, docs_ref, place, length, end, 1 - odd, role)
        write_facts(facts_out, 1, docs_ref, 2 * pairs - 1 - place, length, end, odd, role)

    freq = lax.broadcasted_iota(jnp.int32, (length, 1), 0)
    sign = jnp.where(freq % 2 == 0, 1.0, -1.0).astype(F32)
    lanes = lanes_at(step)
    before = None
    for part in range(REACH + 1):
        if part < REACH:
            values = taps_ref[part * length : (part + 1) * length, :]
            high = values.astype(BF16)
            low = (values - high.astype(F32)).astype(BF16)
            full = nn(table_ref[...], jnp.concatenate([high, high], axis=0))
            full = full + nn(table_ref[:, :length], low)
            now = (full[:length], -full[length:])
        else:
            now = None
        if before is None:
            real, imag = now
        else:
            real, imag = sign * before[1], -sign * before[0]
            if now is not None:
                real, imag = now[0] + real, now[1] + imag
        spec_out[part, :length, lanes] = real
        spec_out[part, length:, lanes] = imag
        before = now

    @pl.when(step == pl.num_programs(0) - 1)
    def _():
        for copy in copies:
            copy.wait()


def prepare(pairs, place, lane, docs, table, back, taps, weight, gate, after):
    count, width = taps.shape
    length = count // REACH
    return pl.pallas_call(
        functools.partial(prepare_kernel, pairs),
        grid=(width // LANES,),
        out_shape=(
            pltpu.VMEM((REACH + 1, 2 * length, width), F32),
            pltpu.VMEM(weight.shape, BF16),
            pltpu.VMEM(gate.shape, BF16),
            pltpu.VMEM((2 * length, length), BF16),
            pltpu.VMEM(back.shape, BF16),
            pltpu.SMEM((2, 8), jnp.int32),
            pltpu.VMEM((8, 128), F32),
        ),
        in_specs=[
            SCALARS,
            SCALARS,
            SCALARS,
            pl.BlockSpec((2 * length, 2 * length), lambda c: (0, 0)),
            OUTSIDE,
            pl.BlockSpec((count, LANES), lambda c: (0, c)),
            OUTSIDE,
            OUTSIDE,
        ]
        + [ANYWHERE] * len(after),
        out_specs=(WHOLE,) * 5 + (SCALARS, WHOLE),
        scratch_shapes=[pltpu.SemaphoreType.DMA((3,))],
        compiler_params=params(2 * VMEM),
        cost_estimate=pl.CostEstimate(
            flops=2 * 3 * 2 * count * length * width,
            bytes_accessed=4 * (count * width + 8 * length * width),
            transcendentals=0,
        ),
    )(place, lane, docs, table, back, taps, weight, gate, *after)


def project_kernel(steps, slot, start, first, last, facts_ref, *refs):
    shards, refs = refs[: len(steps)], refs[len(steps) :]
    weight_ref, gate_ref, out_ref = refs[0], refs[1], refs[-1]
    before_ref = None if first else refs[2]
    rows, depth = shards[0].shape
    count = weight_ref.shape[1] // depth
    for tile in range(weight_ref.shape[0] // LANES):
        lanes = pl.ds(tile * LANES, LANES)
        total = None if first else before_ref[:, lanes]
        for shard, step in zip(shards, steps):
            at = lax.rem(facts_ref[0, 4 + REACH] + count - step, count)
            features = pl.ds(pl.multiple_of(at * depth, depth), depth)
            part = nt(shard[...], weight_ref[lanes, features])
            total = part if total is None else total + part
        if last:
            gate = gate_ref[0, slot, start : start + rows, lanes].astype(F32)
            out_ref[:, lanes] = (total * gate).astype(BF16)
        else:
            out_ref[:, lanes] = total


def project(facts, shards, steps, weight, gate, slot, start, before=None, last=True, after=()):
    rows, depth = shards[0].shape
    width = weight.shape[0]
    operands = [facts, *shards, weight, gate]
    if before is not None:
        operands.append(before)
    body = functools.partial(project_kernel, steps, slot, start, before is None, last)
    return pl.pallas_call(
        body,
        out_shape=pltpu.VMEM((rows, width), BF16 if last else F32),
        in_specs=[SCALARS] + [WHOLE] * (len(operands) - 1) + [ANYWHERE] * len(after),
        out_specs=WHOLE,
        compiler_params=params(),
        cost_estimate=pl.CostEstimate(
            flops=2 * rows * depth * len(shards) * width,
            bytes_accessed=2 * (rows + width) * depth * len(shards),
            transcendentals=0,
        ),
    )(*operands, *after)


class Conv:
    def __init__(self, slot, facts, table, back, spectra):
        self.facts = [facts[slot, at] for at in range(4 + REACH)]
        self.table, self.back, self.spectra = table, back, spectra
        self.length = table.shape[0] // 2
        self.lanes = lanes_at(pl.program_id(0))
        self.row = lax.broadcasted_iota(jnp.int32, (self.length, LANES), 0)

    def joined(self, pieces):
        tiles = [piece[:, self.lanes] for piece in pieces]
        return tiles[0] if len(tiles) == 1 else jnp.concatenate(tiles, axis=0)

    def within(self, low, high):
        return (self.row >= low) & (self.row < high)

    def term(self, values, low, high, distance):
        length = self.length
        kept = jnp.where(self.within(low, high), values.astype(F32), 0.0).astype(BF16)
        full = nn(self.table[...], kept)
        real, imag = full[:length], full[length:]
        k_real = self.spectra[distance, :length, self.lanes]
        k_imag = self.spectra[distance, length:, self.lanes]
        return k_real * real - k_imag * imag, k_real * imag + k_imag * real

    def signal(self, real, imag):
        real, imag = real.astype(BF16), imag.astype(BF16)
        return nn(self.back[...], jnp.concatenate([real, imag, real, imag], axis=0))

    def far_terms(self, acc, chosen, choices):
        for distance in range(1, REACH + 1):
            reach = self.facts[1 + distance]

            @pl.when(reach > 0)
            def _(distance=distance, reach=reach):
                for pieces, holds in choices(distance):

                    @pl.when(holds)
                    def _(pieces=pieces):
                        chosen[...] = self.joined(pieces)

                real, imag = self.term(chosen[...], 0, reach, distance)
                acc[: self.length, :] += real
                acc[self.length :, :] += imag

    def inner_documents(self, own, read, write):
        first_end, last_start = self.facts[0], self.facts[1]

        @pl.when(last_start > 0)
        def _():
            signal = self.signal(*self.term(own, 0, first_end, 0))
            write(jnp.where(self.row < first_end, signal, read()))

        @pl.when(last_start > first_end)
        def _():
            signal = self.signal(*self.term(own, first_end, last_start, 0))
            write(jnp.where(self.within(first_end, last_start), signal, read()))

    def halo(self, pieces, distance, mixed):
        sets = 3 if mixed else 4
        count = len(pieces) // sets
        kinds = [pieces[at * count : (at + 1) * count] for at in range(sets)]
        two, swapped, mate, far = kinds[0], kinds[1], kinds[2], kinds[-1]
        inner = self.facts[5]
        if distance == 2:
            return [(two, inner >= 0)]
        if distance == 1:
            return [(mate, inner == 1), (swapped, inner == 0)]
        return [(swapped, inner == 1), (far, inner == 0)]


def own_kernel(slot, pieces, facts_ref, table_ref, back_ref, spec_ref, *refs):
    own_refs, out_ref = refs[:pieces], refs[-1]
    conv = Conv(slot, facts_ref, table_ref, back_ref, spec_ref)
    own = conv.joined(own_refs)
    out_ref[:, conv.lanes] = conv.signal(*conv.term(own, conv.facts[1], conv.length, 0))

    def write(value):
        out_ref[:, conv.lanes] = value

    conv.inner_documents(own, lambda: out_ref[:, conv.lanes], write)


def far_kernel(slot, pieces, facts_ref, table_ref, back_ref, spec_ref, *refs):
    near_ref, refs = refs[0], refs[1:]
    if slot == 0:
        upper_ref, mate_ref, two_ref, fold_ref = refs[:4]
        halos = refs[4 : 4 + 3 * pieces]
    else:
        halos = refs[: 4 * pieces]
    out_ref, acc_ref, chosen_ref = refs[-3:]
    conv = Conv(slot, facts_ref, table_ref, back_ref, spec_ref)
    role = conv.facts[6]

    def choices(distance):
        found = conv.halo(halos, distance, slot == 0)
        if slot == 0:
            folded = {
                1: [([upper_ref], role == 1)],
                2: [([mate_ref], (role == 1) | (role == 2))],
                3: [([two_ref], role == 1), ([upper_ref], role == 2), ([fold_ref], role == 3)],
            }
            found = found + folded[distance]
        return found

    reaches = conv.facts[2] > 0

    @pl.when(reaches)
    def _():
        acc_ref[...] = jnp.zeros_like(acc_ref)
        conv.far_terms(acc_ref, chosen_ref, choices)
        signal = conv.signal(acc_ref[: conv.length, :], acc_ref[conv.length :, :])
        kept = jnp.where(conv.row >= conv.facts[1], signal, 0.0)
        out_ref[0, 0] = near_ref[:, conv.lanes] + kept

    @pl.when(jnp.logical_not(reaches))
    def _():
        out_ref[0, 0] = near_ref[:, conv.lanes]


def conv_call(body, tabs, facts, arrays, out_shape, out_spec, scratch, after=(), result=None):
    table, back, spectra = tabs
    length = table.shape[0] // 2
    width = spectra.shape[2]
    operands = [facts, table, back, spectra, *arrays]
    specs = [SCALARS] + [WHOLE] * (len(operands) - 1) + [ANYWHERE] * len(after)
    operands.extend(after)
    aliases = {}
    if result is not None:
        aliases = {len(operands): 0}
        operands.append(result)
        specs.append(ANYWHERE)
    return pl.pallas_call(
        body,
        grid=(width // LANES,),
        out_shape=out_shape,
        in_specs=specs,
        out_specs=out_spec,
        scratch_shapes=scratch,
        input_output_aliases=aliases,
        compiler_params=params(),
        cost_estimate=pl.CostEstimate(
            flops=32 * length * length * width,
            bytes_accessed=4 * length * width,
            transcendentals=0,
        ),
    )(*operands)


def own_terms(slot, tabs, facts, pieces, after=()):
    _, back, spectra = tabs
    shape = pltpu.VMEM((back.shape[0], spectra.shape[2]), F32)
    body = functools.partial(own_kernel, slot, len(pieces))
    return conv_call(body, tabs, facts, pieces, shape, WHOLE, [], after)


def far_terms(slot, count, tabs, facts, arrays, result=None):
    _, back, spectra = tabs
    length, width = back.shape[0], spectra.shape[2]
    shape = jax.ShapeDtypeStruct((1, 2, length, width), F32)
    spec = pl.BlockSpec((1, 1, length, LANES), lambda c: (0, slot, 0, c))
    scratch = [pltpu.VMEM((2 * length, LANES), F32), pltpu.VMEM((length, LANES), BF16)]
    body = functools.partial(far_kernel, slot, count)
    return conv_call(body, tabs, facts, arrays, shape, spec, scratch, (), result)


def ordered(value, *earlier):
    return pl.pallas_call(
        lambda *refs: None,
        out_shape=jax.ShapeDtypeStruct(value.shape, value.dtype),
        in_specs=[ANYWHERE] * (1 + len(earlier)),
        out_specs=ANYWHERE,
        input_output_aliases={0: 0},
        compiler_params=params(VMEM // 20),
    )(value, *earlier)


def shifted(value, steps):
    count = lax.axis_size("ctx")
    initial, last = (max(0, -steps), min(count, count - steps))
    return lax.ppermute(value, "ctx", [(source, source + steps) for source in range(initial, last)])


def core_swapped(value):
    count = lax.axis_size("ctx")
    return lax.ppermute(value, "ctx", [(source, source ^ 1) for source in range(count)])


def upper_halo_of(value):
    count = lax.axis_size("ctx")
    far = [(source, source + 3) for source in range(1, count - 3, 2)] + [(count - 1, count - 3)]
    two = shifted(value, 2)
    mate, far = core_swapped(value), lax.ppermute(value, "ctx", far)
    return [two, core_swapped(two), mate, far]


def lower_halo_of(value):
    count = lax.axis_size("ctx")
    mixed = [(source, source - 1) for source in range(1, count, 2)]
    mixed += [(source, source - 3) for source in range(4, count, 2)]
    two = shifted(value, -2)
    mixed = lax.ppermute(value, "ctx", mixed)
    return [two, core_swapped(two), mixed]


def on_device(grad_out, out_weight, gate, filter_taps, doc_starts):
    pairs = lax.axis_size("ctx")
    place = lax.axis_index("ctx")
    length = grad_out.shape[2]
    width = out_weight.shape[0]
    cut = length * 5 // 8
    count = lax.axis_size("ch")
    lane = lax.axis_index("ch").astype(jnp.int32)[None]
    around = [(source, (source + 1) % count) for source in range(count)]
    everything = tuple(range(count))

    def turned(piece):
        return lax.ppermute(piece, "ch", around)

    slices = [grad_out[0, 0, :cut], grad_out[0, 0, cut:]]
    upper_in = [grad_out[0, 1]]
    upper_in.append(turned(upper_in[0]))

    table, back = (jnp.asarray(one) for one in tables(length))
    spectra, weight, gates, table, back, facts, prepared = prepare(
        pairs,
        place.astype(jnp.int32)[None],
        lane,
        doc_starts,
        table,
        back,
        filter_taps,
        out_weight,
        gate,
        slices,
    )
    tabs = (table, back, spectra)

    upper_in[1] = ordered(upper_in[1], prepared)
    for step in range(2, count):
        upper_in.append(turned(upper_in[-1]))
    first_in = [ordered(slices[0], upper_in[-2])]
    for step in range(1, count):
        first_in.append(turned(first_in[-1]))
    second_in = [ordered(slices[1], upper_in[-1])]
    second_in.append(ordered(turned(second_in[0]), first_in[-1]))
    for step in range(2, count):
        second_in.append(turned(second_in[-1]))

    def projected(shards, slot, start, early=(), late=()):
        args = (weight, gates, slot, start)
        partial = project(facts, shards[:-1], everything[:-1], *args, last=False, after=early)
        return project(facts, shards[-1:], everything[-1:], *args, partial, after=late)

    upper = projected(upper_in, 1, 0, early=[first_in[0]], late=[first_in[1]])
    upper_halo = upper_halo_of(upper)
    near = own_terms(1, tabs, facts, [upper])
    result = far_terms(1, 1, tabs, facts, [near, *upper_halo])

    first = projected(first_in, 0, 0, late=[upper_halo[1], upper_halo[3]])
    first_halo = lower_halo_of(first)
    second = projected(second_in, 0, cut)
    second_halo = lower_halo_of(second)
    near = own_terms(0, tabs, facts, [first, second], after=second_halo[:1])
    two, _, mate, fold = upper_halo
    halos = [piece for both in zip(first_halo, second_halo) for piece in both]
    return far_terms(0, 2, tabs, facts, [near, upper, mate, two, fold, *halos], result)


def solution(mesh):
    in_specs = (
        P("ctx", None, None, "ch"),
        P("ch", None),
        P("ctx", None, None, "ch"),
        P(None, "ch"),
        P(),
    )
    out_specs = P("ctx", None, None, "ch")
    return jax.shard_map(
        on_device, mesh=mesh, in_specs=in_specs, out_specs=out_specs, check_vma=False
    )
```

```python
import functools
import math

import jax
import jax.numpy as jnp
import ml_dtypes
import numpy as np
from jax import lax
from jax.experimental import pallas as pl
from jax.experimental.pallas import tpu as pltpu
from jax.sharding import PartitionSpec as P

REACH = 3
LANES = 256
VMEM = 20 * 1024 * 1024
F32 = jnp.float32
BF16 = jnp.bfloat16
WHOLE = pl.BlockSpec(memory_space=pltpu.VMEM)
ANYWHERE = pl.BlockSpec(memory_space=pl.ANY)
OUTSIDE = pl.BlockSpec(memory_space=pltpu.HBM)
SCALARS = pl.BlockSpec(memory_space=pltpu.SMEM)


def parts_of(table):
    high = table.astype(np.float32).astype(ml_dtypes.bfloat16)
    low = (table - high.astype(np.float64)).astype(np.float32).astype(ml_dtypes.bfloat16)
    return high, low


@functools.lru_cache(maxsize=None)
def tables(length):
    angle = np.outer(2 * np.arange(length) + 1, np.arange(length)) % (4 * length)
    angle = angle.astype(np.float64) * (math.pi / (2 * length))
    forward = np.concatenate([np.cos(angle), -np.sin(angle)], axis=0)
    high, low = parts_of(forward)
    back_high, back_low = parts_of(forward.T / length)
    return np.concatenate([high, low], axis=1), np.concatenate([back_high, back_low], axis=1)


def nn(a, b):
    return lax.dot_general(a, b, (((1,), (0,)), ((), ())), preferred_element_type=F32)


def nt(a, b):
    return lax.dot_general(a, b, (((1,), (1,)), ((), ())), preferred_element_type=F32)


def params(limit=VMEM):
    return pltpu.CompilerParams(vmem_limit_bytes=limit)


def lanes_at(tile):
    return pl.ds(pl.multiple_of(tile * LANES, LANES), LANES)


def write_facts(facts_ref, slot, docs_ref, block, length, end, inner, role):
    start = block * length
    stop = start + length - 1

    def visit(at, found):
        first, following, last = found
        here = docs_ref[at]
        first = jnp.minimum(first, jnp.where(here > start, here, end))
        following = jnp.minimum(following, jnp.where(here > stop, here, end))
        last = jnp.maximum(last, jnp.where(here <= stop, here, 0))
        return first, following, last

    whole = jnp.int32(end)
    first, following, last = lax.fori_loop(
        0, docs_ref.shape[0], visit, (whole, whole, jnp.int32(0))
    )
    facts_ref[slot, 0] = jnp.clip(first - start, 0, length)
    facts_ref[slot, 1] = jnp.clip(last - start, 0, length)
    for distance in range(1, REACH + 1):
        facts_ref[slot, 1 + distance] = jnp.clip(following - start - distance * length, 0, length)
    facts_ref[slot, 2 + REACH] = inner
    facts_ref[slot, 3 + REACH] = role


def prepare_kernel(pairs, *refs):
    place_ref, lane_ref, docs_ref, table_ref, back_ref, taps_ref = refs[:6]
    weight_ref, gate_ref, grad_ref = refs[6:9]
    spec_out, weight_out, gate_out, lower_out, table_out, back_out = refs[9:15]
    facts_out, token_out, sems = refs[15:]
    token_out[...] = jnp.zeros_like(token_out)
    copies = [
        pltpu.make_async_copy(source, target, sems.at[at])
        for at, (source, target) in enumerate(
            [
                (grad_ref.at[0, 0], lower_out),
                (weight_ref, weight_out),
                (gate_ref, gate_out),
                (back_ref, back_out),
            ]
        )
    ]
    step = pl.program_id(0)
    length = table_ref.shape[1] // 2

    @pl.when(step == 0)
    def _():
        for copy in copies:
            copy.start()
        table_out[...] = table_ref[:, :length]
        place = place_ref[0]
        odd = lax.rem(place, 2)
        role = jnp.where(place >= pairs - 3, pairs - place, 0)
        end = 2 * pairs * length
        for slot in range(2):
            facts_out[slot, 4 + REACH] = lane_ref[0]
        write_facts(facts_out, 0, docs_ref, place, length, end, 1 - odd, role)
        write_facts(facts_out, 1, docs_ref, 2 * pairs - 1 - place, length, end, odd, role)

    freq = lax.broadcasted_iota(jnp.int32, (length, 1), 0)
    sign = jnp.where(freq % 2 == 0, 1.0, -1.0).astype(F32)
    lanes = lanes_at(step)
    before = None
    for part in range(REACH + 1):
        if part < REACH:
            values = taps_ref[part * length : (part + 1) * length, :]
            high = values.astype(BF16)
            low = (values - high.astype(F32)).astype(BF16)
            full = nn(table_ref[...], jnp.concatenate([high, high], axis=0))
            full = full + nn(table_ref[:, :length], low)
            now = (full[:length], -full[length:])
        else:
            now = None
        if before is None:
            real, imag = now
        else:
            real, imag = sign * before[1], -sign * before[0]
            if now is not None:
                real, imag = now[0] + real, now[1] + imag
        spec_out[part, :length, lanes] = real
        spec_out[part, length:, lanes] = imag
        before = now

    @pl.when(step == pl.num_programs(0) - 1)
    def _():
        for copy in copies:
            copy.wait()


def prepare(pairs, place, lane, docs, table, back, taps, weight, gate, grad):
    count, width = taps.shape
    length = count // REACH
    return pl.pallas_call(
        functools.partial(prepare_kernel, pairs),
        grid=(width // LANES,),
        out_shape=(
            pltpu.VMEM((REACH + 1, 2 * length, width), F32),
            pltpu.VMEM(weight.shape, BF16),
            pltpu.VMEM(gate.shape, BF16),
            pltpu.VMEM(grad.shape[2:], BF16),
            pltpu.VMEM((2 * length, length), BF16),
            pltpu.VMEM(back.shape, BF16),
            pltpu.SMEM((2, 8), jnp.int32),
            pltpu.VMEM((8, 128), F32),
        ),
        in_specs=[
            SCALARS,
            SCALARS,
            SCALARS,
            pl.BlockSpec((2 * length, 2 * length), lambda c: (0, 0)),
            OUTSIDE,
            pl.BlockSpec((count, LANES), lambda c: (0, c)),
            OUTSIDE,
            OUTSIDE,
            OUTSIDE,
        ],
        out_specs=(WHOLE,) * 6 + (SCALARS, WHOLE),
        scratch_shapes=[pltpu.SemaphoreType.DMA((4,))],
        compiler_params=params(2 * VMEM),
        cost_estimate=pl.CostEstimate(
            flops=2 * 3 * 2 * count * length * width,
            bytes_accessed=4 * (count * width + 8 * length * width),
            transcendentals=0,
        ),
    )(place, lane, docs, table, back, taps, weight, gate, grad)


def project_kernel(steps, slot, start, first, last, facts_ref, *refs):
    shards, refs = refs[: len(steps)], refs[len(steps) :]
    weight_ref, gate_ref, out_ref = refs[0], refs[1], refs[-1]
    before_ref = None if first else refs[2]
    rows, depth = shards[0].shape
    count = weight_ref.shape[1] // depth
    for tile in range(weight_ref.shape[0] // LANES):
        lanes = pl.ds(tile * LANES, LANES)
        total = None if first else before_ref[:, lanes]
        for shard, step in zip(shards, steps):
            at = lax.rem(facts_ref[0, 4 + REACH] + count - step, count)
            features = pl.ds(pl.multiple_of(at * depth, depth), depth)
            part = nt(shard[...], weight_ref[lanes, features])
            total = part if total is None else total + part
        if last:
            gate = gate_ref[0, slot, start : start + rows, lanes].astype(F32)
            out_ref[:, lanes] = (total * gate).astype(BF16)
        else:
            out_ref[:, lanes] = total


def project(facts, shards, steps, weight, gate, slot, start, before=None, last=True, after=()):
    rows, depth = shards[0].shape
    width = weight.shape[0]
    operands = [facts, *shards, weight, gate]
    if before is not None:
        operands.append(before)
    body = functools.partial(project_kernel, steps, slot, start, before is None, last)
    return pl.pallas_call(
        body,
        out_shape=pltpu.VMEM((rows, width), BF16 if last else F32),
        in_specs=[SCALARS] + [WHOLE] * (len(operands) - 1) + [ANYWHERE] * len(after),
        out_specs=WHOLE,
        compiler_params=params(),
        cost_estimate=pl.CostEstimate(
            flops=2 * rows * depth * len(shards) * width,
            bytes_accessed=2 * (rows + width) * depth * len(shards),
            transcendentals=0,
        ),
    )(*operands, *after)


class Conv:
    def __init__(self, slot, facts, table, back, spectra):
        self.facts = [facts[slot, at] for at in range(4 + REACH)]
        self.table, self.back, self.spectra = table, back, spectra
        self.length = table.shape[0] // 2
        self.lanes = lanes_at(pl.program_id(0))
        self.row = lax.broadcasted_iota(jnp.int32, (self.length, LANES), 0)

    def joined(self, pieces):
        tiles = [piece[:, self.lanes] for piece in pieces]
        return tiles[0] if len(tiles) == 1 else jnp.concatenate(tiles, axis=0)

    def within(self, low, high):
        return (self.row >= low) & (self.row < high)

    def term(self, values, low, high, distance):
        length = self.length
        kept = jnp.where(self.within(low, high), values.astype(F32), 0.0).astype(BF16)
        full = nn(self.table[...], kept)
        real, imag = full[:length], full[length:]
        k_real = self.spectra[distance, :length, self.lanes]
        k_imag = self.spectra[distance, length:, self.lanes]
        return k_real * real - k_imag * imag, k_real * imag + k_imag * real

    def signal(self, real, imag):
        real, imag = real.astype(BF16), imag.astype(BF16)
        return nn(self.back[...], jnp.concatenate([real, imag, real, imag], axis=0))

    def far_terms(self, acc, chosen, choices):
        for distance in range(1, REACH + 1):
            reach = self.facts[1 + distance]

            @pl.when(reach > 0)
            def _(distance=distance, reach=reach):
                for pieces, holds in choices(distance):

                    @pl.when(holds)
                    def _(pieces=pieces):
                        chosen[...] = self.joined(pieces)

                real, imag = self.term(chosen[...], 0, reach, distance)
                acc[: self.length, :] += real
                acc[self.length :, :] += imag

    def inner_documents(self, own, read, write):
        first_end, last_start = self.facts[0], self.facts[1]

        @pl.when(last_start > 0)
        def _():
            signal = self.signal(*self.term(own, 0, first_end, 0))
            write(jnp.where(self.row < first_end, signal, read()))

        @pl.when(last_start > first_end)
        def _():
            signal = self.signal(*self.term(own, first_end, last_start, 0))
            write(jnp.where(self.within(first_end, last_start), signal, read()))

    def halo(self, pieces, distance, mixed):
        sets = 3 if mixed else 4
        count = len(pieces) // sets
        kinds = [pieces[at * count : (at + 1) * count] for at in range(sets)]
        two, swapped, mate, far = kinds[0], kinds[1], kinds[2], kinds[-1]
        inner = self.facts[5]
        if distance == 2:
            return [(two, inner >= 0)]
        if distance == 1:
            return [(mate, inner == 1), (swapped, inner == 0)]
        return [(swapped, inner == 1), (far, inner == 0)]


def own_kernel(slot, pieces, facts_ref, table_ref, back_ref, spec_ref, *refs):
    own_refs, out_ref = refs[:pieces], refs[-1]
    conv = Conv(slot, facts_ref, table_ref, back_ref, spec_ref)
    own = conv.joined(own_refs)
    out_ref[:, conv.lanes] = conv.signal(*conv.term(own, conv.facts[1], conv.length, 0))

    def write(value):
        out_ref[:, conv.lanes] = value

    conv.inner_documents(own, lambda: out_ref[:, conv.lanes], write)


def far_kernel(slot, pieces, facts_ref, table_ref, back_ref, spec_ref, *refs):
    near_ref, refs = refs[0], refs[1:]
    if slot == 0:
        upper_ref, mate_ref, two_ref, fold_ref = refs[:4]
        halos = refs[4 : 4 + 3 * pieces]
    else:
        halos = refs[: 4 * pieces]
    out_ref, acc_ref, chosen_ref = refs[-3:]
    if slot == 1:
        out_ref, token_ref = refs[-4:-2]
        token_ref[...] = jnp.zeros_like(token_ref)
    conv = Conv(slot, facts_ref, table_ref, back_ref, spec_ref)
    role = conv.facts[6]

    def choices(distance):
        found = conv.halo(halos, distance, slot == 0)
        if slot == 0:
            folded = {
                1: [([upper_ref], role == 1)],
                2: [([mate_ref], (role == 1) | (role == 2))],
                3: [([two_ref], role == 1), ([upper_ref], role == 2), ([fold_ref], role == 3)],
            }
            found = found + folded[distance]
        return found

    reaches = conv.facts[2] > 0

    @pl.when(reaches)
    def _():
        acc_ref[...] = jnp.zeros_like(acc_ref)
        conv.far_terms(acc_ref, chosen_ref, choices)
        signal = conv.signal(acc_ref[: conv.length, :], acc_ref[conv.length :, :])
        kept = jnp.where(conv.row >= conv.facts[1], signal, 0.0)
        out_ref[0, 0] = near_ref[:, conv.lanes] + kept

    @pl.when(jnp.logical_not(reaches))
    def _():
        out_ref[0, 0] = near_ref[:, conv.lanes]


def conv_call(body, tabs, facts, arrays, out_shape, out_spec, scratch, after=(), result=None):
    table, back, spectra = tabs
    length = table.shape[0] // 2
    width = spectra.shape[2]
    operands = [facts, table, back, spectra, *arrays]
    specs = [SCALARS] + [WHOLE] * (len(operands) - 1) + [ANYWHERE] * len(after)
    operands.extend(after)
    aliases = {}
    if result is not None:
        aliases = {len(operands): 0}
        operands.append(result)
        specs.append(ANYWHERE)
    return pl.pallas_call(
        body,
        grid=(width // LANES,),
        out_shape=out_shape,
        in_specs=specs,
        out_specs=out_spec,
        scratch_shapes=scratch,
        input_output_aliases=aliases,
        compiler_params=params(),
        cost_estimate=pl.CostEstimate(
            flops=32 * length * length * width,
            bytes_accessed=4 * length * width,
            transcendentals=0,
        ),
    )(*operands)


def own_terms(slot, tabs, facts, pieces, after=()):
    _, back, spectra = tabs
    shape = pltpu.VMEM((back.shape[0], spectra.shape[2]), F32)
    body = functools.partial(own_kernel, slot, len(pieces))
    return conv_call(body, tabs, facts, pieces, shape, WHOLE, [], after)


def far_terms(slot, count, tabs, facts, arrays, result=None):
    _, back, spectra = tabs
    length, width = back.shape[0], spectra.shape[2]
    shape = jax.ShapeDtypeStruct((1, 2, length, width), F32)
    spec = pl.BlockSpec((1, 1, length, LANES), lambda c: (0, slot, 0, c))
    scratch = [pltpu.VMEM((2 * length, LANES), F32), pltpu.VMEM((length, LANES), BF16)]
    body = functools.partial(far_kernel, slot, count)
    if slot == 1:
        shape, spec = (shape, pltpu.VMEM((8, 128), F32)), (spec, WHOLE)
    return conv_call(body, tabs, facts, arrays, shape, spec, scratch, (), result)


def ordered(value, *earlier):
    return pl.pallas_call(
        lambda *refs: None,
        out_shape=jax.ShapeDtypeStruct(value.shape, value.dtype),
        in_specs=[ANYWHERE] * (1 + len(earlier)),
        out_specs=ANYWHERE,
        input_output_aliases={0: 0},
        compiler_params=params(VMEM // 20),
    )(value, *earlier)


def shifted(value, steps):
    count = lax.axis_size("ctx")
    initial, last = (max(0, -steps), min(count, count - steps))
    return lax.ppermute(value, "ctx", [(source, source + steps) for source in range(initial, last)])


def core_swapped(value):
    count = lax.axis_size("ctx")
    return lax.ppermute(value, "ctx", [(source, source ^ 1) for source in range(count)])


def upper_halo_of(value):
    count = lax.axis_size("ctx")
    far = [(source, source + 3) for source in range(1, count - 3, 2)] + [(count - 1, count - 3)]
    two = shifted(value, 2)
    mate, far = core_swapped(value), lax.ppermute(value, "ctx", far)
    return [two, core_swapped(two), mate, far]


def lower_halo_of(value, own):
    count = lax.axis_size("ctx")
    mixed = [(source, source - 1) for source in range(1, count, 2)]
    mixed += [(source, source - 3) for source in range(4, count, 2)]
    two = ordered(shifted(value, -2), own)
    mixed = lax.ppermute(value, "ctx", mixed)
    return [two, core_swapped(two), mixed]


def on_device(grad_out, out_weight, gate, filter_taps, doc_starts):
    pairs = lax.axis_size("ctx")
    place = lax.axis_index("ctx")
    length = grad_out.shape[2]
    width = out_weight.shape[0]
    count = lax.axis_size("ch")
    lane = lax.axis_index("ch").astype(jnp.int32)[None]
    around = [(source, (source + 1) % count) for source in range(count)]
    everything = tuple(range(count))

    def turned(piece):
        return lax.ppermute(piece, "ch", around)

    upper_in = [grad_out[0, 1]]
    upper_in.append(turned(upper_in[0]))

    table, back = (jnp.asarray(one) for one in tables(length))
    spectra, weight, gates, lower_slice, table, back, facts, prepared = prepare(
        pairs,
        place.astype(jnp.int32)[None],
        lane,
        doc_starts,
        table,
        back,
        filter_taps,
        out_weight,
        gate,
        grad_out,
    )
    tabs = (table, back, spectra)

    upper_in[1] = ordered(upper_in[1], prepared)
    for step in range(2, count):
        upper_in.append(turned(upper_in[-1]))
    def partial_of(shards, slot):
        return project(facts, shards, everything[:-1], weight, gates, slot, 0, last=False)

    def final_of(shard, slot, partial, after=()):
        last = everything[-1:]
        return project(facts, [shard], last, weight, gates, slot, 0, partial, after=after)

    partial = partial_of(upper_in[:-1], 1)
    lower_in = [ordered(lower_slice, upper_in[-1], partial)]
    upper = final_of(upper_in[-1], 1, partial)
    upper_halo = upper_halo_of(upper)
    two, swapped, mate, fold = upper_halo
    lower_in.append(ordered(turned(lower_in[0]), upper, mate))
    near = own_terms(1, tabs, facts, [upper])
    for step in range(2, count):
        received = turned(lower_in[-1])
        if step == count - 1:
            lower_in.append(received)
        else:
            lower_in.append(ordered(received, near, two, fold))
    result, convolved = far_terms(1, 1, tabs, facts, [near, *upper_halo])

    partial = partial_of(lower_in[:-1], 0)
    lower = final_of(lower_in[-1], 0, partial, [swapped, convolved])
    near = own_terms(0, tabs, facts, [lower])
    lower_halo = lower_halo_of(lower, near)
    arrays = [near, upper, mate, two, fold, *lower_halo]
    return far_terms(0, 1, tabs, facts, arrays, result)


def solution(mesh):
    in_specs = (
        P("ctx", None, None, "ch"),
        P("ch", None),
        P("ctx", None, None, "ch"),
        P(None, "ch"),
        P(),
    )
    out_specs = P("ctx", None, None, "ch")
    return jax.shard_map(
        on_device, mesh=mesh, in_specs=in_specs, out_specs=out_specs, check_vma=False
    )
```

```python
import functools
import math

import jax
import jax.numpy as jnp
import ml_dtypes
import numpy as np
from jax import lax
from jax.experimental import pallas as pl
from jax.experimental.pallas import tpu as pltpu
from jax.sharding import PartitionSpec as P

REACH = 3
LANES = 256
VMEM = 20 * 1024 * 1024
F32 = jnp.float32
BF16 = jnp.bfloat16
WHOLE = pl.BlockSpec(memory_space=pltpu.VMEM)
ANYWHERE = pl.BlockSpec(memory_space=pl.ANY)
OUTSIDE = pl.BlockSpec(memory_space=pltpu.HBM)
SCALARS = pl.BlockSpec(memory_space=pltpu.SMEM)


def parts_of(table):
    high = table.astype(np.float32).astype(ml_dtypes.bfloat16)
    low = (table - high.astype(np.float64)).astype(np.float32).astype(ml_dtypes.bfloat16)
    return high, low


@functools.lru_cache(maxsize=None)
def tables(length):
    angle = np.outer(2 * np.arange(length) + 1, np.arange(length)) % (4 * length)
    angle = angle.astype(np.float64) * (math.pi / (2 * length))
    forward = np.concatenate([np.cos(angle), -np.sin(angle)], axis=0)
    high, low = parts_of(forward)
    back_high, back_low = parts_of(forward.T / length)
    return np.concatenate([high, low], axis=1), np.concatenate([back_high, back_low], axis=1)


def nn(a, b):
    return lax.dot_general(a, b, (((1,), (0,)), ((), ())), preferred_element_type=F32)


def nt(a, b):
    return lax.dot_general(a, b, (((1,), (1,)), ((), ())), preferred_element_type=F32)


def params(limit=VMEM):
    return pltpu.CompilerParams(vmem_limit_bytes=limit)


def lanes_at(tile):
    return pl.ds(pl.multiple_of(tile * LANES, LANES), LANES)


def write_facts(facts_ref, slot, docs_ref, block, length, end, inner, role):
    start = block * length
    stop = start + length - 1

    def visit(at, found):
        first, following, last = found
        here = docs_ref[at]
        first = jnp.minimum(first, jnp.where(here > start, here, end))
        following = jnp.minimum(following, jnp.where(here > stop, here, end))
        last = jnp.maximum(last, jnp.where(here <= stop, here, 0))
        return first, following, last

    whole = jnp.int32(end)
    first, following, last = lax.fori_loop(
        0, docs_ref.shape[0], visit, (whole, whole, jnp.int32(0))
    )
    facts_ref[slot, 0] = jnp.clip(first - start, 0, length)
    facts_ref[slot, 1] = jnp.clip(last - start, 0, length)
    for distance in range(1, REACH + 1):
        facts_ref[slot, 1 + distance] = jnp.clip(following - start - distance * length, 0, length)
    facts_ref[slot, 2 + REACH] = inner
    facts_ref[slot, 3 + REACH] = role


def prepare_kernel(pairs, *refs):
    place_ref, lane_ref, docs_ref, table_ref, back_ref, taps_ref = refs[:6]
    weight_ref, gate_ref, grad_ref = refs[6:9]
    spec_out, weight_out, gate_out, lower_out, table_out, back_out = refs[9:15]
    facts_out, token_out, sems = refs[15:]
    token_out[...] = jnp.zeros_like(token_out)
    copies = [
        pltpu.make_async_copy(source, target, sems.at[at])
        for at, (source, target) in enumerate(
            [
                (grad_ref.at[0, 0], lower_out),
                (weight_ref, weight_out),
                (gate_ref, gate_out),
                (back_ref, back_out),
            ]
        )
    ]
    step = pl.program_id(0)
    length = table_ref.shape[1] // 2

    @pl.when(step == 0)
    def _():
        for copy in copies:
            copy.start()
        table_out[...] = table_ref[:, :length]
        place = place_ref[0]
        odd = lax.rem(place, 2)
        role = jnp.where(place >= pairs - 3, pairs - place, 0)
        end = 2 * pairs * length
        for slot in range(2):
            facts_out[slot, 4 + REACH] = lane_ref[0]
        write_facts(facts_out, 0, docs_ref, place, length, end, 1 - odd, role)
        write_facts(facts_out, 1, docs_ref, 2 * pairs - 1 - place, length, end, odd, role)

    freq = lax.broadcasted_iota(jnp.int32, (length, 1), 0)
    sign = jnp.where(freq % 2 == 0, 1.0, -1.0).astype(F32)
    lanes = lanes_at(step)
    before = None
    for part in range(REACH + 1):
        if part < REACH:
            values = taps_ref[part * length : (part + 1) * length, :]
            high = values.astype(BF16)
            low = (values - high.astype(F32)).astype(BF16)
            full = nn(table_ref[...], jnp.concatenate([high, high], axis=0))
            full = full + nn(table_ref[:, :length], low)
            now = (full[:length], -full[length:])
        else:
            now = None
        if before is None:
            real, imag = now
        else:
            real, imag = sign * before[1], -sign * before[0]
            if now is not None:
                real, imag = now[0] + real, now[1] + imag
        spec_out[part, :length, lanes] = real
        spec_out[part, length:, lanes] = imag
        before = now

    @pl.when(step == pl.num_programs(0) - 1)
    def _():
        for copy in copies:
            copy.wait()


def prepare(pairs, place, lane, docs, table, back, taps, weight, gate, grad):
    count, width = taps.shape
    length = count // REACH
    return pl.pallas_call(
        functools.partial(prepare_kernel, pairs),
        grid=(width // LANES,),
        out_shape=(
            pltpu.VMEM((REACH + 1, 2 * length, width), F32),
            pltpu.VMEM(weight.shape, BF16),
            pltpu.VMEM(gate.shape, BF16),
            pltpu.VMEM(grad.shape[2:], BF16),
            pltpu.VMEM((2 * length, length), BF16),
            pltpu.VMEM(back.shape, BF16),
            pltpu.SMEM((2, 8), jnp.int32),
            pltpu.VMEM((8, 128), F32),
        ),
        in_specs=[
            SCALARS,
            SCALARS,
            SCALARS,
            pl.BlockSpec((2 * length, 2 * length), lambda c: (0, 0)),
            OUTSIDE,
            pl.BlockSpec((count, LANES), lambda c: (0, c)),
            OUTSIDE,
            OUTSIDE,
            OUTSIDE,
        ],
        out_specs=(WHOLE,) * 6 + (SCALARS, WHOLE),
        scratch_shapes=[pltpu.SemaphoreType.DMA((4,))],
        compiler_params=params(2 * VMEM),
        cost_estimate=pl.CostEstimate(
            flops=2 * 3 * 2 * count * length * width,
            bytes_accessed=4 * (count * width + 8 * length * width),
            transcendentals=0,
        ),
    )(place, lane, docs, table, back, taps, weight, gate, grad)


def project_kernel(hops, slot, first, last, facts_ref, *refs):
    shards, refs = refs[: len(hops)], refs[len(hops) :]
    weight_ref, gate_ref = refs[:2]
    before_ref = None if first else refs[2]
    out_ref, acc_ref = refs[-2:] if last else (refs[-1], refs[-1])
    depth = shards[0].shape[1]
    count = weight_ref.shape[1] // depth
    tiles = [pl.ds(tile * LANES, LANES) for tile in range(weight_ref.shape[0] // LANES)]
    if not first:
        acc_ref[...] = before_ref[...]
    for shard, hop in zip(shards, hops):
        at = facts_ref[0, 4 + REACH] + hop
        features = pl.ds(pl.multiple_of(jnp.clip(at, 0, count - 1) * depth, depth), depth)

        def add(shard=shard, hop=hop, features=features):
            for lanes in tiles:
                part = nt(shard[...], weight_ref[lanes, features])
                if hop == 0:
                    acc_ref[:, lanes] = part
                else:
                    acc_ref[:, lanes] += part

        if hop == 0:
            add()
        else:
            pl.when((at >= 0) & (at < count))(add)
    if last:
        out_ref[...] = (acc_ref[...] * gate_ref[0, slot].astype(F32)).astype(BF16)


def project(facts, shards, hops, weight, gate, slot, before=None, last=True, after=()):
    rows, depth = shards[0].shape
    width = weight.shape[0]
    operands = [facts, *shards, weight, gate]
    if before is not None:
        operands.append(before)
    return pl.pallas_call(
        functools.partial(project_kernel, hops, slot, before is None, last),
        out_shape=pltpu.VMEM((rows, width), BF16 if last else F32),
        in_specs=[SCALARS] + [WHOLE] * (len(operands) - 1) + [ANYWHERE] * len(after),
        out_specs=WHOLE,
        scratch_shapes=[pltpu.VMEM((rows, width), F32)] if last else [],
        compiler_params=params(),
        cost_estimate=pl.CostEstimate(
            flops=2 * rows * depth * (len(shards) + 1) // 2 * width,
            bytes_accessed=2 * (rows + width) * depth * len(shards),
            transcendentals=0,
        ),
    )(*operands, *after)


class Conv:
    def __init__(self, slot, facts, table, back, spectra):
        self.facts = [facts[slot, at] for at in range(4 + REACH)]
        self.table, self.back, self.spectra = table, back, spectra
        self.length = table.shape[0] // 2
        self.lanes = lanes_at(pl.program_id(0))
        self.row = lax.broadcasted_iota(jnp.int32, (self.length, LANES), 0)

    def joined(self, pieces):
        tiles = [piece[:, self.lanes] for piece in pieces]
        return tiles[0] if len(tiles) == 1 else jnp.concatenate(tiles, axis=0)

    def within(self, low, high):
        return (self.row >= low) & (self.row < high)

    def term(self, values, low, high, distance):
        length = self.length
        kept = jnp.where(self.within(low, high), values.astype(F32), 0.0).astype(BF16)
        full = nn(self.table[...], kept)
        real, imag = full[:length], full[length:]
        k_real = self.spectra[distance, :length, self.lanes]
        k_imag = self.spectra[distance, length:, self.lanes]
        return k_real * real - k_imag * imag, k_real * imag + k_imag * real

    def signal(self, real, imag):
        real, imag = real.astype(BF16), imag.astype(BF16)
        return nn(self.back[...], jnp.concatenate([real, imag, real, imag], axis=0))

    def far_terms(self, acc, chosen, choices):
        for distance in range(1, REACH + 1):
            reach = self.facts[1 + distance]

            @pl.when(reach > 0)
            def _(distance=distance, reach=reach):
                for pieces, holds in choices(distance):

                    @pl.when(holds)
                    def _(pieces=pieces):
                        chosen[...] = self.joined(pieces)

                real, imag = self.term(chosen[...], 0, reach, distance)
                acc[: self.length, :] += real
                acc[self.length :, :] += imag

    def inner_documents(self, own, read, write):
        first_end, last_start = self.facts[0], self.facts[1]

        @pl.when(last_start > 0)
        def _():
            signal = self.signal(*self.term(own, 0, first_end, 0))
            write(jnp.where(self.row < first_end, signal, read()))

        @pl.when(last_start > first_end)
        def _():
            signal = self.signal(*self.term(own, first_end, last_start, 0))
            write(jnp.where(self.within(first_end, last_start), signal, read()))

    def halo(self, pieces, distance, mixed):
        sets = 3 if mixed else 4
        count = len(pieces) // sets
        kinds = [pieces[at * count : (at + 1) * count] for at in range(sets)]
        two, swapped, mate, far = kinds[0], kinds[1], kinds[2], kinds[-1]
        inner = self.facts[5]
        if distance == 2:
            return [(two, inner >= 0)]
        if distance == 1:
            return [(mate, inner == 1), (swapped, inner == 0)]
        return [(swapped, inner == 1), (far, inner == 0)]


def own_kernel(slot, pieces, facts_ref, table_ref, back_ref, spec_ref, *refs):
    own_refs, out_ref = refs[:pieces], refs[-1]
    conv = Conv(slot, facts_ref, table_ref, back_ref, spec_ref)
    own = conv.joined(own_refs)
    out_ref[:, conv.lanes] = conv.signal(*conv.term(own, conv.facts[1], conv.length, 0))

    def write(value):
        out_ref[:, conv.lanes] = value

    conv.inner_documents(own, lambda: out_ref[:, conv.lanes], write)


def far_kernel(slot, pieces, facts_ref, table_ref, back_ref, spec_ref, *refs):
    near_ref, refs = refs[0], refs[1:]
    if slot == 0:
        upper_ref, mate_ref, two_ref, fold_ref = refs[:4]
        halos = refs[4 : 4 + 3 * pieces]
    else:
        halos = refs[: 4 * pieces]
    out_ref, acc_ref, chosen_ref = refs[-3:]
    if slot == 1:
        out_ref, token_ref = refs[-4:-2]
        token_ref[...] = jnp.zeros_like(token_ref)
    conv = Conv(slot, facts_ref, table_ref, back_ref, spec_ref)
    role = conv.facts[6]

    def choices(distance):
        found = conv.halo(halos, distance, slot == 0)
        if slot == 0:
            folded = {
                1: [([upper_ref], role == 1)],
                2: [([mate_ref], (role == 1) | (role == 2))],
                3: [([two_ref], role == 1), ([upper_ref], role == 2), ([fold_ref], role == 3)],
            }
            found = found + folded[distance]
        return found

    reaches = conv.facts[2] > 0

    @pl.when(reaches)
    def _():
        acc_ref[...] = jnp.zeros_like(acc_ref)
        conv.far_terms(acc_ref, chosen_ref, choices)
        signal = conv.signal(acc_ref[: conv.length, :], acc_ref[conv.length :, :])
        kept = jnp.where(conv.row >= conv.facts[1], signal, 0.0)
        out_ref[0, 0] = near_ref[:, conv.lanes] + kept

    @pl.when(jnp.logical_not(reaches))
    def _():
        out_ref[0, 0] = near_ref[:, conv.lanes]


def conv_call(body, tabs, facts, arrays, out_shape, out_spec, scratch, after=(), result=None):
    table, back, spectra = tabs
    length = table.shape[0] // 2
    width = spectra.shape[2]
    operands = [facts, table, back, spectra, *arrays]
    specs = [SCALARS] + [WHOLE] * (len(operands) - 1) + [ANYWHERE] * len(after)
    operands.extend(after)
    aliases = {}
    if result is not None:
        aliases = {len(operands): 0}
        operands.append(result)
        specs.append(ANYWHERE)
    return pl.pallas_call(
        body,
        grid=(width // LANES,),
        out_shape=out_shape,
        in_specs=specs,
        out_specs=out_spec,
        scratch_shapes=scratch,
        input_output_aliases=aliases,
        compiler_params=params(),
        cost_estimate=pl.CostEstimate(
            flops=32 * length * length * width,
            bytes_accessed=4 * length * width,
            transcendentals=0,
        ),
    )(*operands)


def own_terms(slot, tabs, facts, pieces, after=()):
    _, back, spectra = tabs
    shape = pltpu.VMEM((back.shape[0], spectra.shape[2]), F32)
    body = functools.partial(own_kernel, slot, len(pieces))
    return conv_call(body, tabs, facts, pieces, shape, WHOLE, [], after)


def far_terms(slot, count, tabs, facts, arrays, result=None):
    _, back, spectra = tabs
    length, width = back.shape[0], spectra.shape[2]
    shape = jax.ShapeDtypeStruct((1, 2, length, width), F32)
    spec = pl.BlockSpec((1, 1, length, LANES), lambda c: (0, slot, 0, c))
    scratch = [pltpu.VMEM((2 * length, LANES), F32), pltpu.VMEM((length, LANES), BF16)]
    body = functools.partial(far_kernel, slot, count)
    if slot == 1:
        shape, spec = (shape, pltpu.VMEM((8, 128), F32)), (spec, WHOLE)
    return conv_call(body, tabs, facts, arrays, shape, spec, scratch, (), result)


def ordered(value, *earlier):
    return pl.pallas_call(
        lambda *refs: None,
        out_shape=jax.ShapeDtypeStruct(value.shape, value.dtype),
        in_specs=[ANYWHERE] * (1 + len(earlier)),
        out_specs=ANYWHERE,
        input_output_aliases={0: 0},
        compiler_params=params(VMEM // 20),
    )(value, *earlier)


def shifted(value, steps):
    count = lax.axis_size("ctx")
    initial, last = (max(0, -steps), min(count, count - steps))
    return lax.ppermute(value, "ctx", [(source, source + steps) for source in range(initial, last)])


def core_swapped(value):
    count = lax.axis_size("ctx")
    return lax.ppermute(value, "ctx", [(source, source ^ 1) for source in range(count)])


def upper_halo_of(value):
    count = lax.axis_size("ctx")
    far = [(source, source + 3) for source in range(1, count - 3, 2)] + [(count - 1, count - 3)]
    two = shifted(value, 2)
    mate, far = core_swapped(value), lax.ppermute(value, "ctx", far)
    return [two, core_swapped(two), mate, far]


def lower_halo_of(value, own):
    count = lax.axis_size("ctx")
    mixed = [(source, source - 1) for source in range(1, count, 2)]
    mixed += [(source, source - 3) for source in range(4, count, 2)]
    two = ordered(shifted(value, -2), own)
    mixed = lax.ppermute(value, "ctx", mixed)
    return [two, core_swapped(two), mixed]


def on_device(grad_out, out_weight, gate, filter_taps, doc_starts):
    pairs = lax.axis_size("ctx")
    place = lax.axis_index("ctx")
    length = grad_out.shape[2]
    width = out_weight.shape[0]
    count = lax.axis_size("ch")
    lane = lax.axis_index("ch").astype(jnp.int32)[None]

    def sent(step, up, down):
        upward = [(source, source + 1) for source in range(step - 1, count - 1)]
        downward = [(source, source - 1) for source in range(1, count - step + 1)]
        return lax.ppermute(up, "ch", upward), lax.ppermute(down, "ch", downward)

    start = grad_out[0, 1]
    upper_in = [sent(1, start, start)]

    table, back = (jnp.asarray(one) for one in tables(length))
    spectra, weight, gates, lower_slice, table, back, facts, prepared = prepare(
        pairs,
        place.astype(jnp.int32)[None],
        lane,
        doc_starts,
        table,
        back,
        filter_taps,
        out_weight,
        gate,
        grad_out,
    )
    tabs = (table, back, spectra)

    def pass_on(chain, *earlier):
        if earlier:
            chain[-1] = [ordered(one, *earlier) for one in chain[-1]]
        chain.append(sent(len(chain) + 1, *chain[-1]))

    hops = [0] + [way * step for step in range(1, count) for way in (-1, 1)]

    def partial_of(own, arrived, slot):
        shards = [own] + [one for pair in arrived[: count - 2] for one in pair]
        return project(facts, shards, hops[:-2], weight, gates, slot, last=False)

    def final_of(arrived, slot, partial, after=()):
        return project(facts, arrived[-1], hops[-2:], weight, gates, slot, partial, after=after)

    pass_on(upper_in, prepared)
    for _ in range(3, count):
        pass_on(upper_in)
    partial = partial_of(start, upper_in, 1)
    own = ordered(lower_slice, *upper_in[-1], partial)
    lower_in = [sent(1, own, own)]
    upper = final_of(upper_in, 1, partial)
    upper_halo = upper_halo_of(upper)
    two, swapped, mate, fold = upper_halo
    pass_on(lower_in, upper)
    near = own_terms(1, tabs, facts, [upper])
    for _ in range(3, count):
        pass_on(lower_in, near, two, mate, fold)
    result, convolved = far_terms(1, 1, tabs, facts, [near, *upper_halo])

    partial = partial_of(own, lower_in, 0)
    lower = final_of(lower_in, 0, partial, [swapped, convolved])
    near = own_terms(0, tabs, facts, [lower])
    lower_halo = lower_halo_of(lower, near)
    arrays = [near, upper, mate, two, fold, *lower_halo]
    return far_terms(0, 1, tabs, facts, arrays, result)


def solution(mesh):
    in_specs = (
        P("ctx", None, None, "ch"),
        P("ch", None),
        P("ctx", None, None, "ch"),
        P(None, "ch"),
        P(),
    )
    out_specs = P("ctx", None, None, "ch")
    return jax.shard_map(
        on_device, mesh=mesh, in_specs=in_specs, out_specs=out_specs, check_vma=False
    )
```

```python
import functools
import math

import jax
import jax.numpy as jnp
import ml_dtypes
import numpy as np
from jax import lax
from jax.experimental import pallas as pl
from jax.experimental.pallas import tpu as pltpu
from jax.sharding import PartitionSpec as P

REACH = 3
LANES = 256
VMEM = 20 * 1024 * 1024
F32 = jnp.float32
BF16 = jnp.bfloat16
WHOLE = pl.BlockSpec(memory_space=pltpu.VMEM)
ANYWHERE = pl.BlockSpec(memory_space=pl.ANY)
OUTSIDE = pl.BlockSpec(memory_space=pltpu.HBM)
SCALARS = pl.BlockSpec(memory_space=pltpu.SMEM)


def parts_of(table):
    high = table.astype(np.float32).astype(ml_dtypes.bfloat16)
    low = (table - high.astype(np.float64)).astype(np.float32).astype(ml_dtypes.bfloat16)
    return high, low


@functools.lru_cache(maxsize=None)
def tables(length):
    angle = np.outer(2 * np.arange(length) + 1, np.arange(length)) % (4 * length)
    angle = angle.astype(np.float64) * (math.pi / (2 * length))
    forward = np.concatenate([np.cos(angle), -np.sin(angle)], axis=0)
    high, low = parts_of(forward)
    back_high, back_low = parts_of(forward.T / length)
    return np.concatenate([high, low], axis=1), np.concatenate([back_high, back_low], axis=0)


def nn(a, b):
    return lax.dot_general(a, b, (((1,), (0,)), ((), ())), preferred_element_type=F32)


def nt(a, b):
    return lax.dot_general(a, b, (((1,), (1,)), ((), ())), preferred_element_type=F32)


def params(limit=VMEM):
    return pltpu.CompilerParams(vmem_limit_bytes=limit)


def lanes_at(tile):
    return pl.ds(pl.multiple_of(tile * LANES, LANES), LANES)


def write_facts(facts_ref, slot, docs_ref, block, length, end, inner, role):
    start = block * length
    stop = start + length - 1

    def visit(at, found):
        first, following, last = found
        here = docs_ref[at]
        first = jnp.minimum(first, jnp.where(here > start, here, end))
        following = jnp.minimum(following, jnp.where(here > stop, here, end))
        last = jnp.maximum(last, jnp.where(here <= stop, here, 0))
        return first, following, last

    whole = jnp.int32(end)
    first, following, last = lax.fori_loop(
        0, docs_ref.shape[0], visit, (whole, whole, jnp.int32(0))
    )
    facts_ref[slot, 0] = jnp.clip(first - start, 0, length)
    facts_ref[slot, 1] = jnp.clip(last - start, 0, length)
    for distance in range(1, REACH + 1):
        facts_ref[slot, 1 + distance] = jnp.clip(following - start - distance * length, 0, length)
    facts_ref[slot, 2 + REACH] = inner
    facts_ref[slot, 3 + REACH] = role


def prepare_kernel(pairs, *refs):
    place_ref, lane_ref, docs_ref, table_ref, back_ref, taps_ref = refs[:6]
    weight_ref, gate_ref, grad_ref = refs[6:9]
    spec_out, weight_out, gate_out, lower_out, table_out, back_out = refs[9:15]
    facts_out, token_out, sems = refs[15:]
    token_out[...] = jnp.zeros_like(token_out)
    copies = [
        pltpu.make_async_copy(source, target, sems.at[at])
        for at, (source, target) in enumerate(
            [
                (grad_ref.at[0, 0], lower_out),
                (weight_ref, weight_out),
                (gate_ref, gate_out),
                (back_ref, back_out),
            ]
        )
    ]
    step = pl.program_id(0)
    length = table_ref.shape[1] // 2

    @pl.when(step == 0)
    def _():
        for copy in copies:
            copy.start()
        table_out[...] = table_ref[:, :length]
        place = place_ref[0]
        odd = lax.rem(place, 2)
        role = jnp.where(place >= pairs - 3, pairs - place, 0)
        end = 2 * pairs * length
        for slot in range(2):
            facts_out[slot, 4 + REACH] = lane_ref[0]
        write_facts(facts_out, 0, docs_ref, place, length, end, 1 - odd, role)
        write_facts(facts_out, 1, docs_ref, 2 * pairs - 1 - place, length, end, odd, role)

    freq = lax.broadcasted_iota(jnp.int32, (length, 1), 0)
    sign = jnp.where(freq % 2 == 0, 1.0, -1.0).astype(F32)
    lanes = lanes_at(step)
    before = None
    for part in range(REACH + 1):
        if part < REACH:
            values = taps_ref[part * length : (part + 1) * length, :]
            high = values.astype(BF16)
            low = (values - high.astype(F32)).astype(BF16)
            full = nn(table_ref[...], jnp.concatenate([high, high], axis=0))
            full = full + nn(table_ref[:, :length], low)
            now = (full[:length], -full[length:])
        else:
            now = None
        if before is None:
            real, imag = now
        else:
            real, imag = sign * before[1], -sign * before[0]
            if now is not None:
                real, imag = now[0] + real, now[1] + imag
        spec_out[part, :length, lanes] = real
        spec_out[part, length:, lanes] = imag
        before = now

    @pl.when(step == pl.num_programs(0) - 1)
    def _():
        for copy in copies:
            copy.wait()


def prepare(pairs, place, lane, docs, table, back, taps, weight, gate, grad):
    count, width = taps.shape
    length = count // REACH
    return pl.pallas_call(
        functools.partial(prepare_kernel, pairs),
        grid=(width // LANES,),
        out_shape=(
            pltpu.VMEM((REACH + 1, 2 * length, width), F32),
            pltpu.VMEM(weight.shape, BF16),
            pltpu.VMEM(gate.shape, BF16),
            pltpu.VMEM(grad.shape[2:], BF16),
            pltpu.VMEM((2 * length, length), BF16),
            pltpu.VMEM(back.shape, BF16),
            pltpu.SMEM((2, 8), jnp.int32),
            pltpu.VMEM((8, 128), F32),
        ),
        in_specs=[
            SCALARS,
            SCALARS,
            SCALARS,
            pl.BlockSpec((2 * length, 2 * length), lambda c: (0, 0)),
            OUTSIDE,
            pl.BlockSpec((count, LANES), lambda c: (0, c)),
            OUTSIDE,
            OUTSIDE,
            OUTSIDE,
        ],
        out_specs=(WHOLE,) * 6 + (SCALARS, WHOLE),
        scratch_shapes=[pltpu.SemaphoreType.DMA((4,))],
        compiler_params=params(2 * VMEM),
        cost_estimate=pl.CostEstimate(
            flops=2 * 3 * 2 * count * length * width,
            bytes_accessed=4 * (count * width + 8 * length * width),
            transcendentals=0,
        ),
    )(place, lane, docs, table, back, taps, weight, gate, grad)


def project_kernel(hops, slot, first, last, facts_ref, *refs):
    shards, refs = refs[: len(hops)], refs[len(hops) :]
    weight_ref, gate_ref = refs[:2]
    before_ref = None if first else refs[2]
    out_ref, acc_ref = refs[-2:] if last else (refs[-1], refs[-1])
    depth = shards[0].shape[1]
    count = weight_ref.shape[1] // depth
    tiles = [pl.ds(tile * LANES, LANES) for tile in range(weight_ref.shape[0] // LANES)]
    if not first:
        acc_ref[...] = before_ref[...]
    for shard, hop in zip(shards, hops):
        at = facts_ref[0, 4 + REACH] + hop
        features = pl.ds(pl.multiple_of(jnp.clip(at, 0, count - 1) * depth, depth), depth)

        def add(shard=shard, hop=hop, features=features):
            for lanes in tiles:
                part = nt(shard[...], weight_ref[lanes, features])
                if hop == 0:
                    acc_ref[:, lanes] = part
                else:
                    acc_ref[:, lanes] += part

        if hop == 0:
            add()
        else:
            pl.when((at >= 0) & (at < count))(add)
    if last:
        out_ref[...] = (acc_ref[...] * gate_ref[0, slot].astype(F32)).astype(BF16)


def project(facts, shards, hops, weight, gate, slot, before=None, last=True, after=()):
    rows, depth = shards[0].shape
    width = weight.shape[0]
    operands = [facts, *shards, weight, gate]
    if before is not None:
        operands.append(before)
    return pl.pallas_call(
        functools.partial(project_kernel, hops, slot, before is None, last),
        out_shape=pltpu.VMEM((rows, width), BF16 if last else F32),
        in_specs=[SCALARS] + [WHOLE] * (len(operands) - 1) + [ANYWHERE] * len(after),
        out_specs=WHOLE,
        scratch_shapes=[pltpu.VMEM((rows, width), F32)] if last else [],
        compiler_params=params(),
        cost_estimate=pl.CostEstimate(
            flops=2 * rows * depth * (len(shards) + 1) // 2 * width,
            bytes_accessed=2 * (rows + width) * depth * len(shards),
            transcendentals=0,
        ),
    )(*operands, *after)


class Conv:
    def __init__(self, slot, facts, table, back, spectra):
        self.facts = [facts[slot, at] for at in range(4 + REACH)]
        self.table, self.back, self.spectra = table, back, spectra
        self.length = table.shape[0] // 2
        self.lanes = lanes_at(pl.program_id(0))
        self.row = lax.broadcasted_iota(jnp.int32, (self.length, LANES), 0)

    def joined(self, pieces):
        tiles = [piece[:, self.lanes] for piece in pieces]
        return tiles[0] if len(tiles) == 1 else jnp.concatenate(tiles, axis=0)

    def within(self, low, high):
        return (self.row >= low) & (self.row < high)

    def term(self, values, low, high, distance):
        length = self.length
        kept = jnp.where(self.within(low, high), values.astype(F32), 0.0).astype(BF16)
        full = nn(self.table[...], kept)
        real, imag = full[:length], full[length:]
        k_real = self.spectra[distance, :length, self.lanes]
        k_imag = self.spectra[distance, length:, self.lanes]
        return k_real * real - k_imag * imag, k_real * imag + k_imag * real

    def signal(self, real, imag):
        total = jnp.concatenate([real.astype(BF16), imag.astype(BF16)], axis=0)
        both = nn(self.back[...], total)
        return both[: self.length] + both[self.length :]

    def far_terms(self, acc, chosen, choices):
        for distance in range(1, REACH + 1):
            reach = self.facts[1 + distance]

            @pl.when(reach > 0)
            def _(distance=distance, reach=reach):
                for pieces, holds in choices(distance):

                    @pl.when(holds)
                    def _(pieces=pieces):
                        chosen[...] = self.joined(pieces)

                real, imag = self.term(chosen[...], 0, reach, distance)
                acc[: self.length, :] += real
                acc[self.length :, :] += imag

    def inner_documents(self, own, read, write):
        first_end, last_start = self.facts[0], self.facts[1]

        @pl.when(last_start > 0)
        def _():
            signal = self.signal(*self.term(own, 0, first_end, 0))
            write(jnp.where(self.row < first_end, signal, read()))

        @pl.when(last_start > first_end)
        def _():
            signal = self.signal(*self.term(own, first_end, last_start, 0))
            write(jnp.where(self.within(first_end, last_start), signal, read()))

    def halo(self, pieces, distance, mixed):
        sets = 3 if mixed else 4
        count = len(pieces) // sets
        kinds = [pieces[at * count : (at + 1) * count] for at in range(sets)]
        two, swapped, mate, far = kinds[0], kinds[1], kinds[2], kinds[-1]
        inner = self.facts[5]
        if distance == 2:
            return [(two, inner >= 0)]
        if distance == 1:
            return [(mate, inner == 1), (swapped, inner == 0)]
        return [(swapped, inner == 1), (far, inner == 0)]


def own_kernel(slot, pieces, facts_ref, table_ref, back_ref, spec_ref, *refs):
    own_refs, out_ref = refs[:pieces], refs[-1]
    conv = Conv(slot, facts_ref, table_ref, back_ref, spec_ref)
    own = conv.joined(own_refs)
    out_ref[:, conv.lanes] = conv.signal(*conv.term(own, conv.facts[1], conv.length, 0))

    def write(value):
        out_ref[:, conv.lanes] = value

    conv.inner_documents(own, lambda: out_ref[:, conv.lanes], write)


def far_kernel(slot, pieces, facts_ref, table_ref, back_ref, spec_ref, *refs):
    near_ref, refs = refs[0], refs[1:]
    if slot == 0:
        upper_ref, mate_ref, two_ref, fold_ref = refs[:4]
        halos = refs[4 : 4 + 3 * pieces]
    else:
        halos = refs[: 4 * pieces]
    out_ref, acc_ref, chosen_ref = refs[-3:]
    if slot == 1:
        out_ref, token_ref = refs[-4:-2]
        token_ref[...] = jnp.zeros_like(token_ref)
    conv = Conv(slot, facts_ref, table_ref, back_ref, spec_ref)
    role = conv.facts[6]

    def choices(distance):
        found = conv.halo(halos, distance, slot == 0)
        if slot == 0:
            folded = {
                1: [([upper_ref], role == 1)],
                2: [([mate_ref], (role == 1) | (role == 2))],
                3: [([two_ref], role == 1), ([upper_ref], role == 2), ([fold_ref], role == 3)],
            }
            found = found + folded[distance]
        return found

    reaches = conv.facts[2] > 0

    @pl.when(reaches)
    def _():
        acc_ref[...] = jnp.zeros_like(acc_ref)
        conv.far_terms(acc_ref, chosen_ref, choices)
        signal = conv.signal(acc_ref[: conv.length, :], acc_ref[conv.length :, :])
        kept = jnp.where(conv.row >= conv.facts[1], signal, 0.0)
        out_ref[0, 0] = near_ref[:, conv.lanes] + kept

    @pl.when(jnp.logical_not(reaches))
    def _():
        out_ref[0, 0] = near_ref[:, conv.lanes]


def conv_call(body, tabs, facts, arrays, out_shape, out_spec, scratch, after=(), result=None):
    table, back, spectra = tabs
    length = table.shape[0] // 2
    width = spectra.shape[2]
    operands = [facts, table, back, spectra, *arrays]
    specs = [SCALARS] + [WHOLE] * (len(operands) - 1) + [ANYWHERE] * len(after)
    operands.extend(after)
    aliases = {}
    if result is not None:
        aliases = {len(operands): 0}
        operands.append(result)
        specs.append(ANYWHERE)
    return pl.pallas_call(
        body,
        grid=(width // LANES,),
        out_shape=out_shape,
        in_specs=specs,
        out_specs=out_spec,
        scratch_shapes=scratch,
        input_output_aliases=aliases,
        compiler_params=params(),
        cost_estimate=pl.CostEstimate(
            flops=32 * length * length * width,
            bytes_accessed=4 * length * width,
            transcendentals=0,
        ),
    )(*operands)


def own_terms(slot, tabs, facts, pieces, after=()):
    _, back, spectra = tabs
    shape = pltpu.VMEM((back.shape[0] // 2, spectra.shape[2]), F32)
    body = functools.partial(own_kernel, slot, len(pieces))
    return conv_call(body, tabs, facts, pieces, shape, WHOLE, [], after)


def far_terms(slot, count, tabs, facts, arrays, result=None):
    _, back, spectra = tabs
    length, width = back.shape[0] // 2, spectra.shape[2]
    shape = jax.ShapeDtypeStruct((1, 2, length, width), F32)
    spec = pl.BlockSpec((1, 1, length, LANES), lambda c: (0, slot, 0, c))
    scratch = [pltpu.VMEM((2 * length, LANES), F32), pltpu.VMEM((length, LANES), BF16)]
    body = functools.partial(far_kernel, slot, count)
    if slot == 1:
        shape, spec = (shape, pltpu.VMEM((8, 128), F32)), (spec, WHOLE)
    return conv_call(body, tabs, facts, arrays, shape, spec, scratch, (), result)


def ordered(value, *earlier):
    return pl.pallas_call(
        lambda *refs: None,
        out_shape=jax.ShapeDtypeStruct(value.shape, value.dtype),
        in_specs=[ANYWHERE] * (1 + len(earlier)),
        out_specs=ANYWHERE,
        input_output_aliases={0: 0},
        compiler_params=params(VMEM // 20),
    )(value, *earlier)


def shifted(value, steps):
    count = lax.axis_size("ctx")
    initial, last = (max(0, -steps), min(count, count - steps))
    return lax.ppermute(value, "ctx", [(source, source + steps) for source in range(initial, last)])


def core_swapped(value):
    count = lax.axis_size("ctx")
    return lax.ppermute(value, "ctx", [(source, source ^ 1) for source in range(count)])


def upper_halo_of(value):
    count = lax.axis_size("ctx")
    far = [(source, source + 3) for source in range(1, count - 3, 2)] + [(count - 1, count - 3)]
    two = shifted(value, 2)
    mate, far = core_swapped(value), lax.ppermute(value, "ctx", far)
    return [two, core_swapped(two), mate, far]


def lower_halo_of(value, own):
    count = lax.axis_size("ctx")
    mixed = [(source, source - 1) for source in range(1, count, 2)]
    mixed += [(source, source - 3) for source in range(4, count, 2)]
    two = ordered(shifted(value, -2), own)
    mixed = lax.ppermute(value, "ctx", mixed)
    return [two, core_swapped(two), mixed]


def on_device(grad_out, out_weight, gate, filter_taps, doc_starts):
    pairs = lax.axis_size("ctx")
    place = lax.axis_index("ctx")
    length = grad_out.shape[2]
    width = out_weight.shape[0]
    count = lax.axis_size("ch")
    lane = lax.axis_index("ch").astype(jnp.int32)[None]

    def sent(step, up, down):
        upward = [(source, source + 1) for source in range(step - 1, count - 1)]
        downward = [(source, source - 1) for source in range(1, count - step + 1)]
        return lax.ppermute(up, "ch", upward), lax.ppermute(down, "ch", downward)

    start = grad_out[0, 1]
    upper_in = [sent(1, start, start)]

    table, back = (jnp.asarray(one) for one in tables(length))
    spectra, weight, gates, lower_slice, table, back, facts, prepared = prepare(
        pairs,
        place.astype(jnp.int32)[None],
        lane,
        doc_starts,
        table,
        back,
        filter_taps,
        out_weight,
        gate,
        grad_out,
    )
    tabs = (table, back, spectra)

    def pass_on(chain, *earlier):
        if earlier:
            chain[-1] = [ordered(one, *earlier) for one in chain[-1]]
        chain.append(sent(len(chain) + 1, *chain[-1]))

    hops = [0] + [way * step for step in range(1, count) for way in (-1, 1)]

    def partial_of(own, arrived, slot):
        shards = [own] + [one for pair in arrived[: count - 2] for one in pair]
        return project(facts, shards, hops[:-2], weight, gates, slot, last=False)

    def final_of(arrived, slot, partial, after=()):
        return project(facts, arrived[-1], hops[-2:], weight, gates, slot, partial, after=after)

    pass_on(upper_in, prepared)
    for _ in range(3, count):
        pass_on(upper_in)
    partial = partial_of(start, upper_in, 1)
    own = ordered(lower_slice, *upper_in[-1], partial)
    lower_in = [sent(1, own, own)]
    upper = final_of(upper_in, 1, partial)
    upper_halo = upper_halo_of(upper)
    two, swapped, mate, fold = upper_halo
    pass_on(lower_in, upper)
    near = own_terms(1, tabs, facts, [upper])
    for _ in range(3, count):
        pass_on(lower_in, near, two, mate, fold)
    result, convolved = far_terms(1, 1, tabs, facts, [near, *upper_halo])

    partial = partial_of(own, lower_in, 0)
    lower = final_of(lower_in, 0, partial, [swapped, convolved])
    near = own_terms(0, tabs, facts, [lower])
    lower_halo = lower_halo_of(lower, near)
    arrays = [near, upper, mate, two, fold, *lower_halo]
    return far_terms(0, 1, tabs, facts, arrays, result)


def solution(mesh):
    in_specs = (
        P("ctx", None, None, "ch"),
        P("ch", None),
        P("ctx", None, None, "ch"),
        P(None, "ch"),
        P(),
    )
    out_specs = P("ctx", None, None, "ch")
    return jax.shard_map(
        on_device, mesh=mesh, in_specs=in_specs, out_specs=out_specs, check_vma=False
    )
```

```python
import functools
import math

import jax
import jax.numpy as jnp
import ml_dtypes
import numpy as np
from jax import lax
from jax.experimental import pallas as pl
from jax.experimental.pallas import tpu as pltpu
from jax.sharding import PartitionSpec as P

REACH = 3
LANES = 512
VMEM = 20 * 1024 * 1024
F32 = jnp.float32
BF16 = jnp.bfloat16
WHOLE = pl.BlockSpec(memory_space=pltpu.VMEM)
ANYWHERE = pl.BlockSpec(memory_space=pl.ANY)
OUTSIDE = pl.BlockSpec(memory_space=pltpu.HBM)
SCALARS = pl.BlockSpec(memory_space=pltpu.SMEM)


def parts_of(table):
    high = table.astype(np.float32).astype(ml_dtypes.bfloat16)
    low = (table - high.astype(np.float64)).astype(np.float32).astype(ml_dtypes.bfloat16)
    return high, low


@functools.lru_cache(maxsize=None)
def tables(length):
    angle = np.outer(2 * np.arange(length) + 1, np.arange(length)) % (4 * length)
    angle = angle.astype(np.float64) * (math.pi / (2 * length))
    forward = np.concatenate([np.cos(angle), -np.sin(angle)], axis=0)
    high, low = parts_of(forward)
    back_high, back_low = parts_of(forward.T / length)
    return np.concatenate([high, low], axis=1), np.concatenate([back_high, back_low], axis=0)


def nn(a, b):
    return lax.dot_general(a, b, (((1,), (0,)), ((), ())), preferred_element_type=F32)


def nt(a, b):
    return lax.dot_general(a, b, (((1,), (1,)), ((), ())), preferred_element_type=F32)


def params(limit=VMEM):
    return pltpu.CompilerParams(vmem_limit_bytes=limit)


def lanes_at(tile):
    return pl.ds(pl.multiple_of(tile * LANES, LANES), LANES)


def write_facts(facts_ref, slot, docs_ref, block, length, end, inner, role):
    start = block * length
    stop = start + length - 1

    def visit(at, found):
        first, following, last = found
        here = docs_ref[at]
        first = jnp.minimum(first, jnp.where(here > start, here, end))
        following = jnp.minimum(following, jnp.where(here > stop, here, end))
        last = jnp.maximum(last, jnp.where(here <= stop, here, 0))
        return first, following, last

    whole = jnp.int32(end)
    first, following, last = lax.fori_loop(
        0, docs_ref.shape[0], visit, (whole, whole, jnp.int32(0))
    )
    facts_ref[slot, 0] = jnp.clip(first - start, 0, length)
    facts_ref[slot, 1] = jnp.clip(last - start, 0, length)
    for distance in range(1, REACH + 1):
        facts_ref[slot, 1 + distance] = jnp.clip(following - start - distance * length, 0, length)
    facts_ref[slot, 2 + REACH] = inner
    facts_ref[slot, 3 + REACH] = role


def prepare_kernel(pairs, *refs):
    place_ref, lane_ref, docs_ref, table_ref, back_ref, taps_ref = refs[:6]
    weight_ref, gate_ref, grad_ref = refs[6:9]
    spec_out, weight_out, gate_out, lower_out, table_out, back_out = refs[9:15]
    facts_out, token_out, sems = refs[15:]
    token_out[...] = jnp.zeros_like(token_out)
    copies = [
        pltpu.make_async_copy(source, target, sems.at[at])
        for at, (source, target) in enumerate(
            [
                (grad_ref.at[0, 0], lower_out),
                (weight_ref, weight_out),
                (gate_ref, gate_out),
                (back_ref, back_out),
            ]
        )
    ]
    step = pl.program_id(0)
    length = table_ref.shape[1] // 2

    @pl.when(step == 0)
    def _():
        for copy in copies:
            copy.start()
        table_out[...] = table_ref[:, :length]
        place = place_ref[0]
        odd = lax.rem(place, 2)
        role = jnp.where(place >= pairs - 3, pairs - place, 0)
        end = 2 * pairs * length
        for slot in range(2):
            facts_out[slot, 4 + REACH] = lane_ref[0]
        write_facts(facts_out, 0, docs_ref, place, length, end, 1 - odd, role)
        write_facts(facts_out, 1, docs_ref, 2 * pairs - 1 - place, length, end, odd, role)

    freq = lax.broadcasted_iota(jnp.int32, (length, 1), 0)
    sign = jnp.where(freq % 2 == 0, 1.0, -1.0).astype(F32)
    lanes = lanes_at(step)
    before = None
    for part in range(REACH + 1):
        if part < REACH:
            values = taps_ref[part * length : (part + 1) * length, :]
            high = values.astype(BF16)
            low = (values - high.astype(F32)).astype(BF16)
            full = nn(table_ref[...], jnp.concatenate([high, high], axis=0))
            full = full + nn(table_ref[:, :length], low)
            now = (full[:length], -full[length:])
        else:
            now = None
        if before is None:
            real, imag = now
        else:
            real, imag = sign * before[1], -sign * before[0]
            if now is not None:
                real, imag = now[0] + real, now[1] + imag
        spec_out[part, :length, lanes] = real
        spec_out[part, length:, lanes] = imag
        before = now

    @pl.when(step == pl.num_programs(0) - 1)
    def _():
        for copy in copies:
            copy.wait()


def prepare(pairs, place, lane, docs, table, back, taps, weight, gate, grad):
    count, width = taps.shape
    length = count // REACH
    return pl.pallas_call(
        functools.partial(prepare_kernel, pairs),
        grid=(width // LANES,),
        out_shape=(
            pltpu.VMEM((REACH + 1, 2 * length, width), F32),
            pltpu.VMEM(weight.shape, BF16),
            pltpu.VMEM(gate.shape, BF16),
            pltpu.VMEM(grad.shape[2:], BF16),
            pltpu.VMEM((2 * length, length), BF16),
            pltpu.VMEM(back.shape, BF16),
            pltpu.SMEM((2, 8), jnp.int32),
            pltpu.VMEM((8, 128), F32),
        ),
        in_specs=[
            SCALARS,
            SCALARS,
            SCALARS,
            pl.BlockSpec((2 * length, 2 * length), lambda c: (0, 0)),
            OUTSIDE,
            pl.BlockSpec((count, LANES), lambda c: (0, c)),
            OUTSIDE,
            OUTSIDE,
            OUTSIDE,
        ],
        out_specs=(WHOLE,) * 6 + (SCALARS, WHOLE),
        scratch_shapes=[pltpu.SemaphoreType.DMA((4,))],
        compiler_params=params(2 * VMEM),
        cost_estimate=pl.CostEstimate(
            flops=2 * 3 * 2 * count * length * width,
            bytes_accessed=4 * (count * width + 8 * length * width),
            transcendentals=0,
        ),
    )(place, lane, docs, table, back, taps, weight, gate, grad)


def project_kernel(hops, slot, first, last, facts_ref, *refs):
    shards, refs = refs[: len(hops)], refs[len(hops) :]
    weight_ref, gate_ref = refs[:2]
    before_ref = None if first else refs[2]
    out_ref, acc_ref = refs[-2:] if last else (refs[-1], refs[-1])
    depth = shards[0].shape[1]
    count = weight_ref.shape[1] // depth
    tiles = [pl.ds(tile * LANES, LANES) for tile in range(weight_ref.shape[0] // LANES)]
    if not first:
        acc_ref[...] = before_ref[...]
    for shard, hop in zip(shards, hops):
        at = facts_ref[0, 4 + REACH] + hop
        features = pl.ds(pl.multiple_of(jnp.clip(at, 0, count - 1) * depth, depth), depth)

        def add(shard=shard, hop=hop, features=features):
            for lanes in tiles:
                part = nt(shard[...], weight_ref[lanes, features])
                if hop == 0:
                    acc_ref[:, lanes] = part
                else:
                    acc_ref[:, lanes] += part

        if hop == 0:
            add()
        else:
            pl.when((at >= 0) & (at < count))(add)
    if last:
        out_ref[...] = (acc_ref[...] * gate_ref[0, slot].astype(F32)).astype(BF16)


def project(facts, shards, hops, weight, gate, slot, before=None, last=True, after=()):
    rows, depth = shards[0].shape
    width = weight.shape[0]
    operands = [facts, *shards, weight, gate]
    if before is not None:
        operands.append(before)
    return pl.pallas_call(
        functools.partial(project_kernel, hops, slot, before is None, last),
        out_shape=pltpu.VMEM((rows, width), BF16 if last else F32),
        in_specs=[SCALARS] + [WHOLE] * (len(operands) - 1) + [ANYWHERE] * len(after),
        out_specs=WHOLE,
        scratch_shapes=[pltpu.VMEM((rows, width), F32)] if last else [],
        compiler_params=params(),
        cost_estimate=pl.CostEstimate(
            flops=2 * rows * depth * (len(shards) + 1) // 2 * width,
            bytes_accessed=2 * (rows + width) * depth * len(shards),
            transcendentals=0,
        ),
    )(*operands, *after)


class Conv:
    def __init__(self, slot, facts, table, back, spectra):
        self.facts = [facts[slot, at] for at in range(4 + REACH)]
        self.table, self.back, self.spectra = table, back, spectra
        self.length = table.shape[0] // 2
        self.lanes = lanes_at(pl.program_id(0))
        self.row = lax.broadcasted_iota(jnp.int32, (self.length, LANES), 0)

    def joined(self, pieces):
        tiles = [piece[:, self.lanes] for piece in pieces]
        return tiles[0] if len(tiles) == 1 else jnp.concatenate(tiles, axis=0)

    def within(self, low, high):
        return (self.row >= low) & (self.row < high)

    def term(self, values, low, high, distance):
        length = self.length
        kept = jnp.where(self.within(low, high), values.astype(F32), 0.0).astype(BF16)
        full = nn(self.table[...], kept)
        real, imag = full[:length], full[length:]
        k_real = self.spectra[distance, :length, self.lanes]
        k_imag = self.spectra[distance, length:, self.lanes]
        return k_real * real - k_imag * imag, k_real * imag + k_imag * real

    def signal(self, real, imag):
        total = jnp.concatenate([real.astype(BF16), imag.astype(BF16)], axis=0)
        both = nn(self.back[...], total)
        return both[: self.length] + both[self.length :]

    def far_terms(self, acc, chosen, choices):
        for distance in range(1, REACH + 1):
            reach = self.facts[1 + distance]

            @pl.when(reach > 0)
            def _(distance=distance, reach=reach):
                for pieces, holds in choices(distance):

                    @pl.when(holds)
                    def _(pieces=pieces):
                        chosen[...] = self.joined(pieces)

                real, imag = self.term(chosen[...], 0, reach, distance)
                acc[: self.length, :] += real
                acc[self.length :, :] += imag

    def inner_documents(self, own, read, write):
        first_end, last_start = self.facts[0], self.facts[1]

        @pl.when(last_start > 0)
        def _():
            signal = self.signal(*self.term(own, 0, first_end, 0))
            write(jnp.where(self.row < first_end, signal, read()))

        @pl.when(last_start > first_end)
        def _():
            signal = self.signal(*self.term(own, first_end, last_start, 0))
            write(jnp.where(self.within(first_end, last_start), signal, read()))

    def halo(self, pieces, distance, mixed):
        sets = 3 if mixed else 4
        count = len(pieces) // sets
        kinds = [pieces[at * count : (at + 1) * count] for at in range(sets)]
        two, swapped, mate, far = kinds[0], kinds[1], kinds[2], kinds[-1]
        inner = self.facts[5]
        if distance == 2:
            return [(two, inner >= 0)]
        if distance == 1:
            return [(mate, inner == 1), (swapped, inner == 0)]
        return [(swapped, inner == 1), (far, inner == 0)]


def own_kernel(slot, pieces, facts_ref, table_ref, back_ref, spec_ref, *refs):
    own_refs, out_ref = refs[:pieces], refs[-1]
    conv = Conv(slot, facts_ref, table_ref, back_ref, spec_ref)
    own = conv.joined(own_refs)
    out_ref[:, conv.lanes] = conv.signal(*conv.term(own, conv.facts[1], conv.length, 0))

    def write(value):
        out_ref[:, conv.lanes] = value

    conv.inner_documents(own, lambda: out_ref[:, conv.lanes], write)


def far_kernel(slot, pieces, facts_ref, table_ref, back_ref, spec_ref, *refs):
    near_ref, refs = refs[0], refs[1:]
    if slot == 0:
        upper_ref, mate_ref, two_ref, fold_ref = refs[:4]
        halos = refs[4 : 4 + 3 * pieces]
    else:
        halos = refs[: 4 * pieces]
    out_ref, acc_ref, chosen_ref = refs[-3:]
    if slot == 1:
        out_ref, token_ref = refs[-4:-2]
        token_ref[...] = jnp.zeros_like(token_ref)
    conv = Conv(slot, facts_ref, table_ref, back_ref, spec_ref)
    role = conv.facts[6]

    def choices(distance):
        found = conv.halo(halos, distance, slot == 0)
        if slot == 0:
            folded = {
                1: [([upper_ref], role == 1)],
                2: [([mate_ref], (role == 1) | (role == 2))],
                3: [([two_ref], role == 1), ([upper_ref], role == 2), ([fold_ref], role == 3)],
            }
            found = found + folded[distance]
        return found

    reaches = conv.facts[2] > 0

    @pl.when(reaches)
    def _():
        acc_ref[...] = jnp.zeros_like(acc_ref)
        conv.far_terms(acc_ref, chosen_ref, choices)
        signal = conv.signal(acc_ref[: conv.length, :], acc_ref[conv.length :, :])
        kept = jnp.where(conv.row >= conv.facts[1], signal, 0.0)
        out_ref[0, 0] = near_ref[:, conv.lanes] + kept

    @pl.when(jnp.logical_not(reaches))
    def _():
        out_ref[0, 0] = near_ref[:, conv.lanes]


def conv_call(body, tabs, facts, arrays, out_shape, out_spec, scratch, after=(), result=None):
    table, back, spectra = tabs
    length = table.shape[0] // 2
    width = spectra.shape[2]
    operands = [facts, table, back, spectra, *arrays]
    specs = [SCALARS] + [WHOLE] * (len(operands) - 1) + [ANYWHERE] * len(after)
    operands.extend(after)
    aliases = {}
    if result is not None:
        aliases = {len(operands): 0}
        operands.append(result)
        specs.append(ANYWHERE)
    return pl.pallas_call(
        body,
        grid=(width // LANES,),
        out_shape=out_shape,
        in_specs=specs,
        out_specs=out_spec,
        scratch_shapes=scratch,
        input_output_aliases=aliases,
        compiler_params=params(),
        cost_estimate=pl.CostEstimate(
            flops=32 * length * length * width,
            bytes_accessed=4 * length * width,
            transcendentals=0,
        ),
    )(*operands)


def own_terms(slot, tabs, facts, pieces, after=()):
    _, back, spectra = tabs
    shape = pltpu.VMEM((back.shape[0] // 2, spectra.shape[2]), F32)
    body = functools.partial(own_kernel, slot, len(pieces))
    return conv_call(body, tabs, facts, pieces, shape, WHOLE, [], after)


def far_terms(slot, count, tabs, facts, arrays, result=None):
    _, back, spectra = tabs
    length, width = back.shape[0] // 2, spectra.shape[2]
    shape = jax.ShapeDtypeStruct((1, 2, length, width), F32)
    spec = pl.BlockSpec((1, 1, length, LANES), lambda c: (0, slot, 0, c))
    scratch = [pltpu.VMEM((2 * length, LANES), F32), pltpu.VMEM((length, LANES), BF16)]
    body = functools.partial(far_kernel, slot, count)
    if slot == 1:
        shape, spec = (shape, pltpu.VMEM((8, 128), F32)), (spec, WHOLE)
    return conv_call(body, tabs, facts, arrays, shape, spec, scratch, (), result)


def ordered(value, *earlier):
    return pl.pallas_call(
        lambda *refs: None,
        out_shape=jax.ShapeDtypeStruct(value.shape, value.dtype),
        in_specs=[ANYWHERE] * (1 + len(earlier)),
        out_specs=ANYWHERE,
        input_output_aliases={0: 0},
        compiler_params=params(VMEM // 20),
    )(value, *earlier)


def shifted(value, steps):
    count = lax.axis_size("ctx")
    initial, last = (max(0, -steps), min(count, count - steps))
    return lax.ppermute(value, "ctx", [(source, source + steps) for source in range(initial, last)])


def core_swapped(value):
    count = lax.axis_size("ctx")
    return lax.ppermute(value, "ctx", [(source, source ^ 1) for source in range(count)])


def upper_halo_of(value):
    count = lax.axis_size("ctx")
    far = [(source, source + 3) for source in range(1, count - 3, 2)] + [(count - 1, count - 3)]
    two = shifted(value, 2)
    mate, far = core_swapped(value), lax.ppermute(value, "ctx", far)
    return [two, core_swapped(two), mate, far]


def lower_halo_of(value, own):
    count = lax.axis_size("ctx")
    mixed = [(source, source - 1) for source in range(1, count, 2)]
    mixed += [(source, source - 3) for source in range(4, count, 2)]
    two = ordered(shifted(value, -2), own)
    mixed = lax.ppermute(value, "ctx", mixed)
    return [two, core_swapped(two), mixed]


def on_device(grad_out, out_weight, gate, filter_taps, doc_starts):
    pairs = lax.axis_size("ctx")
    place = lax.axis_index("ctx")
    length = grad_out.shape[2]
    width = out_weight.shape[0]
    count = lax.axis_size("ch")
    lane = lax.axis_index("ch").astype(jnp.int32)[None]

    def sent(step, up, down):
        upward = [(source, source + 1) for source in range(step - 1, count - 1)]
        downward = [(source, source - 1) for source in range(1, count - step + 1)]
        return lax.ppermute(up, "ch", upward), lax.ppermute(down, "ch", downward)

    start = grad_out[0, 1]
    upper_in = [sent(1, start, start)]

    table, back = (jnp.asarray(one) for one in tables(length))
    spectra, weight, gates, lower_slice, table, back, facts, prepared = prepare(
        pairs,
        place.astype(jnp.int32)[None],
        lane,
        doc_starts,
        table,
        back,
        filter_taps,
        out_weight,
        gate,
        grad_out,
    )
    tabs = (table, back, spectra)

    def pass_on(chain, *earlier):
        if earlier:
            chain[-1] = [ordered(one, *earlier) for one in chain[-1]]
        chain.append(sent(len(chain) + 1, *chain[-1]))

    hops = [0] + [way * step for step in range(1, count) for way in (-1, 1)]

    def partial_of(own, arrived, slot):
        shards = [own] + [one for pair in arrived[: count - 2] for one in pair]
        return project(facts, shards, hops[:-2], weight, gates, slot, last=False)

    def final_of(arrived, slot, partial, after=()):
        return project(facts, arrived[-1], hops[-2:], weight, gates, slot, partial, after=after)

    pass_on(upper_in, prepared)
    for _ in range(3, count):
        pass_on(upper_in)
    partial = partial_of(start, upper_in, 1)
    own = ordered(lower_slice, *upper_in[-1], partial)
    lower_in = [sent(1, own, own)]
    upper = final_of(upper_in, 1, partial)
    upper_halo = upper_halo_of(upper)
    two, swapped, mate, fold = upper_halo
    pass_on(lower_in, upper)
    near = own_terms(1, tabs, facts, [upper])
    for _ in range(3, count):
        pass_on(lower_in, near, two, mate, fold)
    result, convolved = far_terms(1, 1, tabs, facts, [near, *upper_halo])

    partial = partial_of(own, lower_in, 0)
    lower = final_of(lower_in, 0, partial, [swapped, convolved])
    near = own_terms(0, tabs, facts, [lower])
    lower_halo = lower_halo_of(lower, near)
    arrays = [near, upper, mate, two, fold, *lower_halo]
    return far_terms(0, 1, tabs, facts, arrays, result)


def solution(mesh):
    in_specs = (
        P("ctx", None, None, "ch"),
        P("ch", None),
        P("ctx", None, None, "ch"),
        P(None, "ch"),
        P(),
    )
    out_specs = P("ctx", None, None, "ch")
    return jax.shard_map(
        on_device, mesh=mesh, in_specs=in_specs, out_specs=out_specs, check_vma=False
    )
```

```python
import functools
import math

import jax
import jax.numpy as jnp
import ml_dtypes
import numpy as np
from jax import lax
from jax.experimental import pallas as pl
from jax.experimental.pallas import tpu as pltpu
from jax.sharding import PartitionSpec as P

REACH = 3
LANES = 512
VMEM = 20 * 1024 * 1024
F32 = jnp.float32
BF16 = jnp.bfloat16
WHOLE = pl.BlockSpec(memory_space=pltpu.VMEM)
ANYWHERE = pl.BlockSpec(memory_space=pl.ANY)
OUTSIDE = pl.BlockSpec(memory_space=pltpu.HBM)
SCALARS = pl.BlockSpec(memory_space=pltpu.SMEM)


def parts_of(table):
    high = table.astype(np.float32).astype(ml_dtypes.bfloat16)
    low = (table - high.astype(np.float64)).astype(np.float32).astype(ml_dtypes.bfloat16)
    return high, low


@functools.lru_cache(maxsize=None)
def tables(length):
    angle = np.outer(2 * np.arange(length) + 1, np.arange(length)) % (4 * length)
    angle = angle.astype(np.float64) * (math.pi / (2 * length))
    forward = np.concatenate([np.cos(angle), -np.sin(angle)], axis=0)
    high, low = parts_of(forward)
    back_high, back_low = parts_of(forward.T / length)
    return np.concatenate([high, low], axis=1), np.concatenate([back_high, back_low], axis=0)


def nn(a, b):
    return lax.dot_general(a, b, (((1,), (0,)), ((), ())), preferred_element_type=F32)


def nt(a, b):
    return lax.dot_general(a, b, (((1,), (1,)), ((), ())), preferred_element_type=F32)


def params(limit=VMEM):
    return pltpu.CompilerParams(vmem_limit_bytes=limit)


def lanes_at(tile):
    return pl.ds(pl.multiple_of(tile * LANES, LANES), LANES)


def write_facts(facts_ref, slot, docs_ref, block, length, end, inner, role):
    start = block * length
    stop = start + length - 1

    def visit(at, found):
        first, following, last = found
        here = docs_ref[at]
        first = jnp.minimum(first, jnp.where(here > start, here, end))
        following = jnp.minimum(following, jnp.where(here > stop, here, end))
        last = jnp.maximum(last, jnp.where(here <= stop, here, 0))
        return first, following, last

    whole = jnp.int32(end)
    first, following, last = lax.fori_loop(
        0, docs_ref.shape[0], visit, (whole, whole, jnp.int32(0))
    )
    facts_ref[slot, 0] = jnp.clip(first - start, 0, length)
    facts_ref[slot, 1] = jnp.clip(last - start, 0, length)
    for distance in range(1, REACH + 1):
        facts_ref[slot, 1 + distance] = jnp.clip(following - start - distance * length, 0, length)
    facts_ref[slot, 2 + REACH] = inner
    facts_ref[slot, 3 + REACH] = role


def prepare_kernel(pairs, *refs):
    place_ref, lane_ref, docs_ref, table_ref, back_ref, taps_ref = refs[:6]
    weight_ref, gate_ref, grad_ref = refs[6:9]
    spec_out, weight_out, gate_out, lower_out, table_out, back_out = refs[9:15]
    facts_out, token_out, sems = refs[15:]
    token_out[...] = jnp.zeros_like(token_out)
    copies = [
        pltpu.make_async_copy(source, target, sems.at[at])
        for at, (source, target) in enumerate(
            [
                (grad_ref.at[0, 0], lower_out),
                (weight_ref, weight_out),
                (gate_ref, gate_out),
                (back_ref, back_out),
            ]
        )
    ]
    step = pl.program_id(0)
    length = table_ref.shape[1] // 2

    @pl.when(step == 0)
    def _():
        for copy in copies:
            copy.start()
        table_out[...] = table_ref[:, :length]
        place = place_ref[0]
        odd = lax.rem(place, 2)
        role = jnp.where(place >= pairs - 3, pairs - place, 0)
        end = 2 * pairs * length
        for slot in range(2):
            facts_out[slot, 4 + REACH] = lane_ref[0]
        write_facts(facts_out, 0, docs_ref, place, length, end, 1 - odd, role)
        write_facts(facts_out, 1, docs_ref, 2 * pairs - 1 - place, length, end, odd, role)

    freq = lax.broadcasted_iota(jnp.int32, (length, 1), 0)
    sign = jnp.where(freq % 2 == 0, 1.0, -1.0).astype(F32)
    lanes = lanes_at(step)
    before = None
    for part in range(REACH + 1):
        if part < REACH:
            values = taps_ref[part * length : (part + 1) * length, :]
            high = values.astype(BF16)
            low = (values - high.astype(F32)).astype(BF16)
            full = nn(table_ref[...], jnp.concatenate([high, high], axis=0))
            full = full + nn(table_ref[:, :length], low)
            now = (full[:length], -full[length:])
        else:
            now = None
        if before is None:
            real, imag = now
        else:
            real, imag = sign * before[1], -sign * before[0]
            if now is not None:
                real, imag = now[0] + real, now[1] + imag
        spec_out[part, :length, lanes] = real
        spec_out[part, length:, lanes] = imag
        before = now

    @pl.when(step == pl.num_programs(0) - 1)
    def _():
        for copy in copies:
            copy.wait()


def prepare(pairs, place, lane, docs, table, back, taps, weight, gate, grad):
    count, width = taps.shape
    length = count // REACH
    return pl.pallas_call(
        functools.partial(prepare_kernel, pairs),
        grid=(width // LANES,),
        out_shape=(
            pltpu.VMEM((REACH + 1, 2 * length, width), F32),
            pltpu.VMEM(weight.shape, BF16),
            pltpu.VMEM(gate.shape, BF16),
            pltpu.VMEM(grad.shape[2:], BF16),
            pltpu.VMEM((2 * length, length), BF16),
            pltpu.VMEM(back.shape, BF16),
            pltpu.SMEM((2, 8), jnp.int32),
            pltpu.VMEM((8, 128), F32),
        ),
        in_specs=[
            SCALARS,
            SCALARS,
            SCALARS,
            pl.BlockSpec((2 * length, 2 * length), lambda c: (0, 0)),
            OUTSIDE,
            pl.BlockSpec((count, LANES), lambda c: (0, c)),
            OUTSIDE,
            OUTSIDE,
            OUTSIDE,
        ],
        out_specs=(WHOLE,) * 6 + (SCALARS, WHOLE),
        scratch_shapes=[pltpu.SemaphoreType.DMA((4,))],
        compiler_params=params(2 * VMEM),
        cost_estimate=pl.CostEstimate(
            flops=2 * 3 * 2 * count * length * width,
            bytes_accessed=4 * (count * width + 8 * length * width),
            transcendentals=0,
        ),
    )(place, lane, docs, table, back, taps, weight, gate, grad)


def project_kernel(hops, slot, first, last, facts_ref, *refs):
    shards, refs = refs[: len(hops)], refs[len(hops) :]
    weight_ref, gate_ref = refs[:2]
    before_ref = None if first else refs[2]
    out_ref, acc_ref = refs[-2:] if last else (refs[-1], refs[-1])
    depth = shards[0].shape[1]
    count = weight_ref.shape[1] // depth
    tiles = [pl.ds(tile * LANES, LANES) for tile in range(weight_ref.shape[0] // LANES)]
    if not first:
        acc_ref[...] = before_ref[...]
    for shard, hop in zip(shards, hops):
        at = facts_ref[0, 4 + REACH] + hop
        features = pl.ds(pl.multiple_of(jnp.clip(at, 0, count - 1) * depth, depth), depth)

        def add(shard=shard, hop=hop, features=features):
            for lanes in tiles:
                part = nt(shard[...], weight_ref[lanes, features])
                if hop == 0:
                    acc_ref[:, lanes] = part
                else:
                    acc_ref[:, lanes] += part

        if hop == 0:
            add()
        else:
            pl.when((at >= 0) & (at < count))(add)
    if last:
        out_ref[...] = (acc_ref[...] * gate_ref[0, slot].astype(F32)).astype(BF16)


def project(facts, shards, hops, weight, gate, slot, before=None, last=True, after=()):
    rows, depth = shards[0].shape
    width = weight.shape[0]
    operands = [facts, *shards, weight, gate]
    if before is not None:
        operands.append(before)
    return pl.pallas_call(
        functools.partial(project_kernel, hops, slot, before is None, last),
        out_shape=pltpu.VMEM((rows, width), BF16 if last else F32),
        in_specs=[SCALARS] + [WHOLE] * (len(operands) - 1) + [ANYWHERE] * len(after),
        out_specs=WHOLE,
        scratch_shapes=[pltpu.VMEM((rows, width), F32)] if last else [],
        compiler_params=params(),
        cost_estimate=pl.CostEstimate(
            flops=2 * rows * depth * (len(shards) + 1) // 2 * width,
            bytes_accessed=2 * (rows + width) * depth * len(shards),
            transcendentals=0,
        ),
    )(*operands, *after)


class Conv:
    def __init__(self, slot, facts, table, back, spectra):
        self.facts = [facts[slot, at] for at in range(4 + REACH)]
        self.table, self.back, self.spectra = table, back, spectra
        self.length = table.shape[0] // 2
        self.lanes = lanes_at(pl.program_id(0))
        self.row = lax.broadcasted_iota(jnp.int32, (self.length, LANES), 0)

    def joined(self, pieces):
        tiles = [piece[:, self.lanes] for piece in pieces]
        return tiles[0] if len(tiles) == 1 else jnp.concatenate(tiles, axis=0)

    def within(self, low, high):
        return (self.row >= low) & (self.row < high)

    def term(self, values, low, high, distance):
        length = self.length
        kept = jnp.where(self.within(low, high), values.astype(F32), 0.0).astype(BF16)
        full = nn(self.table[...], kept)
        real, imag = full[:length], full[length:]
        k_real = self.spectra[distance, :length, self.lanes]
        k_imag = self.spectra[distance, length:, self.lanes]
        return k_real * real - k_imag * imag, k_real * imag + k_imag * real

    def signal(self, real, imag):
        total = jnp.concatenate([real.astype(BF16), imag.astype(BF16)], axis=0)
        both = nn(self.back[...], total)
        return both[: self.length] + both[self.length :]

    def far_terms(self, acc, chosen, choices):
        for distance in range(1, REACH + 1):
            reach = self.facts[1 + distance]

            @pl.when(reach > 0)
            def _(distance=distance, reach=reach):
                for pieces, holds in choices(distance):

                    @pl.when(holds)
                    def _(pieces=pieces):
                        chosen[...] = self.joined(pieces)

                real, imag = self.term(chosen[...], 0, reach, distance)
                acc[: self.length, :] += real
                acc[self.length :, :] += imag

    def inner_documents(self, own, read, write):
        first_end, last_start = self.facts[0], self.facts[1]

        @pl.when(last_start > 0)
        def _():
            signal = self.signal(*self.term(own, 0, first_end, 0))
            write(jnp.where(self.row < first_end, signal, read()))

        @pl.when(last_start > first_end)
        def _():
            signal = self.signal(*self.term(own, first_end, last_start, 0))
            write(jnp.where(self.within(first_end, last_start), signal, read()))

    def halo(self, pieces, distance, mixed):
        sets = 3 if mixed else 4
        count = len(pieces) // sets
        kinds = [pieces[at * count : (at + 1) * count] for at in range(sets)]
        two, swapped, mate, far = kinds[0], kinds[1], kinds[2], kinds[-1]
        inner = self.facts[5]
        if distance == 2:
            return [(two, inner >= 0)]
        if distance == 1:
            return [(mate, inner == 1), (swapped, inner == 0)]
        return [(swapped, inner == 1), (far, inner == 0)]


def own_kernel(slot, pieces, facts_ref, table_ref, back_ref, spec_ref, *refs):
    own_refs, out_ref = refs[:pieces], refs[-1]
    conv = Conv(slot, facts_ref, table_ref, back_ref, spec_ref)
    own = conv.joined(own_refs)
    out_ref[:, conv.lanes] = conv.signal(*conv.term(own, conv.facts[1], conv.length, 0))

    def write(value):
        out_ref[:, conv.lanes] = value

    conv.inner_documents(own, lambda: out_ref[:, conv.lanes], write)


def far_kernel(slot, pieces, facts_ref, table_ref, back_ref, spec_ref, *refs):
    near_ref, refs = refs[0], refs[1:]
    if slot == 0:
        upper_ref, mate_ref, two_ref, fold_ref = refs[:4]
        halos = refs[4 : 4 + 3 * pieces]
    else:
        halos = refs[: 4 * pieces]
    out_ref, acc_ref, chosen_ref = refs[-3:]
    if slot == 1:
        out_ref, token_ref = refs[-4:-2]
        token_ref[...] = jnp.zeros_like(token_ref)
    conv = Conv(slot, facts_ref, table_ref, back_ref, spec_ref)
    role = conv.facts[6]

    def choices(distance):
        found = conv.halo(halos, distance, slot == 0)
        if slot == 0:
            folded = {
                1: [([upper_ref], role == 1)],
                2: [([mate_ref], (role == 1) | (role == 2))],
                3: [([two_ref], role == 1), ([upper_ref], role == 2), ([fold_ref], role == 3)],
            }
            found = found + folded[distance]
        return found

    reaches = conv.facts[2] > 0

    @pl.when(reaches)
    def _():
        acc_ref[...] = jnp.zeros_like(acc_ref)
        conv.far_terms(acc_ref, chosen_ref, choices)
        signal = conv.signal(acc_ref[: conv.length, :], acc_ref[conv.length :, :])
        kept = jnp.where(conv.row >= conv.facts[1], signal, 0.0)
        out_ref[0, 0] = near_ref[:, conv.lanes] + kept

    @pl.when(jnp.logical_not(reaches))
    def _():
        out_ref[0, 0] = near_ref[:, conv.lanes]


def conv_call(body, tabs, facts, arrays, out_shape, out_spec, scratch, after=(), result=None):
    table, back, spectra = tabs
    length = table.shape[0] // 2
    width = spectra.shape[2]
    operands = [facts, table, back, spectra, *arrays]
    specs = [SCALARS] + [WHOLE] * (len(operands) - 1) + [ANYWHERE] * len(after)
    operands.extend(after)
    aliases = {}
    if result is not None:
        aliases = {len(operands): 0}
        operands.append(result)
        specs.append(ANYWHERE)
    return pl.pallas_call(
        body,
        grid=(width // LANES,),
        out_shape=out_shape,
        in_specs=specs,
        out_specs=out_spec,
        scratch_shapes=scratch,
        input_output_aliases=aliases,
        compiler_params=params(),
        cost_estimate=pl.CostEstimate(
            flops=32 * length * length * width,
            bytes_accessed=4 * length * width,
            transcendentals=0,
        ),
    )(*operands)


def own_terms(slot, tabs, facts, pieces, after=()):
    _, back, spectra = tabs
    shape = pltpu.VMEM((back.shape[0] // 2, spectra.shape[2]), F32)
    body = functools.partial(own_kernel, slot, len(pieces))
    return conv_call(body, tabs, facts, pieces, shape, WHOLE, [], after)


def far_terms(slot, count, tabs, facts, arrays, result=None):
    _, back, spectra = tabs
    length, width = back.shape[0] // 2, spectra.shape[2]
    shape = jax.ShapeDtypeStruct((1, 2, length, width), F32)
    spec = pl.BlockSpec((1, 1, length, LANES), lambda c: (0, slot, 0, c))
    scratch = [pltpu.VMEM((2 * length, LANES), F32), pltpu.VMEM((length, LANES), BF16)]
    body = functools.partial(far_kernel, slot, count)
    if slot == 1:
        shape, spec = (shape, pltpu.VMEM((8, 128), F32)), (spec, WHOLE)
    return conv_call(body, tabs, facts, arrays, shape, spec, scratch, (), result)


def ordered(value, *earlier):
    return pl.pallas_call(
        lambda *refs: None,
        out_shape=jax.ShapeDtypeStruct(value.shape, value.dtype),
        in_specs=[ANYWHERE] * (1 + len(earlier)),
        out_specs=ANYWHERE,
        input_output_aliases={0: 0},
        compiler_params=params(VMEM // 20),
    )(value, *earlier)


def shifted(value, steps):
    count = lax.axis_size("ctx")
    initial, last = (max(0, -steps), min(count, count - steps))
    return lax.ppermute(value, "ctx", [(source, source + steps) for source in range(initial, last)])


def core_swapped(value):
    count = lax.axis_size("ctx")
    return lax.ppermute(value, "ctx", [(source, source ^ 1) for source in range(count)])


def upper_halo_of(value):
    count = lax.axis_size("ctx")
    far = [(source, source + 3) for source in range(1, count - 3, 2)] + [(count - 1, count - 3)]
    two = shifted(value, 2)
    mate, far = core_swapped(value), lax.ppermute(value, "ctx", far)
    return [two, core_swapped(two), mate, far]


def lower_halo_of(value, own):
    count = lax.axis_size("ctx")
    mixed = [(source, source - 1) for source in range(1, count, 2)]
    mixed += [(source, source - 3) for source in range(4, count, 2)]
    two = ordered(shifted(value, -2), own)
    mixed = lax.ppermute(value, "ctx", mixed)
    return [two, core_swapped(two), mixed]


def on_device(grad_out, out_weight, gate, filter_taps, doc_starts):
    pairs = lax.axis_size("ctx")
    place = lax.axis_index("ctx")
    length = grad_out.shape[2]
    width = out_weight.shape[0]
    count = lax.axis_size("ch")
    lane = lax.axis_index("ch").astype(jnp.int32)[None]

    def sent(step, up, down):
        upward = [(source, source + 1) for source in range(step - 1, count - 1)]
        downward = [(source, source - 1) for source in range(1, count - step + 1)]
        return lax.ppermute(up, "ch", upward), lax.ppermute(down, "ch", downward)

    start = grad_out[0, 1]
    upper_in = [sent(1, start, start)]

    table, back = (jnp.asarray(one) for one in tables(length))
    spectra, weight, gates, lower_slice, table, back, facts, prepared = prepare(
        pairs,
        place.astype(jnp.int32)[None],
        lane,
        doc_starts,
        table,
        back,
        filter_taps,
        out_weight,
        gate,
        grad_out,
    )
    tabs = (table, back, spectra)

    def pass_on(chain, *earlier):
        if earlier:
            chain[-1] = [ordered(one, *earlier) for one in chain[-1]]
        chain.append(sent(len(chain) + 1, *chain[-1]))

    hops = [0] + [way * step for step in range(1, count) for way in (-1, 1)]

    def partial_of(own, arrived, slot, after=()):
        shards = [own] + [one for pair in arrived[: count - 2] for one in pair]
        return project(
            facts, shards, hops[:-2], weight, gates, slot, last=False, after=after
        )

    def final_of(arrived, slot, partial, after=()):
        return project(facts, arrived[-1], hops[-2:], weight, gates, slot, partial, after=after)

    pass_on(upper_in, prepared)
    own = ordered(lower_slice, *upper_in[0])
    lower_in = [sent(1, own, own)]
    for _ in range(3, count):
        pass_on(upper_in)
        pass_on(lower_in, *upper_in[-2])
    partial = partial_of(start, upper_in, 1)
    pass_on(lower_in, partial)

    upper = final_of(upper_in, 1, partial)
    upper_halo = upper_halo_of(upper)
    two, swapped, mate, fold = upper_halo
    near = own_terms(1, tabs, facts, [upper])
    result, _ = far_terms(1, 1, tabs, facts, [near, *upper_halo])

    partial = partial_of(own, lower_in, 0, [near, mate])
    lower = final_of(lower_in, 0, partial, [two, fold])
    near = own_terms(0, tabs, facts, [lower])
    lower_halo = lower_halo_of(lower, near)
    arrays = [near, upper, mate, two, fold, *lower_halo]
    return far_terms(0, 1, tabs, facts, arrays, result)


def solution(mesh):
    in_specs = (
        P("ctx", None, None, "ch"),
        P("ch", None),
        P("ctx", None, None, "ch"),
        P(None, "ch"),
        P(),
    )
    out_specs = P("ctx", None, None, "ch")
    return jax.shard_map(
        on_device, mesh=mesh, in_specs=in_specs, out_specs=out_specs, check_vma=False
    )
```

```python
import functools
import math

import jax
import jax.numpy as jnp
import ml_dtypes
import numpy as np
from jax import lax
from jax.experimental import pallas as pl
from jax.experimental.pallas import tpu as pltpu
from jax.sharding import PartitionSpec as P

REACH = 3
LANES = 512
VMEM = 20 * 1024 * 1024
F32 = jnp.float32
BF16 = jnp.bfloat16
WHOLE = pl.BlockSpec(memory_space=pltpu.VMEM)
ANYWHERE = pl.BlockSpec(memory_space=pl.ANY)
OUTSIDE = pl.BlockSpec(memory_space=pltpu.HBM)
SCALARS = pl.BlockSpec(memory_space=pltpu.SMEM)


def parts_of(table):
    high = table.astype(np.float32).astype(ml_dtypes.bfloat16)
    low = (table - high.astype(np.float64)).astype(np.float32).astype(ml_dtypes.bfloat16)
    return high, low


@functools.lru_cache(maxsize=None)
def tables(length):
    angle = np.outer(2 * np.arange(length) + 1, np.arange(length)) % (4 * length)
    angle = angle.astype(np.float64) * (math.pi / (2 * length))
    forward = np.concatenate([np.cos(angle), -np.sin(angle)], axis=0)
    high, low = parts_of(forward)
    back_high, back_low = parts_of(forward.T / length)
    return np.concatenate([high, low], axis=1), np.concatenate([back_high, back_low], axis=0)


def nn(a, b):
    return lax.dot_general(a, b, (((1,), (0,)), ((), ())), preferred_element_type=F32)


def nt(a, b):
    return lax.dot_general(a, b, (((1,), (1,)), ((), ())), preferred_element_type=F32)


def params(limit=VMEM):
    return pltpu.CompilerParams(vmem_limit_bytes=limit)


def lanes_at(tile):
    return pl.ds(pl.multiple_of(tile * LANES, LANES), LANES)


def write_facts(facts_ref, slot, docs_ref, block, length, end, inner, role):
    start = block * length
    stop = start + length - 1

    def visit(at, found):
        first, following, last = found
        here = docs_ref[at]
        first = jnp.minimum(first, jnp.where(here > start, here, end))
        following = jnp.minimum(following, jnp.where(here > stop, here, end))
        last = jnp.maximum(last, jnp.where(here <= stop, here, 0))
        return first, following, last

    whole = jnp.int32(end)
    first, following, last = lax.fori_loop(
        0, docs_ref.shape[0], visit, (whole, whole, jnp.int32(0))
    )
    facts_ref[slot, 0] = jnp.clip(first - start, 0, length)
    facts_ref[slot, 1] = jnp.clip(last - start, 0, length)
    for distance in range(1, REACH + 1):
        facts_ref[slot, 1 + distance] = jnp.clip(following - start - distance * length, 0, length)
    facts_ref[slot, 2 + REACH] = inner
    facts_ref[slot, 3 + REACH] = role


def prepare_kernel(pairs, *refs):
    place_ref, lane_ref, docs_ref, table_ref, back_ref, taps_ref = refs[:6]
    weight_ref, gate_ref, grad_ref = refs[6:9]
    spec_out, weight_out, gate_out, lower_out, table_out, back_out = refs[9:15]
    facts_out, token_out, sems = refs[15:]
    token_out[...] = jnp.zeros_like(token_out)
    copies = [
        pltpu.make_async_copy(source, target, sems.at[at])
        for at, (source, target) in enumerate(
            [
                (grad_ref.at[0, 0], lower_out),
                (weight_ref, weight_out),
                (gate_ref, gate_out),
                (back_ref, back_out),
            ]
        )
    ]
    step = pl.program_id(0)
    length = table_ref.shape[1] // 2

    @pl.when(step == 0)
    def _():
        for copy in copies:
            copy.start()
        table_out[...] = table_ref[:, :length]
        place = place_ref[0]
        odd = lax.rem(place, 2)
        role = jnp.where(place >= pairs - 3, pairs - place, 0)
        end = 2 * pairs * length
        for slot in range(2):
            facts_out[slot, 4 + REACH] = lane_ref[0]
        write_facts(facts_out, 0, docs_ref, place, length, end, 1 - odd, role)
        write_facts(facts_out, 1, docs_ref, 2 * pairs - 1 - place, length, end, odd, role)

    freq = lax.broadcasted_iota(jnp.int32, (length, 1), 0)
    sign = jnp.where(freq % 2 == 0, 1.0, -1.0).astype(F32)
    lanes = lanes_at(step)
    before = None
    for part in range(REACH + 1):
        if part < REACH:
            values = taps_ref[part * length : (part + 1) * length, :]
            high = values.astype(BF16)
            low = (values - high.astype(F32)).astype(BF16)
            full = nn(table_ref[...], jnp.concatenate([high, high], axis=0))
            full = full + nn(table_ref[:, :length], low)
            now = (full[:length], -full[length:])
        else:
            now = None
        if before is None:
            real, imag = now
        else:
            real, imag = sign * before[1], -sign * before[0]
            if now is not None:
                real, imag = now[0] + real, now[1] + imag
        spec_out[part, :length, lanes] = real
        spec_out[part, length:, lanes] = imag
        before = now

    @pl.when(step == pl.num_programs(0) - 1)
    def _():
        for copy in copies:
            copy.wait()


def prepare(pairs, place, lane, docs, table, back, taps, weight, gate, grad):
    count, width = taps.shape
    length = count // REACH
    return pl.pallas_call(
        functools.partial(prepare_kernel, pairs),
        grid=(width // LANES,),
        out_shape=(
            pltpu.VMEM((REACH + 1, 2 * length, width), F32),
            pltpu.VMEM(weight.shape, BF16),
            pltpu.VMEM(gate.shape, BF16),
            pltpu.VMEM(grad.shape[2:], BF16),
            pltpu.VMEM((2 * length, length), BF16),
            pltpu.VMEM(back.shape, BF16),
            pltpu.SMEM((2, 8), jnp.int32),
            pltpu.VMEM((8, 128), F32),
        ),
        in_specs=[
            SCALARS,
            SCALARS,
            SCALARS,
            pl.BlockSpec((2 * length, 2 * length), lambda c: (0, 0)),
            OUTSIDE,
            pl.BlockSpec((count, LANES), lambda c: (0, c)),
            OUTSIDE,
            OUTSIDE,
            OUTSIDE,
        ],
        out_specs=(WHOLE,) * 6 + (SCALARS, WHOLE),
        scratch_shapes=[pltpu.SemaphoreType.DMA((4,))],
        compiler_params=params(2 * VMEM),
        cost_estimate=pl.CostEstimate(
            flops=2 * 3 * 2 * count * length * width,
            bytes_accessed=4 * (count * width + 8 * length * width),
            transcendentals=0,
        ),
    )(place, lane, docs, table, back, taps, weight, gate, grad)


def project_kernel(hops, slot, first, last, facts_ref, *refs):
    shards, refs = refs[: len(hops)], refs[len(hops) :]
    weight_ref, gate_ref = refs[:2]
    before_ref = None if first else refs[2]
    out_ref, acc_ref = refs[-2:] if last else (refs[-1], refs[-1])
    depth = shards[0].shape[1]
    count = weight_ref.shape[1] // depth
    tiles = [pl.ds(tile * LANES, LANES) for tile in range(weight_ref.shape[0] // LANES)]
    if not first:
        acc_ref[...] = before_ref[...]
    for shard, hop in zip(shards, hops):
        at = facts_ref[0, 4 + REACH] + hop
        features = pl.ds(pl.multiple_of(jnp.clip(at, 0, count - 1) * depth, depth), depth)

        def add(shard=shard, hop=hop, features=features):
            for lanes in tiles:
                part = nt(shard[...], weight_ref[lanes, features])
                if hop == 0:
                    acc_ref[:, lanes] = part
                else:
                    acc_ref[:, lanes] += part

        if hop == 0:
            add()
        else:
            pl.when((at >= 0) & (at < count))(add)
    if last:
        out_ref[...] = (acc_ref[...] * gate_ref[0, slot].astype(F32)).astype(BF16)


def project(facts, shards, hops, weight, gate, slot, before=None, last=True, after=()):
    rows, depth = shards[0].shape
    width = weight.shape[0]
    operands = [facts, *shards, weight, gate]
    if before is not None:
        operands.append(before)
    return pl.pallas_call(
        functools.partial(project_kernel, hops, slot, before is None, last),
        out_shape=pltpu.VMEM((rows, width), BF16 if last else F32),
        in_specs=[SCALARS] + [WHOLE] * (len(operands) - 1) + [ANYWHERE] * len(after),
        out_specs=WHOLE,
        scratch_shapes=[pltpu.VMEM((rows, width), F32)] if last else [],
        compiler_params=params(),
        cost_estimate=pl.CostEstimate(
            flops=2 * rows * depth * (len(shards) + 1) // 2 * width,
            bytes_accessed=2 * (rows + width) * depth * len(shards),
            transcendentals=0,
        ),
    )(*operands, *after)


class Conv:
    def __init__(self, slot, facts, table, back, spectra):
        self.facts = [facts[slot, at] for at in range(4 + REACH)]
        self.table, self.back, self.spectra = table, back, spectra
        self.length = table.shape[0] // 2
        self.lanes = lanes_at(pl.program_id(0))
        self.row = lax.broadcasted_iota(jnp.int32, (self.length, LANES), 0)

    def joined(self, pieces):
        tiles = [piece[:, self.lanes] for piece in pieces]
        return tiles[0] if len(tiles) == 1 else jnp.concatenate(tiles, axis=0)

    def within(self, low, high):
        return (self.row >= low) & (self.row < high)

    def term(self, values, low, high, distance):
        length = self.length
        kept = jnp.where(self.within(low, high), values.astype(F32), 0.0).astype(BF16)
        full = nn(self.table[...], kept)
        real, imag = full[:length], full[length:]
        k_real = self.spectra[distance, :length, self.lanes]
        k_imag = self.spectra[distance, length:, self.lanes]
        return k_real * real - k_imag * imag, k_real * imag + k_imag * real

    def signal(self, real, imag):
        total = jnp.concatenate([real.astype(BF16), imag.astype(BF16)], axis=0)
        both = nn(self.back[...], total)
        return both[: self.length] + both[self.length :]

    def far_terms(self, acc, chosen, choices):
        for distance in range(1, REACH + 1):
            reach = self.facts[1 + distance]

            @pl.when(reach > 0)
            def _(distance=distance, reach=reach):
                for pieces, holds in choices(distance):

                    @pl.when(holds)
                    def _(pieces=pieces):
                        chosen[...] = self.joined(pieces)

                real, imag = self.term(chosen[...], 0, reach, distance)
                acc[: self.length, :] += real
                acc[self.length :, :] += imag

    def inner_documents(self, own, read, write):
        first_end, last_start = self.facts[0], self.facts[1]

        @pl.when(last_start > 0)
        def _():
            signal = self.signal(*self.term(own, 0, first_end, 0))
            write(jnp.where(self.row < first_end, signal, read()))

        @pl.when(last_start > first_end)
        def _():
            signal = self.signal(*self.term(own, first_end, last_start, 0))
            write(jnp.where(self.within(first_end, last_start), signal, read()))

    def halo(self, pieces, distance, mixed):
        sets = 3 if mixed else 4
        count = len(pieces) // sets
        kinds = [pieces[at * count : (at + 1) * count] for at in range(sets)]
        two, swapped, mate, far = kinds[0], kinds[1], kinds[2], kinds[-1]
        inner = self.facts[5]
        if distance == 2:
            return [(two, inner >= 0)]
        if distance == 1:
            return [(mate, inner == 1), (swapped, inner == 0)]
        return [(swapped, inner == 1), (far, inner == 0)]


def own_kernel(slot, pieces, facts_ref, table_ref, back_ref, spec_ref, *refs):
    own_refs, out_ref = refs[:pieces], refs[-1]
    conv = Conv(slot, facts_ref, table_ref, back_ref, spec_ref)
    own = conv.joined(own_refs)
    out_ref[:, conv.lanes] = conv.signal(*conv.term(own, conv.facts[1], conv.length, 0))

    def write(value):
        out_ref[:, conv.lanes] = value

    conv.inner_documents(own, lambda: out_ref[:, conv.lanes], write)


def far_kernel(slot, pieces, facts_ref, table_ref, back_ref, spec_ref, *refs):
    near_ref, refs = refs[0], refs[1:]
    if slot == 0:
        upper_ref, mate_ref, two_ref, fold_ref = refs[:4]
        halos = refs[4 : 4 + 3 * pieces]
    else:
        halos = refs[: 4 * pieces]
    out_ref, acc_ref, chosen_ref = refs[-3:]
    if slot == 1:
        out_ref, token_ref = refs[-4:-2]
        token_ref[...] = jnp.zeros_like(token_ref)
    conv = Conv(slot, facts_ref, table_ref, back_ref, spec_ref)
    role = conv.facts[6]

    def choices(distance):
        found = conv.halo(halos, distance, slot == 0)
        if slot == 0:
            folded = {
                1: [([upper_ref], role == 1)],
                2: [([mate_ref], (role == 1) | (role == 2))],
                3: [([two_ref], role == 1), ([upper_ref], role == 2), ([fold_ref], role == 3)],
            }
            found = found + folded[distance]
        return found

    reaches = conv.facts[2] > 0

    @pl.when(reaches)
    def _():
        acc_ref[...] = jnp.zeros_like(acc_ref)
        conv.far_terms(acc_ref, chosen_ref, choices)
        signal = conv.signal(acc_ref[: conv.length, :], acc_ref[conv.length :, :])
        kept = jnp.where(conv.row >= conv.facts[1], signal, 0.0)
        out_ref[0, 0] = near_ref[:, conv.lanes] + kept

    @pl.when(jnp.logical_not(reaches))
    def _():
        out_ref[0, 0] = near_ref[:, conv.lanes]


def conv_call(body, tabs, facts, arrays, out_shape, out_spec, scratch, after=(), result=None):
    table, back, spectra = tabs
    length = table.shape[0] // 2
    width = spectra.shape[2]
    operands = [facts, table, back, spectra, *arrays]
    specs = [SCALARS] + [WHOLE] * (len(operands) - 1) + [ANYWHERE] * len(after)
    operands.extend(after)
    aliases = {}
    if result is not None:
        aliases = {len(operands): 0}
        operands.append(result)
        specs.append(ANYWHERE)
    return pl.pallas_call(
        body,
        grid=(width // LANES,),
        out_shape=out_shape,
        in_specs=specs,
        out_specs=out_spec,
        scratch_shapes=scratch,
        input_output_aliases=aliases,
        compiler_params=params(),
        cost_estimate=pl.CostEstimate(
            flops=32 * length * length * width,
            bytes_accessed=4 * length * width,
            transcendentals=0,
        ),
    )(*operands)


def own_terms(slot, tabs, facts, pieces, after=()):
    _, back, spectra = tabs
    shape = pltpu.VMEM((back.shape[0] // 2, spectra.shape[2]), F32)
    body = functools.partial(own_kernel, slot, len(pieces))
    return conv_call(body, tabs, facts, pieces, shape, WHOLE, [], after)


def far_terms(slot, count, tabs, facts, arrays, result=None):
    _, back, spectra = tabs
    length, width = back.shape[0] // 2, spectra.shape[2]
    shape = jax.ShapeDtypeStruct((1, 2, length, width), F32)
    spec = pl.BlockSpec((1, 1, length, LANES), lambda c: (0, slot, 0, c))
    scratch = [pltpu.VMEM((2 * length, LANES), F32), pltpu.VMEM((length, LANES), BF16)]
    body = functools.partial(far_kernel, slot, count)
    if slot == 1:
        shape, spec = (shape, pltpu.VMEM((8, 128), F32)), (spec, WHOLE)
    return conv_call(body, tabs, facts, arrays, shape, spec, scratch, (), result)


def ordered(value, *earlier):
    return pl.pallas_call(
        lambda *refs: None,
        out_shape=jax.ShapeDtypeStruct(value.shape, value.dtype),
        in_specs=[ANYWHERE] * (1 + len(earlier)),
        out_specs=ANYWHERE,
        input_output_aliases={0: 0},
        compiler_params=params(VMEM // 20),
    )(value, *earlier)


def shifted(value, steps):
    count = lax.axis_size("ctx")
    initial, last = (max(0, -steps), min(count, count - steps))
    return lax.ppermute(value, "ctx", [(source, source + steps) for source in range(initial, last)])


def core_swapped(value):
    count = lax.axis_size("ctx")
    return lax.ppermute(value, "ctx", [(source, source ^ 1) for source in range(count)])


def upper_halo_of(value):
    count = lax.axis_size("ctx")
    far = [(source, source + 3) for source in range(1, count - 3, 2)] + [(count - 1, count - 3)]
    two = shifted(value, 2)
    mate, far = core_swapped(value), lax.ppermute(value, "ctx", far)
    return [two, core_swapped(two), mate, far]


def lower_halo_of(value, own):
    count = lax.axis_size("ctx")
    mixed = [(source, source - 1) for source in range(1, count, 2)]
    mixed += [(source, source - 3) for source in range(4, count, 2)]
    two = ordered(shifted(value, -2), own)
    mixed = lax.ppermute(value, "ctx", mixed)
    return [two, core_swapped(two), mixed]


def on_device(grad_out, out_weight, gate, filter_taps, doc_starts):
    pairs = lax.axis_size("ctx")
    place = lax.axis_index("ctx")
    length = grad_out.shape[2]
    width = out_weight.shape[0]
    count = lax.axis_size("ch")
    lane = lax.axis_index("ch").astype(jnp.int32)[None]

    def sent(step, up, down):
        upward = [(source, source + 1) for source in range(step - 1, count - 1)]
        downward = [(source, source - 1) for source in range(1, count - step + 1)]
        return lax.ppermute(up, "ch", upward), lax.ppermute(down, "ch", downward)

    start = grad_out[0, 1]
    upper_in = [sent(1, start, start)]

    table, back = (jnp.asarray(one) for one in tables(length))
    spectra, weight, gates, lower_slice, table, back, facts, prepared = prepare(
        pairs,
        place.astype(jnp.int32)[None],
        lane,
        doc_starts,
        table,
        back,
        filter_taps,
        out_weight,
        gate,
        grad_out,
    )
    tabs = (table, back, spectra)

    def pass_on(chain, *earlier):
        if earlier:
            chain[-1] = [ordered(one, *earlier) for one in chain[-1]]
        chain.append(sent(len(chain) + 1, *chain[-1]))

    hops = [0] + [way * step for step in range(1, count) for way in (-1, 1)]

    def partial_of(own, arrived, slot, after=()):
        shards = [own] + [one for pair in arrived[: count - 2] for one in pair]
        return project(
            facts, shards, hops[:-2], weight, gates, slot, last=False, after=after
        )

    def final_of(arrived, slot, partial, after=()):
        return project(facts, arrived[-1], hops[-2:], weight, gates, slot, partial, after=after)

    pass_on(upper_in, prepared)
    own = ordered(lower_slice, *upper_in[0])
    lower_in = [sent(1, own, own)]
    for _ in range(3, count):
        pass_on(upper_in)
        pass_on(lower_in, *upper_in[-2])
    partial = partial_of(start, upper_in, 1)
    upper = final_of(upper_in, 1, partial)
    pass_on(lower_in, upper)

    upper_halo = upper_halo_of(upper)
    two, swapped, mate, fold = upper_halo
    near = own_terms(1, tabs, facts, [upper])
    result, _ = far_terms(1, 1, tabs, facts, [near, *upper_halo])

    partial = partial_of(own, lower_in, 0, [near])
    lower = final_of(lower_in, 0, partial, [two, mate])
    near = own_terms(0, tabs, facts, [lower], after=[fold])
    lower_halo = lower_halo_of(lower, near)
    arrays = [near, upper, mate, two, fold, *lower_halo]
    return far_terms(0, 1, tabs, facts, arrays, result)


def solution(mesh):
    in_specs = (
        P("ctx", None, None, "ch"),
        P("ch", None),
        P("ctx", None, None, "ch"),
        P(None, "ch"),
        P(),
    )
    out_specs = P("ctx", None, None, "ch")
    return jax.shard_map(
        on_device, mesh=mesh, in_specs=in_specs, out_specs=out_specs, check_vma=False
    )
```

```python
import functools
import math

import jax
import jax.numpy as jnp
import ml_dtypes
import numpy as np
from jax import lax
from jax.experimental import pallas as pl
from jax.experimental.pallas import tpu as pltpu
from jax.sharding import PartitionSpec as P

REACH = 3
LANES = 512
VMEM = 20 * 1024 * 1024
F32 = jnp.float32
BF16 = jnp.bfloat16
WHOLE = pl.BlockSpec(memory_space=pltpu.VMEM)
ANYWHERE = pl.BlockSpec(memory_space=pl.ANY)
OUTSIDE = pl.BlockSpec(memory_space=pltpu.HBM)
SCALARS = pl.BlockSpec(memory_space=pltpu.SMEM)


def parts_of(table):
    high = table.astype(np.float32).astype(ml_dtypes.bfloat16)
    low = (table - high.astype(np.float64)).astype(np.float32).astype(ml_dtypes.bfloat16)
    return high, low


@functools.lru_cache(maxsize=None)
def tables(length):
    angle = np.outer(2 * np.arange(length) + 1, np.arange(length)) % (4 * length)
    angle = angle.astype(np.float64) * (math.pi / (2 * length))
    forward = np.concatenate([np.cos(angle), -np.sin(angle)], axis=0)
    high, low = parts_of(forward)
    back_high, back_low = parts_of(forward.T / length)
    return np.concatenate([high, low], axis=1), np.concatenate([back_high, back_low], axis=0)


def nn(a, b):
    return lax.dot_general(a, b, (((1,), (0,)), ((), ())), preferred_element_type=F32)


def nt(a, b):
    return lax.dot_general(a, b, (((1,), (1,)), ((), ())), preferred_element_type=F32)


def params(limit=VMEM):
    return pltpu.CompilerParams(vmem_limit_bytes=limit)


def lanes_at(tile):
    return pl.ds(pl.multiple_of(tile * LANES, LANES), LANES)


def write_facts(facts_ref, slot, docs_ref, block, length, end, inner, role):
    start = block * length
    stop = start + length - 1

    def visit(at, found):
        first, following, last = found
        here = docs_ref[at]
        first = jnp.minimum(first, jnp.where(here > start, here, end))
        following = jnp.minimum(following, jnp.where(here > stop, here, end))
        last = jnp.maximum(last, jnp.where(here <= stop, here, 0))
        return first, following, last

    whole = jnp.int32(end)
    first, following, last = lax.fori_loop(
        0, docs_ref.shape[0], visit, (whole, whole, jnp.int32(0))
    )
    facts_ref[slot, 0] = jnp.clip(first - start, 0, length)
    facts_ref[slot, 1] = jnp.clip(last - start, 0, length)
    for distance in range(1, REACH + 1):
        facts_ref[slot, 1 + distance] = jnp.clip(following - start - distance * length, 0, length)
    facts_ref[slot, 2 + REACH] = inner
    facts_ref[slot, 3 + REACH] = role


def prepare_kernel(pairs, *refs):
    place_ref, lane_ref, docs_ref, table_ref, back_ref, taps_ref = refs[:6]
    weight_ref, gate_ref, grad_ref = refs[6:9]
    spec_out, weight_out, gate_out, lower_out, table_out, back_out = refs[9:15]
    facts_out, token_out, sems = refs[15:]
    token_out[...] = jnp.zeros_like(token_out)
    copies = [
        pltpu.make_async_copy(source, target, sems.at[at])
        for at, (source, target) in enumerate(
            [
                (grad_ref.at[0, 0], lower_out),
                (weight_ref, weight_out),
                (gate_ref, gate_out),
                (back_ref, back_out),
            ]
        )
    ]
    step = pl.program_id(0)
    length = table_ref.shape[1] // 2

    @pl.when(step == 0)
    def _():
        for copy in copies:
            copy.start()
        table_out[...] = table_ref[:, :length]
        place = place_ref[0]
        odd = lax.rem(place, 2)
        role = jnp.where(place >= pairs - 3, pairs - place, 0)
        end = 2 * pairs * length
        for slot in range(2):
            facts_out[slot, 4 + REACH] = lane_ref[0]
        write_facts(facts_out, 0, docs_ref, place, length, end, 1 - odd, role)
        write_facts(facts_out, 1, docs_ref, 2 * pairs - 1 - place, length, end, odd, role)

    freq = lax.broadcasted_iota(jnp.int32, (length, 1), 0)
    sign = jnp.where(freq % 2 == 0, 1.0, -1.0).astype(F32)
    lanes = lanes_at(step)
    before = None
    for part in range(REACH + 1):
        if part < REACH:
            values = taps_ref[part * length : (part + 1) * length, :]
            high = values.astype(BF16)
            low = (values - high.astype(F32)).astype(BF16)
            full = nn(table_ref[...], jnp.concatenate([high, high], axis=0))
            full = full + nn(table_ref[:, :length], low)
            now = (full[:length], -full[length:])
        else:
            now = None
        if before is None:
            real, imag = now
        else:
            real, imag = sign * before[1], -sign * before[0]
            if now is not None:
                real, imag = now[0] + real, now[1] + imag
        spec_out[part, :length, lanes] = real
        spec_out[part, length:, lanes] = imag
        before = now

    @pl.when(step == pl.num_programs(0) - 1)
    def _():
        for copy in copies:
            copy.wait()


def prepare(pairs, place, lane, docs, table, back, taps, weight, gate, grad):
    count, width = taps.shape
    length = count // REACH
    return pl.pallas_call(
        functools.partial(prepare_kernel, pairs),
        grid=(width // LANES,),
        out_shape=(
            pltpu.VMEM((REACH + 1, 2 * length, width), F32),
            pltpu.VMEM(weight.shape, BF16),
            pltpu.VMEM(gate.shape, BF16),
            pltpu.VMEM(grad.shape[2:], BF16),
            pltpu.VMEM((2 * length, length), BF16),
            pltpu.VMEM(back.shape, BF16),
            pltpu.SMEM((2, 8), jnp.int32),
            pltpu.VMEM((8, 128), F32),
        ),
        in_specs=[
            SCALARS,
            SCALARS,
            SCALARS,
            pl.BlockSpec((2 * length, 2 * length), lambda c: (0, 0)),
            OUTSIDE,
            pl.BlockSpec((count, LANES), lambda c: (0, c)),
            OUTSIDE,
            OUTSIDE,
            OUTSIDE,
        ],
        out_specs=(WHOLE,) * 6 + (SCALARS, WHOLE),
        scratch_shapes=[pltpu.SemaphoreType.DMA((4,))],
        compiler_params=params(2 * VMEM),
        cost_estimate=pl.CostEstimate(
            flops=2 * 3 * 2 * count * length * width,
            bytes_accessed=4 * (count * width + 8 * length * width),
            transcendentals=0,
        ),
    )(place, lane, docs, table, back, taps, weight, gate, grad)


def project_kernel(hops, slot, first, last, facts_ref, *refs):
    shards, refs = refs[: len(hops)], refs[len(hops) :]
    weight_ref, gate_ref = refs[:2]
    before_ref = None if first else refs[2]
    out_ref, acc_ref = refs[-2:] if last else (refs[-1], refs[-1])
    depth = shards[0].shape[1]
    count = weight_ref.shape[1] // depth
    tiles = [pl.ds(tile * LANES, LANES) for tile in range(weight_ref.shape[0] // LANES)]
    if not first:
        acc_ref[...] = before_ref[...]
    for shard, hop in zip(shards, hops):
        at = facts_ref[0, 4 + REACH] + hop
        features = pl.ds(pl.multiple_of(jnp.clip(at, 0, count - 1) * depth, depth), depth)

        def add(shard=shard, hop=hop, features=features):
            for lanes in tiles:
                part = nt(shard[...], weight_ref[lanes, features])
                if hop == 0:
                    acc_ref[:, lanes] = part
                else:
                    acc_ref[:, lanes] += part

        if hop == 0:
            add()
        else:
            pl.when((at >= 0) & (at < count))(add)
    if last:
        out_ref[...] = (acc_ref[...] * gate_ref[0, slot].astype(F32)).astype(BF16)


def project(facts, shards, hops, weight, gate, slot, before=None, last=True, after=()):
    rows, depth = shards[0].shape
    width = weight.shape[0]
    operands = [facts, *shards, weight, gate]
    if before is not None:
        operands.append(before)
    return pl.pallas_call(
        functools.partial(project_kernel, hops, slot, before is None, last),
        out_shape=pltpu.VMEM((rows, width), BF16 if last else F32),
        in_specs=[SCALARS] + [WHOLE] * (len(operands) - 1) + [ANYWHERE] * len(after),
        out_specs=WHOLE,
        scratch_shapes=[pltpu.VMEM((rows, width), F32)] if last else [],
        compiler_params=params(),
        cost_estimate=pl.CostEstimate(
            flops=2 * rows * depth * (len(shards) + 1) // 2 * width,
            bytes_accessed=2 * (rows + width) * depth * len(shards),
            transcendentals=0,
        ),
    )(*operands, *after)


class Conv:
    def __init__(self, slot, facts, table, back, spectra):
        self.facts = [facts[slot, at] for at in range(4 + REACH)]
        self.table, self.back, self.spectra = table, back, spectra
        self.length = table.shape[0] // 2
        self.lanes = lanes_at(pl.program_id(0))
        self.row = lax.broadcasted_iota(jnp.int32, (self.length, LANES), 0)

    def joined(self, pieces):
        tiles = [piece[:, self.lanes] for piece in pieces]
        return tiles[0] if len(tiles) == 1 else jnp.concatenate(tiles, axis=0)

    def within(self, low, high):
        return (self.row >= low) & (self.row < high)

    def term(self, values, low, high, distance):
        length = self.length
        kept = jnp.where(self.within(low, high), values.astype(F32), 0.0).astype(BF16)
        full = nn(self.table[...], kept)
        real, imag = full[:length], full[length:]
        k_real = self.spectra[distance, :length, self.lanes]
        k_imag = self.spectra[distance, length:, self.lanes]
        return k_real * real - k_imag * imag, k_real * imag + k_imag * real

    def signal(self, real, imag):
        total = jnp.concatenate([real.astype(BF16), imag.astype(BF16)], axis=0)
        both = nn(self.back[...], total)
        return both[: self.length] + both[self.length :]

    def far_terms(self, acc, chosen, choices):
        for distance in range(1, REACH + 1):
            reach = self.facts[1 + distance]

            @pl.when(reach > 0)
            def _(distance=distance, reach=reach):
                for pieces, holds in choices(distance):

                    @pl.when(holds)
                    def _(pieces=pieces):
                        chosen[...] = self.joined(pieces)

                real, imag = self.term(chosen[...], 0, reach, distance)
                acc[: self.length, :] += real
                acc[self.length :, :] += imag

    def inner_documents(self, own, read, write):
        first_end, last_start = self.facts[0], self.facts[1]

        @pl.when(last_start > 0)
        def _():
            signal = self.signal(*self.term(own, 0, first_end, 0))
            write(jnp.where(self.row < first_end, signal, read()))

        @pl.when(last_start > first_end)
        def _():
            signal = self.signal(*self.term(own, first_end, last_start, 0))
            write(jnp.where(self.within(first_end, last_start), signal, read()))

    def halo(self, pieces, distance, mixed):
        sets = 3 if mixed else 4
        count = len(pieces) // sets
        kinds = [pieces[at * count : (at + 1) * count] for at in range(sets)]
        two, swapped, mate, far = kinds[0], kinds[1], kinds[2], kinds[-1]
        inner = self.facts[5]
        if distance == 2:
            return [(two, inner >= 0)]
        if distance == 1:
            return [(mate, inner == 1), (swapped, inner == 0)]
        return [(swapped, inner == 1), (far, inner == 0)]


def own_kernel(slot, pieces, facts_ref, table_ref, back_ref, spec_ref, *refs):
    own_refs, out_ref = refs[:pieces], refs[-1]
    conv = Conv(slot, facts_ref, table_ref, back_ref, spec_ref)
    own = conv.joined(own_refs)
    out_ref[:, conv.lanes] = conv.signal(*conv.term(own, conv.facts[1], conv.length, 0))

    def write(value):
        out_ref[:, conv.lanes] = value

    conv.inner_documents(own, lambda: out_ref[:, conv.lanes], write)


def far_kernel(slot, pieces, facts_ref, table_ref, back_ref, spec_ref, *refs):
    near_ref, refs = refs[0], refs[1:]
    if slot == 0:
        upper_ref, mate_ref, two_ref, fold_ref = refs[:4]
        halos = refs[4 : 4 + 3 * pieces]
    else:
        halos = refs[: 4 * pieces]
    out_ref, acc_ref, chosen_ref = refs[-3:]
    if slot == 1:
        out_ref, token_ref = refs[-4:-2]
        token_ref[...] = jnp.zeros_like(token_ref)
    conv = Conv(slot, facts_ref, table_ref, back_ref, spec_ref)
    role = conv.facts[6]

    def choices(distance):
        found = conv.halo(halos, distance, slot == 0)
        if slot == 0:
            folded = {
                1: [([upper_ref], role == 1)],
                2: [([mate_ref], (role == 1) | (role == 2))],
                3: [([two_ref], role == 1), ([upper_ref], role == 2), ([fold_ref], role == 3)],
            }
            found = found + folded[distance]
        return found

    reaches = conv.facts[2] > 0

    @pl.when(reaches)
    def _():
        acc_ref[...] = jnp.zeros_like(acc_ref)
        conv.far_terms(acc_ref, chosen_ref, choices)
        signal = conv.signal(acc_ref[: conv.length, :], acc_ref[conv.length :, :])
        kept = jnp.where(conv.row >= conv.facts[1], signal, 0.0)
        out_ref[0, 0] = near_ref[:, conv.lanes] + kept

    @pl.when(jnp.logical_not(reaches))
    def _():
        out_ref[0, 0] = near_ref[:, conv.lanes]


def conv_call(body, tabs, facts, arrays, out_shape, out_spec, scratch, after=(), result=None):
    table, back, spectra = tabs
    length = table.shape[0] // 2
    width = spectra.shape[2]
    operands = [facts, table, back, spectra, *arrays]
    specs = [SCALARS] + [WHOLE] * (len(operands) - 1) + [ANYWHERE] * len(after)
    operands.extend(after)
    aliases = {}
    if result is not None:
        aliases = {len(operands): 0}
        operands.append(result)
        specs.append(ANYWHERE)
    return pl.pallas_call(
        body,
        grid=(width // LANES,),
        out_shape=out_shape,
        in_specs=specs,
        out_specs=out_spec,
        scratch_shapes=scratch,
        input_output_aliases=aliases,
        compiler_params=params(),
        cost_estimate=pl.CostEstimate(
            flops=32 * length * length * width,
            bytes_accessed=4 * length * width,
            transcendentals=0,
        ),
    )(*operands)


def own_terms(slot, tabs, facts, pieces, after=()):
    _, back, spectra = tabs
    shape = pltpu.VMEM((back.shape[0] // 2, spectra.shape[2]), F32)
    body = functools.partial(own_kernel, slot, len(pieces))
    return conv_call(body, tabs, facts, pieces, shape, WHOLE, [], after)


def far_terms(slot, count, tabs, facts, arrays, result=None):
    _, back, spectra = tabs
    length, width = back.shape[0] // 2, spectra.shape[2]
    shape = jax.ShapeDtypeStruct((1, 2, length, width), F32)
    spec = pl.BlockSpec((1, 1, length, LANES), lambda c: (0, slot, 0, c))
    scratch = [pltpu.VMEM((2 * length, LANES), F32), pltpu.VMEM((length, LANES), BF16)]
    body = functools.partial(far_kernel, slot, count)
    if slot == 1:
        shape, spec = (shape, pltpu.VMEM((8, 128), F32)), (spec, WHOLE)
    return conv_call(body, tabs, facts, arrays, shape, spec, scratch, (), result)


def together(values, *earlier):
    return pl.pallas_call(
        lambda *refs: None,
        out_shape=[jax.ShapeDtypeStruct(one.shape, one.dtype) for one in values],
        in_specs=[ANYWHERE] * (len(values) + len(earlier)),
        out_specs=[ANYWHERE] * len(values),
        input_output_aliases={at: at for at in range(len(values))},
        compiler_params=params(VMEM // 20),
    )(*values, *earlier)


def ordered(value, *earlier):
    return together([value], *earlier)[0]


def shifted(value, steps):
    count = lax.axis_size("ctx")
    initial, last = (max(0, -steps), min(count, count - steps))
    return lax.ppermute(value, "ctx", [(source, source + steps) for source in range(initial, last)])


def core_swapped(value):
    count = lax.axis_size("ctx")
    return lax.ppermute(value, "ctx", [(source, source ^ 1) for source in range(count)])


def upper_halo_of(value):
    count = lax.axis_size("ctx")
    far = [(source, source + 3) for source in range(1, count - 3, 2)] + [(count - 1, count - 3)]
    two = shifted(value, 2)
    mate, far = core_swapped(value), lax.ppermute(value, "ctx", far)
    return [two, core_swapped(two), mate, far]


def lower_halo_of(value, own):
    count = lax.axis_size("ctx")
    mixed = [(source, source - 1) for source in range(1, count, 2)]
    mixed += [(source, source - 3) for source in range(4, count, 2)]
    two = ordered(shifted(value, -2), own)
    mixed = lax.ppermute(ordered(value, two), "ctx", mixed)
    return [two, core_swapped(two), mixed]


def on_device(grad_out, out_weight, gate, filter_taps, doc_starts):
    pairs = lax.axis_size("ctx")
    place = lax.axis_index("ctx")
    length = grad_out.shape[2]
    width = out_weight.shape[0]
    count = lax.axis_size("ch")
    lane = lax.axis_index("ch").astype(jnp.int32)[None]

    def sent(step, up, down):
        upward = [(source, source + 1) for source in range(step - 1, count - 1)]
        downward = [(source, source - 1) for source in range(1, count - step + 1)]
        return lax.ppermute(up, "ch", upward), lax.ppermute(down, "ch", downward)

    start = grad_out[0, 1]
    upper_in = [sent(1, start, start)]

    table, back = (jnp.asarray(one) for one in tables(length))
    spectra, weight, gates, lower_slice, table, back, facts, prepared = prepare(
        pairs,
        place.astype(jnp.int32)[None],
        lane,
        doc_starts,
        table,
        back,
        filter_taps,
        out_weight,
        gate,
        grad_out,
    )
    tabs = (table, back, spectra)

    def pass_on(chain, *earlier):
        if earlier:
            chain[-1] = together(chain[-1], *earlier)
        chain.append(sent(len(chain) + 1, *chain[-1]))

    hops = [0] + [way * step for step in range(1, count) for way in (-1, 1)]

    def partial_of(own, arrived, slot, after=()):
        shards = [own] + [one for pair in arrived[: count - 2] for one in pair]
        return project(
            facts, shards, hops[:-2], weight, gates, slot, last=False, after=after
        )

    def final_of(arrived, slot, partial, after=()):
        return project(facts, arrived[-1], hops[-2:], weight, gates, slot, partial, after=after)

    pass_on(upper_in, prepared)
    own = ordered(lower_slice, *upper_in[0])
    lower_in = [sent(1, own, own)]
    for _ in range(3, count):
        pass_on(upper_in)
        pass_on(lower_in, *upper_in[-2])
    partial = partial_of(start, upper_in, 1)
    upper = final_of(upper_in, 1, partial)
    upper_halo = upper_halo_of(upper)
    two, swapped, mate, fold = upper_halo
    near = own_terms(1, tabs, facts, [upper])
    pass_on(lower_in, upper, mate, near)
    result, _ = far_terms(1, 1, tabs, facts, [near, *upper_halo])

    partial = partial_of(own, lower_in, 0)
    lower = final_of(lower_in, 0, partial, [two])
    near = own_terms(0, tabs, facts, [lower], after=[fold])
    lower_halo = lower_halo_of(lower, near)
    arrays = [near, upper, mate, two, fold, *lower_halo]
    return far_terms(0, 1, tabs, facts, arrays, result)


def solution(mesh):
    in_specs = (
        P("ctx", None, None, "ch"),
        P("ch", None),
        P("ctx", None, None, "ch"),
        P(None, "ch"),
        P(),
    )
    out_specs = P("ctx", None, None, "ch")
    return jax.shard_map(
        on_device, mesh=mesh, in_specs=in_specs, out_specs=out_specs, check_vma=False
    )
```

```python
import functools
import math

import jax
import jax.numpy as jnp
import ml_dtypes
import numpy as np
from jax import lax
from jax.experimental import pallas as pl
from jax.experimental.pallas import tpu as pltpu
from jax.sharding import PartitionSpec as P

REACH = 3
LANES = 512
VMEM = 20 * 1024 * 1024
F32 = jnp.float32
BF16 = jnp.bfloat16
WHOLE = pl.BlockSpec(memory_space=pltpu.VMEM)
ANYWHERE = pl.BlockSpec(memory_space=pl.ANY)
OUTSIDE = pl.BlockSpec(memory_space=pltpu.HBM)
SCALARS = pl.BlockSpec(memory_space=pltpu.SMEM)


def parts_of(table):
    high = table.astype(np.float32).astype(ml_dtypes.bfloat16)
    low = (table - high.astype(np.float64)).astype(np.float32).astype(ml_dtypes.bfloat16)
    return high, low


@functools.lru_cache(maxsize=None)
def tables(length):
    angle = np.outer(2 * np.arange(length) + 1, np.arange(length)) % (4 * length)
    angle = angle.astype(np.float64) * (math.pi / (2 * length))
    forward = np.concatenate([np.cos(angle), -np.sin(angle)], axis=0)
    high, low = parts_of(forward)
    back_high, back_low = parts_of(forward.T / length)
    return np.concatenate([high, low], axis=1), np.concatenate([back_high, back_low], axis=0)


def nn(a, b):
    return lax.dot_general(a, b, (((1,), (0,)), ((), ())), preferred_element_type=F32)


def nt(a, b):
    return lax.dot_general(a, b, (((1,), (1,)), ((), ())), preferred_element_type=F32)


def params(limit=VMEM):
    return pltpu.CompilerParams(vmem_limit_bytes=limit)


def lanes_at(tile):
    return pl.ds(pl.multiple_of(tile * LANES, LANES), LANES)


def write_facts(facts_ref, slot, docs_ref, block, length, end, inner, role):
    start = block * length
    stop = start + length - 1

    def visit(at, found):
        first, following, last = found
        here = docs_ref[at]
        first = jnp.minimum(first, jnp.where(here > start, here, end))
        following = jnp.minimum(following, jnp.where(here > stop, here, end))
        last = jnp.maximum(last, jnp.where(here <= stop, here, 0))
        return first, following, last

    whole = jnp.int32(end)
    first, following, last = lax.fori_loop(
        0, docs_ref.shape[0], visit, (whole, whole, jnp.int32(0))
    )
    facts_ref[slot, 0] = jnp.clip(first - start, 0, length)
    facts_ref[slot, 1] = jnp.clip(last - start, 0, length)
    for distance in range(1, REACH + 1):
        facts_ref[slot, 1 + distance] = jnp.clip(following - start - distance * length, 0, length)
    facts_ref[slot, 2 + REACH] = inner
    facts_ref[slot, 3 + REACH] = role


def prepare_kernel(pairs, *refs):
    place_ref, lane_ref, docs_ref, table_ref, back_ref, taps_ref = refs[:6]
    weight_ref, gate_ref, grad_ref = refs[6:9]
    spec_out, weight_out, gate_out, grad_out, table_out, back_out = refs[9:15]
    facts_out, token_out, sems = refs[15:]
    token_out[...] = jnp.zeros_like(token_out)
    copies = [
        pltpu.make_async_copy(source, target, sems.at[at])
        for at, (source, target) in enumerate(
            [
                (grad_ref, grad_out),
                (weight_ref, weight_out),
                (gate_ref, gate_out),
                (back_ref, back_out),
            ]
        )
    ]
    step = pl.program_id(0)
    length = table_ref.shape[1] // 2

    @pl.when(step == 0)
    def _():
        for copy in copies:
            copy.start()
        table_out[...] = table_ref[:, :length]
        place = place_ref[0]
        odd = lax.rem(place, 2)
        role = jnp.where(place >= pairs - 3, pairs - place, 0)
        end = 2 * pairs * length
        for slot in range(2):
            facts_out[slot, 4 + REACH] = lane_ref[0]
        write_facts(facts_out, 0, docs_ref, place, length, end, 1 - odd, role)
        write_facts(facts_out, 1, docs_ref, 2 * pairs - 1 - place, length, end, odd, role)

    freq = lax.broadcasted_iota(jnp.int32, (length, 1), 0)
    sign = jnp.where(freq % 2 == 0, 1.0, -1.0).astype(F32)
    lanes = lanes_at(step)
    before = None
    for part in range(REACH + 1):
        if part < REACH:
            values = taps_ref[part * length : (part + 1) * length, :]
            high = values.astype(BF16)
            low = (values - high.astype(F32)).astype(BF16)
            full = nn(table_ref[...], jnp.concatenate([high, high], axis=0))
            full = full + nn(table_ref[:, :length], low)
            now = (full[:length], -full[length:])
        else:
            now = None
        if before is None:
            real, imag = now
        else:
            real, imag = sign * before[1], -sign * before[0]
            if now is not None:
                real, imag = now[0] + real, now[1] + imag
        spec_out[part, :length, lanes] = real
        spec_out[part, length:, lanes] = imag
        before = now

    @pl.when(step == pl.num_programs(0) - 1)
    def _():
        for copy in copies:
            copy.wait()


def prepare(pairs, place, lane, docs, table, back, taps, weight, gate, grad):
    count, width = taps.shape
    length = count // REACH
    return pl.pallas_call(
        functools.partial(prepare_kernel, pairs),
        grid=(width // LANES,),
        out_shape=(
            pltpu.VMEM((REACH + 1, 2 * length, width), F32),
            pltpu.VMEM(weight.shape, BF16),
            pltpu.VMEM(gate.shape, BF16),
            pltpu.VMEM(grad.shape, BF16),
            pltpu.VMEM((2 * length, length), BF16),
            pltpu.VMEM(back.shape, BF16),
            pltpu.SMEM((2, 8), jnp.int32),
            pltpu.VMEM((8, 128), F32),
        ),
        in_specs=[
            SCALARS,
            SCALARS,
            SCALARS,
            pl.BlockSpec((2 * length, 2 * length), lambda c: (0, 0)),
            OUTSIDE,
            pl.BlockSpec((count, LANES), lambda c: (0, c)),
            OUTSIDE,
            OUTSIDE,
            OUTSIDE,
        ],
        out_specs=(WHOLE,) * 6 + (SCALARS, WHOLE),
        scratch_shapes=[pltpu.SemaphoreType.DMA((4,))],
        compiler_params=params(2 * VMEM),
        cost_estimate=pl.CostEstimate(
            flops=2 * 3 * 2 * count * length * width,
            bytes_accessed=4 * (count * width + 8 * length * width),
            transcendentals=0,
        ),
    )(place, lane, docs, table, back, taps, weight, gate, grad)


def project_kernel(hops, slot, first, last, facts_ref, *refs):
    shards, refs = refs[: len(hops)], refs[len(hops) :]
    weight_ref, gate_ref = refs[:2]
    before_ref = None if first else refs[2]
    out_ref, acc_ref = refs[-2:] if last else (refs[-1], refs[-1])
    depth = shards[0].shape[-1]
    count = weight_ref.shape[1] // depth
    tiles = [pl.ds(tile * LANES, LANES) for tile in range(weight_ref.shape[0] // LANES)]
    if not first:
        acc_ref[...] = before_ref[...]
    for shard, hop in zip(shards, hops):
        at = facts_ref[0, 4 + REACH] + hop
        features = pl.ds(pl.multiple_of(jnp.clip(at, 0, count - 1) * depth, depth), depth)

        def add(shard=shard, hop=hop, features=features):
            for lanes in tiles:
                values = shard[...] if len(shard.shape) == 2 else shard[0, slot]
                part = nt(values, weight_ref[lanes, features])
                if hop == 0:
                    acc_ref[:, lanes] = part
                else:
                    acc_ref[:, lanes] += part

        if hop == 0:
            add()
        else:
            pl.when((at >= 0) & (at < count))(add)
    if last:
        out_ref[...] = (acc_ref[...] * gate_ref[0, slot].astype(F32)).astype(BF16)


def project(facts, shards, hops, weight, gate, slot, before=None, last=True, after=()):
    rows, depth = shards[0].shape[-2:]
    width = weight.shape[0]
    operands = [facts, *shards, weight, gate]
    if before is not None:
        operands.append(before)
    return pl.pallas_call(
        functools.partial(project_kernel, hops, slot, before is None, last),
        out_shape=pltpu.VMEM((rows, width), BF16 if last else F32),
        in_specs=[SCALARS] + [WHOLE] * (len(operands) - 1) + [ANYWHERE] * len(after),
        out_specs=WHOLE,
        scratch_shapes=[pltpu.VMEM((rows, width), F32)] if last else [],
        compiler_params=params(),
        cost_estimate=pl.CostEstimate(
            flops=2 * rows * depth * (len(shards) + 1) // 2 * width,
            bytes_accessed=2 * (rows + width) * depth * len(shards),
            transcendentals=0,
        ),
    )(*operands, *after)


class Conv:
    def __init__(self, slot, facts, table, back, spectra):
        self.facts = [facts[slot, at] for at in range(4 + REACH)]
        self.table, self.back, self.spectra = table, back, spectra
        self.length = table.shape[0] // 2
        self.lanes = lanes_at(pl.program_id(0))
        self.row = lax.broadcasted_iota(jnp.int32, (self.length, LANES), 0)

    def joined(self, pieces):
        tiles = [piece[:, self.lanes] for piece in pieces]
        return tiles[0] if len(tiles) == 1 else jnp.concatenate(tiles, axis=0)

    def within(self, low, high):
        return (self.row >= low) & (self.row < high)

    def term(self, values, low, high, distance):
        length = self.length
        kept = jnp.where(self.within(low, high), values.astype(F32), 0.0).astype(BF16)
        full = nn(self.table[...], kept)
        real, imag = full[:length], full[length:]
        k_real = self.spectra[distance, :length, self.lanes]
        k_imag = self.spectra[distance, length:, self.lanes]
        return k_real * real - k_imag * imag, k_real * imag + k_imag * real

    def signal(self, real, imag):
        total = jnp.concatenate([real.astype(BF16), imag.astype(BF16)], axis=0)
        both = nn(self.back[...], total)
        return both[: self.length] + both[self.length :]

    def far_terms(self, acc, chosen, choices):
        for distance in range(1, REACH + 1):
            reach = self.facts[1 + distance]

            @pl.when(reach > 0)
            def _(distance=distance, reach=reach):
                for pieces, holds in choices(distance):

                    @pl.when(holds)
                    def _(pieces=pieces):
                        chosen[...] = self.joined(pieces)

                real, imag = self.term(chosen[...], 0, reach, distance)
                acc[: self.length, :] += real
                acc[self.length :, :] += imag

    def inner_documents(self, own, read, write):
        first_end, last_start = self.facts[0], self.facts[1]

        @pl.when(last_start > 0)
        def _():
            signal = self.signal(*self.term(own, 0, first_end, 0))
            write(jnp.where(self.row < first_end, signal, read()))

        @pl.when(last_start > first_end)
        def _():
            signal = self.signal(*self.term(own, first_end, last_start, 0))
            write(jnp.where(self.within(first_end, last_start), signal, read()))

    def halo(self, pieces, distance, mixed):
        sets = 3 if mixed else 4
        count = len(pieces) // sets
        kinds = [pieces[at * count : (at + 1) * count] for at in range(sets)]
        two, swapped, mate, far = kinds[0], kinds[1], kinds[2], kinds[-1]
        inner = self.facts[5]
        if distance == 2:
            return [(two, inner >= 0)]
        if distance == 1:
            return [(mate, inner == 1), (swapped, inner == 0)]
        return [(swapped, inner == 1), (far, inner == 0)]


def own_kernel(slot, pieces, facts_ref, table_ref, back_ref, spec_ref, *refs):
    own_refs, out_ref = refs[:pieces], refs[-1]
    conv = Conv(slot, facts_ref, table_ref, back_ref, spec_ref)
    own = conv.joined(own_refs)
    out_ref[:, conv.lanes] = conv.signal(*conv.term(own, conv.facts[1], conv.length, 0))

    def write(value):
        out_ref[:, conv.lanes] = value

    conv.inner_documents(own, lambda: out_ref[:, conv.lanes], write)


def far_kernel(slot, pieces, facts_ref, table_ref, back_ref, spec_ref, *refs):
    near_ref, refs = refs[0], refs[1:]
    if slot == 0:
        upper_ref, mate_ref, two_ref, fold_ref = refs[:4]
        halos = refs[4 : 4 + 3 * pieces]
    else:
        halos = refs[: 4 * pieces]
    out_ref, acc_ref, chosen_ref = refs[-3:]
    if slot == 1:
        out_ref, token_ref = refs[-4:-2]
        token_ref[...] = jnp.zeros_like(token_ref)
    conv = Conv(slot, facts_ref, table_ref, back_ref, spec_ref)
    role = conv.facts[6]

    def choices(distance):
        found = conv.halo(halos, distance, slot == 0)
        if slot == 0:
            folded = {
                1: [([upper_ref], role == 1)],
                2: [([mate_ref], (role == 1) | (role == 2))],
                3: [([two_ref], role == 1), ([upper_ref], role == 2), ([fold_ref], role == 3)],
            }
            found = found + folded[distance]
        return found

    reaches = conv.facts[2] > 0

    @pl.when(reaches)
    def _():
        acc_ref[...] = jnp.zeros_like(acc_ref)
        conv.far_terms(acc_ref, chosen_ref, choices)
        signal = conv.signal(acc_ref[: conv.length, :], acc_ref[conv.length :, :])
        kept = jnp.where(conv.row >= conv.facts[1], signal, 0.0)
        out_ref[0, 0] = near_ref[:, conv.lanes] + kept

    @pl.when(jnp.logical_not(reaches))
    def _():
        out_ref[0, 0] = near_ref[:, conv.lanes]


def conv_call(body, tabs, facts, arrays, out_shape, out_spec, scratch, after=(), result=None):
    table, back, spectra = tabs
    length = table.shape[0] // 2
    width = spectra.shape[2]
    operands = [facts, table, back, spectra, *arrays]
    specs = [SCALARS] + [WHOLE] * (len(operands) - 1) + [ANYWHERE] * len(after)
    operands.extend(after)
    aliases = {}
    if result is not None:
        aliases = {len(operands): 0}
        operands.append(result)
        specs.append(ANYWHERE)
    return pl.pallas_call(
        body,
        grid=(width // LANES,),
        out_shape=out_shape,
        in_specs=specs,
        out_specs=out_spec,
        scratch_shapes=scratch,
        input_output_aliases=aliases,
        compiler_params=params(),
        cost_estimate=pl.CostEstimate(
            flops=32 * length * length * width,
            bytes_accessed=4 * length * width,
            transcendentals=0,
        ),
    )(*operands)


def own_terms(slot, tabs, facts, pieces, after=()):
    _, back, spectra = tabs
    shape = pltpu.VMEM((back.shape[0] // 2, spectra.shape[2]), F32)
    body = functools.partial(own_kernel, slot, len(pieces))
    return conv_call(body, tabs, facts, pieces, shape, WHOLE, [], after)


def far_terms(slot, count, tabs, facts, arrays, result=None):
    _, back, spectra = tabs
    length, width = back.shape[0] // 2, spectra.shape[2]
    shape = jax.ShapeDtypeStruct((1, 2, length, width), F32)
    spec = pl.BlockSpec((1, 1, length, LANES), lambda c: (0, slot, 0, c))
    scratch = [pltpu.VMEM((2 * length, LANES), F32), pltpu.VMEM((length, LANES), BF16)]
    body = functools.partial(far_kernel, slot, count)
    if slot == 1:
        shape, spec = (shape, pltpu.VMEM((8, 128), F32)), (spec, WHOLE)
    return conv_call(body, tabs, facts, arrays, shape, spec, scratch, (), result)


def together(values, *earlier):
    return pl.pallas_call(
        lambda *refs: None,
        out_shape=[jax.ShapeDtypeStruct(one.shape, one.dtype) for one in values],
        in_specs=[ANYWHERE] * (len(values) + len(earlier)),
        out_specs=[ANYWHERE] * len(values),
        input_output_aliases={at: at for at in range(len(values))},
        compiler_params=params(VMEM // 20),
    )(*values, *earlier)


def ordered(value, *earlier):
    return together([value], *earlier)[0]


def block_kernel(slot, *refs):
    count = len(refs) // 2
    for source, target in zip(refs[:count], refs[count:]):
        target[...] = source[0, slot]


def block_of(values, slot):
    shape = values[0].shape[2:]
    return pl.pallas_call(
        functools.partial(block_kernel, slot),
        out_shape=[pltpu.VMEM(shape, BF16)] * len(values),
        in_specs=[WHOLE] * len(values),
        out_specs=[WHOLE] * len(values),
        compiler_params=params(),
    )(*values)


def shifted(value, steps):
    count = lax.axis_size("ctx")
    initial, last = (max(0, -steps), min(count, count - steps))
    return lax.ppermute(value, "ctx", [(source, source + steps) for source in range(initial, last)])


def core_swapped(value):
    count = lax.axis_size("ctx")
    return lax.ppermute(value, "ctx", [(source, source ^ 1) for source in range(count)])


def upper_halo_of(value):
    count = lax.axis_size("ctx")
    far = [(source, source + 3) for source in range(1, count - 3, 2)] + [(count - 1, count - 3)]
    two = shifted(value, 2)
    mate, far = core_swapped(value), lax.ppermute(value, "ctx", far)
    return [two, core_swapped(two), mate, far]


def lower_halo_of(value, own):
    count = lax.axis_size("ctx")
    mixed = [(source, source - 1) for source in range(1, count, 2)]
    mixed += [(source, source - 3) for source in range(4, count, 2)]
    two = ordered(shifted(value, -2), own)
    mixed = lax.ppermute(value, "ctx", mixed)
    return [two, core_swapped(two), mixed]


def on_device(grad_out, out_weight, gate, filter_taps, doc_starts):
    pairs = lax.axis_size("ctx")
    place = lax.axis_index("ctx")
    length = grad_out.shape[2]
    width = out_weight.shape[0]
    count = lax.axis_size("ch")
    lane = lax.axis_index("ch").astype(jnp.int32)[None]

    def sent(step, up, down):
        upward = [(source, source + 1) for source in range(step - 1, count - 1)]
        downward = [(source, source - 1) for source in range(1, count - step + 1)]
        return lax.ppermute(up, "ch", upward), lax.ppermute(down, "ch", downward)

    chain = [sent(1, grad_out, grad_out)]

    table, back = (jnp.asarray(one) for one in tables(length))
    spectra, weight, gates, own, table, back, facts, prepared = prepare(
        pairs,
        place.astype(jnp.int32)[None],
        lane,
        doc_starts,
        table,
        back,
        filter_taps,
        out_weight,
        gate,
        grad_out,
    )
    tabs = (table, back, spectra)

    hops = [0] + [way * step for step in range(1, count) for way in (-1, 1)]

    def partial_of(slot, after=()):
        shards = [own] + [one for pair in chain for one in pair]
        args = (weight, gates, slot)
        return project(facts, shards, hops[:-2], *args, last=False, after=after)

    def final_of(arrived, slot, partial, after=()):
        return project(facts, arrived, hops[-2:], weight, gates, slot, partial, after=after)

    chain[0] = together(chain[0], prepared)
    for step in range(2, count - 1):
        chain.append(sent(step, *chain[-1]))
    arrived = sent(count - 1, *block_of(chain[-1], 1))
    partial, lower_partial = partial_of(1), partial_of(0)
    lower_part = together(block_of(chain[-1], 0), *arrived, partial)
    lower_arrived = sent(count - 1, *lower_part)

    upper = final_of(arrived, 1, partial, [lower_partial])
    upper_halo = upper_halo_of(upper)
    two, swapped, mate, fold = upper_halo
    near = own_terms(1, tabs, facts, [upper])
    result, _ = far_terms(1, 1, tabs, facts, [near, *upper_halo])

    lower = final_of(lower_arrived, 0, lower_partial, [mate, near])
    near = own_terms(0, tabs, facts, [lower], after=[fold])
    lower_halo = lower_halo_of(lower, near)
    arrays = [near, upper, mate, two, fold, *lower_halo]
    return far_terms(0, 1, tabs, facts, arrays, result)


def solution(mesh):
    in_specs = (
        P("ctx", None, None, "ch"),
        P("ch", None),
        P("ctx", None, None, "ch"),
        P(None, "ch"),
        P(),
    )
    out_specs = P("ctx", None, None, "ch")
    return jax.shard_map(
        on_device, mesh=mesh, in_specs=in_specs, out_specs=out_specs, check_vma=False
    )
```

```python
import functools
import math

import jax
import jax.numpy as jnp
import ml_dtypes
import numpy as np
from jax import lax
from jax.experimental import pallas as pl
from jax.experimental.pallas import tpu as pltpu
from jax.sharding import PartitionSpec as P

REACH = 3
LANES = 512
VMEM = 20 * 1024 * 1024
F32 = jnp.float32
BF16 = jnp.bfloat16
WHOLE = pl.BlockSpec(memory_space=pltpu.VMEM)
ANYWHERE = pl.BlockSpec(memory_space=pl.ANY)
OUTSIDE = pl.BlockSpec(memory_space=pltpu.HBM)
SCALARS = pl.BlockSpec(memory_space=pltpu.SMEM)


def parts_of(table):
    high = table.astype(np.float32).astype(ml_dtypes.bfloat16)
    low = (table - high.astype(np.float64)).astype(np.float32).astype(ml_dtypes.bfloat16)
    return high, low


@functools.lru_cache(maxsize=None)
def tables(length):
    angle = np.outer(2 * np.arange(length) + 1, np.arange(length)) % (4 * length)
    angle = angle.astype(np.float64) * (math.pi / (2 * length))
    forward = np.concatenate([np.cos(angle), -np.sin(angle)], axis=0)
    high, low = parts_of(forward)
    back_high, back_low = parts_of(forward.T / length)
    return np.concatenate([high, low], axis=1), np.concatenate([back_high, back_low], axis=0)


def nn(a, b):
    return lax.dot_general(a, b, (((1,), (0,)), ((), ())), preferred_element_type=F32)


def nt(a, b):
    return lax.dot_general(a, b, (((1,), (1,)), ((), ())), preferred_element_type=F32)


def params(limit=VMEM):
    return pltpu.CompilerParams(vmem_limit_bytes=limit)


def lanes_at(tile):
    return pl.ds(pl.multiple_of(tile * LANES, LANES), LANES)


def write_facts(facts_ref, slot, docs_ref, block, length, end, inner, role):
    start = block * length
    stop = start + length - 1

    def visit(at, found):
        first, following, last = found
        here = docs_ref[at]
        first = jnp.minimum(first, jnp.where(here > start, here, end))
        following = jnp.minimum(following, jnp.where(here > stop, here, end))
        last = jnp.maximum(last, jnp.where(here <= stop, here, 0))
        return first, following, last

    whole = jnp.int32(end)
    first, following, last = lax.fori_loop(
        0, docs_ref.shape[0], visit, (whole, whole, jnp.int32(0))
    )
    facts_ref[slot, 0] = jnp.clip(first - start, 0, length)
    facts_ref[slot, 1] = jnp.clip(last - start, 0, length)
    for distance in range(1, REACH + 1):
        facts_ref[slot, 1 + distance] = jnp.clip(following - start - distance * length, 0, length)
    facts_ref[slot, 2 + REACH] = inner
    facts_ref[slot, 3 + REACH] = role


def prepare_kernel(pairs, *refs):
    place_ref, lane_ref, docs_ref, table_ref, back_ref, taps_ref = refs[:6]
    weight_ref, gate_ref, grad_ref = refs[6:9]
    spec_out, weight_out, gate_out, lower_out, table_out, back_out = refs[9:15]
    facts_out, token_out, sems = refs[15:]
    token_out[...] = jnp.zeros_like(token_out)
    copies = [
        pltpu.make_async_copy(source, target, sems.at[at])
        for at, (source, target) in enumerate(
            [
                (grad_ref.at[0, 0], lower_out),
                (weight_ref, weight_out),
                (gate_ref, gate_out),
                (back_ref, back_out),
            ]
        )
    ]
    step = pl.program_id(0)
    length = table_ref.shape[1] // 2

    @pl.when(step == 0)
    def _():
        for copy in copies:
            copy.start()
        table_out[...] = table_ref[:, :length]
        place = place_ref[0]
        odd = lax.rem(place, 2)
        role = jnp.where(place >= pairs - 3, pairs - place, 0)
        end = 2 * pairs * length
        for slot in range(2):
            facts_out[slot, 4 + REACH] = lane_ref[0]
        write_facts(facts_out, 0, docs_ref, place, length, end, 1 - odd, role)
        write_facts(facts_out, 1, docs_ref, 2 * pairs - 1 - place, length, end, odd, role)

    freq = lax.broadcasted_iota(jnp.int32, (length, 1), 0)
    sign = jnp.where(freq % 2 == 0, 1.0, -1.0).astype(F32)
    lanes = lanes_at(step)
    before = None
    for part in range(REACH + 1):
        if part < REACH:
            values = taps_ref[part * length : (part + 1) * length, :]
            high = values.astype(BF16)
            low = (values - high.astype(F32)).astype(BF16)
            full = nn(table_ref[...], jnp.concatenate([high, high], axis=0))
            full = full + nn(table_ref[:, :length], low)
            now = (full[:length], -full[length:])
        else:
            now = None
        if before is None:
            real, imag = now
        else:
            real, imag = sign * before[1], -sign * before[0]
            if now is not None:
                real, imag = now[0] + real, now[1] + imag
        spec_out[part, :length, lanes] = real
        spec_out[part, length:, lanes] = imag
        before = now

    @pl.when(step == pl.num_programs(0) - 1)
    def _():
        for copy in copies:
            copy.wait()


def prepare(pairs, place, lane, docs, table, back, taps, weight, gate, grad):
    count, width = taps.shape
    length = count // REACH
    return pl.pallas_call(
        functools.partial(prepare_kernel, pairs),
        grid=(width // LANES,),
        out_shape=(
            pltpu.VMEM((REACH + 1, 2 * length, width), F32),
            pltpu.VMEM(weight.shape, BF16),
            pltpu.VMEM(gate.shape, BF16),
            pltpu.VMEM(grad.shape[2:], BF16),
            pltpu.VMEM((2 * length, length), BF16),
            pltpu.VMEM(back.shape, BF16),
            pltpu.SMEM((2, 8), jnp.int32),
            pltpu.VMEM((8, 128), F32),
        ),
        in_specs=[
            SCALARS,
            SCALARS,
            SCALARS,
            pl.BlockSpec((2 * length, 2 * length), lambda c: (0, 0)),
            OUTSIDE,
            pl.BlockSpec((count, LANES), lambda c: (0, c)),
            OUTSIDE,
            OUTSIDE,
            OUTSIDE,
        ],
        out_specs=(WHOLE,) * 6 + (SCALARS, WHOLE),
        scratch_shapes=[pltpu.SemaphoreType.DMA((4,))],
        compiler_params=params(2 * VMEM),
        cost_estimate=pl.CostEstimate(
            flops=2 * 3 * 2 * count * length * width,
            bytes_accessed=4 * (count * width + 8 * length * width),
            transcendentals=0,
        ),
    )(place, lane, docs, table, back, taps, weight, gate, grad)


def project_kernel(hops, slot, first, last, facts_ref, *refs):
    shards, refs = refs[: len(hops)], refs[len(hops) :]
    weight_ref, gate_ref = refs[:2]
    before_ref = None if first else refs[2]
    out_ref, acc_ref = refs[-2:] if last else (refs[-1], refs[-1])
    depth = shards[0].shape[1]
    count = weight_ref.shape[1] // depth
    tiles = [pl.ds(tile * LANES, LANES) for tile in range(weight_ref.shape[0] // LANES)]
    if not first:
        acc_ref[...] = before_ref[...]
    for shard, hop in zip(shards, hops):
        at = facts_ref[0, 4 + REACH] + hop
        features = pl.ds(pl.multiple_of(jnp.clip(at, 0, count - 1) * depth, depth), depth)

        def add(shard=shard, hop=hop, features=features):
            for lanes in tiles:
                part = nt(shard[...], weight_ref[lanes, features])
                if hop == 0:
                    acc_ref[:, lanes] = part
                else:
                    acc_ref[:, lanes] += part

        if hop == 0:
            add()
        else:
            pl.when((at >= 0) & (at < count))(add)
    if last:
        out_ref[...] = (acc_ref[...] * gate_ref[0, slot].astype(F32)).astype(BF16)


def project(facts, shards, hops, weight, gate, slot, before=None, last=True, after=()):
    rows, depth = shards[0].shape
    width = weight.shape[0]
    operands = [facts, *shards, weight, gate]
    if before is not None:
        operands.append(before)
    return pl.pallas_call(
        functools.partial(project_kernel, hops, slot, before is None, last),
        out_shape=pltpu.VMEM((rows, width), BF16 if last else F32),
        in_specs=[SCALARS] + [WHOLE] * (len(operands) - 1) + [ANYWHERE] * len(after),
        out_specs=WHOLE,
        scratch_shapes=[pltpu.VMEM((rows, width), F32)] if last else [],
        compiler_params=params(),
        cost_estimate=pl.CostEstimate(
            flops=2 * rows * depth * (len(shards) + 1) // 2 * width,
            bytes_accessed=2 * (rows + width) * depth * len(shards),
            transcendentals=0,
        ),
    )(*operands, *after)


class Conv:
    def __init__(self, slot, facts, table, back, spectra):
        self.facts = [facts[slot, at] for at in range(4 + REACH)]
        self.table, self.back, self.spectra = table, back, spectra
        self.length = table.shape[0] // 2
        self.lanes = lanes_at(pl.program_id(0))
        self.row = lax.broadcasted_iota(jnp.int32, (self.length, LANES), 0)

    def joined(self, pieces):
        tiles = [piece[:, self.lanes] for piece in pieces]
        return tiles[0] if len(tiles) == 1 else jnp.concatenate(tiles, axis=0)

    def within(self, low, high):
        return (self.row >= low) & (self.row < high)

    def term(self, values, low, high, distance):
        length = self.length
        kept = jnp.where(self.within(low, high), values.astype(F32), 0.0).astype(BF16)
        full = nn(self.table[...], kept)
        real, imag = full[:length], full[length:]
        k_real = self.spectra[distance, :length, self.lanes]
        k_imag = self.spectra[distance, length:, self.lanes]
        return k_real * real - k_imag * imag, k_real * imag + k_imag * real

    def signal(self, real, imag):
        total = jnp.concatenate([real.astype(BF16), imag.astype(BF16)], axis=0)
        both = nn(self.back[...], total)
        return both[: self.length] + both[self.length :]

    def far_terms(self, acc, chosen, choices):
        for distance in range(1, REACH + 1):
            reach = self.facts[1 + distance]

            @pl.when(reach > 0)
            def _(distance=distance, reach=reach):
                for pieces, holds in choices(distance):

                    @pl.when(holds)
                    def _(pieces=pieces):
                        chosen[...] = self.joined(pieces)

                real, imag = self.term(chosen[...], 0, reach, distance)
                acc[: self.length, :] += real
                acc[self.length :, :] += imag

    def inner_documents(self, own, read, write):
        first_end, last_start = self.facts[0], self.facts[1]

        @pl.when(last_start > 0)
        def _():
            signal = self.signal(*self.term(own, 0, first_end, 0))
            write(jnp.where(self.row < first_end, signal, read()))

        @pl.when(last_start > first_end)
        def _():
            signal = self.signal(*self.term(own, first_end, last_start, 0))
            write(jnp.where(self.within(first_end, last_start), signal, read()))

    def halo(self, pieces, distance, mixed):
        sets = 3 if mixed else 4
        count = len(pieces) // sets
        kinds = [pieces[at * count : (at + 1) * count] for at in range(sets)]
        two, swapped, mate, far = kinds[0], kinds[1], kinds[2], kinds[-1]
        inner = self.facts[5]
        if distance == 2:
            return [(two, inner >= 0)]
        if distance == 1:
            return [(mate, inner == 1), (swapped, inner == 0)]
        return [(swapped, inner == 1), (far, inner == 0)]


def own_kernel(slot, pieces, facts_ref, table_ref, back_ref, spec_ref, *refs):
    own_refs, out_ref = refs[:pieces], refs[-1]
    conv = Conv(slot, facts_ref, table_ref, back_ref, spec_ref)
    own = conv.joined(own_refs)
    out_ref[:, conv.lanes] = conv.signal(*conv.term(own, conv.facts[1], conv.length, 0))

    def write(value):
        out_ref[:, conv.lanes] = value

    conv.inner_documents(own, lambda: out_ref[:, conv.lanes], write)


def far_kernel(slot, pieces, facts_ref, table_ref, back_ref, spec_ref, *refs):
    near_ref, refs = refs[0], refs[1:]
    if slot == 0:
        upper_ref, mate_ref, two_ref, fold_ref = refs[:4]
        halos = refs[4 : 4 + 3 * pieces]
    else:
        halos = refs[: 4 * pieces]
    out_ref, acc_ref, chosen_ref = refs[-3:]
    if slot == 1:
        out_ref, token_ref = refs[-4:-2]
        token_ref[...] = jnp.zeros_like(token_ref)
    conv = Conv(slot, facts_ref, table_ref, back_ref, spec_ref)
    role = conv.facts[6]

    def choices(distance):
        found = conv.halo(halos, distance, slot == 0)
        if slot == 0:
            folded = {
                1: [([upper_ref], role == 1)],
                2: [([mate_ref], (role == 1) | (role == 2))],
                3: [([two_ref], role == 1), ([upper_ref], role == 2), ([fold_ref], role == 3)],
            }
            found = found + folded[distance]
        return found

    reaches = conv.facts[2] > 0

    @pl.when(reaches)
    def _():
        acc_ref[...] = jnp.zeros_like(acc_ref)
        conv.far_terms(acc_ref, chosen_ref, choices)
        signal = conv.signal(acc_ref[: conv.length, :], acc_ref[conv.length :, :])
        kept = jnp.where(conv.row >= conv.facts[1], signal, 0.0)
        out_ref[0, 0] = near_ref[:, conv.lanes] + kept

    @pl.when(jnp.logical_not(reaches))
    def _():
        out_ref[0, 0] = near_ref[:, conv.lanes]


def conv_call(body, tabs, facts, arrays, out_shape, out_spec, scratch, after=(), result=None):
    table, back, spectra = tabs
    length = table.shape[0] // 2
    width = spectra.shape[2]
    operands = [facts, table, back, spectra, *arrays]
    specs = [SCALARS] + [WHOLE] * (len(operands) - 1) + [ANYWHERE] * len(after)
    operands.extend(after)
    aliases = {}
    if result is not None:
        aliases = {len(operands): 0}
        operands.append(result)
        specs.append(ANYWHERE)
    return pl.pallas_call(
        body,
        grid=(width // LANES,),
        out_shape=out_shape,
        in_specs=specs,
        out_specs=out_spec,
        scratch_shapes=scratch,
        input_output_aliases=aliases,
        compiler_params=params(),
        cost_estimate=pl.CostEstimate(
            flops=32 * length * length * width,
            bytes_accessed=4 * length * width,
            transcendentals=0,
        ),
    )(*operands)


def own_terms(slot, tabs, facts, pieces, after=()):
    _, back, spectra = tabs
    shape = pltpu.VMEM((back.shape[0] // 2, spectra.shape[2]), F32)
    body = functools.partial(own_kernel, slot, len(pieces))
    return conv_call(body, tabs, facts, pieces, shape, WHOLE, [], after)


def far_terms(slot, count, tabs, facts, arrays, result=None):
    _, back, spectra = tabs
    length, width = back.shape[0] // 2, spectra.shape[2]
    shape = jax.ShapeDtypeStruct((1, 2, length, width), F32)
    spec = pl.BlockSpec((1, 1, length, LANES), lambda c: (0, slot, 0, c))
    scratch = [pltpu.VMEM((2 * length, LANES), F32), pltpu.VMEM((length, LANES), BF16)]
    body = functools.partial(far_kernel, slot, count)
    if slot == 1:
        shape, spec = (shape, pltpu.VMEM((8, 128), F32)), (spec, WHOLE)
    return conv_call(body, tabs, facts, arrays, shape, spec, scratch, (), result)


def together(values, *earlier):
    return pl.pallas_call(
        lambda *refs: None,
        out_shape=[jax.ShapeDtypeStruct(one.shape, one.dtype) for one in values],
        in_specs=[ANYWHERE] * (len(values) + len(earlier)),
        out_specs=[ANYWHERE] * len(values),
        input_output_aliases={at: at for at in range(len(values))},
        compiler_params=params(VMEM // 20),
    )(*values, *earlier)


def ordered(value, *earlier):
    return together([value], *earlier)[0]


def shifted(value, steps):
    count = lax.axis_size("ctx")
    initial, last = (max(0, -steps), min(count, count - steps))
    return lax.ppermute(value, "ctx", [(source, source + steps) for source in range(initial, last)])


def core_swapped(value):
    count = lax.axis_size("ctx")
    return lax.ppermute(value, "ctx", [(source, source ^ 1) for source in range(count)])


def upper_halo_of(value):
    count = lax.axis_size("ctx")
    far = [(source, source + 3) for source in range(1, count - 3, 2)] + [(count - 1, count - 3)]
    two = shifted(value, 2)
    mate, far = core_swapped(value), lax.ppermute(value, "ctx", far)
    return [two, core_swapped(two), mate, far]


def lower_halo_of(value, own):
    count = lax.axis_size("ctx")
    mixed = [(source, source - 1) for source in range(1, count, 2)]
    mixed += [(source, source - 3) for source in range(4, count, 2)]
    two = ordered(shifted(value, -2), own)
    mixed = lax.ppermute(value, "ctx", mixed)
    return [two, core_swapped(two), mixed]


def on_device(grad_out, out_weight, gate, filter_taps, doc_starts):
    pairs = lax.axis_size("ctx")
    place = lax.axis_index("ctx")
    length = grad_out.shape[2]
    width = out_weight.shape[0]
    count = lax.axis_size("ch")
    lane = lax.axis_index("ch").astype(jnp.int32)[None]

    def sent(step, up, down):
        upward = [(source, source + 1) for source in range(step - 1, count - 1)]
        downward = [(source, source - 1) for source in range(1, count - step + 1)]
        return lax.ppermute(up, "ch", upward), lax.ppermute(down, "ch", downward)

    start = grad_out[0, 1]
    upper_in = [sent(1, start, start)]

    table, back = (jnp.asarray(one) for one in tables(length))
    spectra, weight, gates, lower_slice, table, back, facts, prepared = prepare(
        pairs,
        place.astype(jnp.int32)[None],
        lane,
        doc_starts,
        table,
        back,
        filter_taps,
        out_weight,
        gate,
        grad_out,
    )
    tabs = (table, back, spectra)

    def pass_on(chain, *earlier):
        if earlier:
            chain[-1] = together(chain[-1], *earlier)
        chain.append(sent(len(chain) + 1, *chain[-1]))

    hops = [0] + [way * step for step in range(1, count) for way in (-1, 1)]

    def partial_of(own, arrived, slot, after=()):
        shards = [own] + [one for pair in arrived[: count - 2] for one in pair]
        return project(
            facts, shards, hops[:-2], weight, gates, slot, last=False, after=after
        )

    def final_of(arrived, slot, partial, after=()):
        return project(facts, arrived[-1], hops[-2:], weight, gates, slot, partial, after=after)

    pass_on(upper_in, prepared)
    own = ordered(lower_slice, *upper_in[0])
    lower_in = [sent(1, own, own)]
    for _ in range(3, count):
        pass_on(upper_in)
        pass_on(lower_in, *upper_in[-2])
    partial = partial_of(start, upper_in, 1)
    upper = final_of(upper_in, 1, partial)
    upper_halo = upper_halo_of(upper)
    two, swapped, mate, fold = upper_halo
    near = own_terms(1, tabs, facts, [upper])
    pass_on(lower_in, upper, mate)
    result, _ = far_terms(1, 1, tabs, facts, [near, *upper_halo])

    partial = partial_of(own, lower_in, 0, [near])
    lower = final_of(lower_in, 0, partial, [two])
    near = own_terms(0, tabs, facts, [lower], after=[fold])
    lower_halo = lower_halo_of(lower, near)
    arrays = [near, upper, mate, two, fold, *lower_halo]
    return far_terms(0, 1, tabs, facts, arrays, result)


def solution(mesh):
    in_specs = (
        P("ctx", None, None, "ch"),
        P("ch", None),
        P("ctx", None, None, "ch"),
        P(None, "ch"),
        P(),
    )
    out_specs = P("ctx", None, None, "ch")
    return jax.shard_map(
        on_device, mesh=mesh, in_specs=in_specs, out_specs=out_specs, check_vma=False
    )
```

```python
import functools
import math

import jax
import jax.numpy as jnp
import ml_dtypes
import numpy as np
from jax import lax
from jax.experimental import pallas as pl
from jax.experimental.pallas import tpu as pltpu
from jax.sharding import PartitionSpec as P

REACH = 3
LANES = 512
VMEM = 20 * 1024 * 1024
F32 = jnp.float32
BF16 = jnp.bfloat16
WHOLE = pl.BlockSpec(memory_space=pltpu.VMEM)
ANYWHERE = pl.BlockSpec(memory_space=pl.ANY)
OUTSIDE = pl.BlockSpec(memory_space=pltpu.HBM)
SCALARS = pl.BlockSpec(memory_space=pltpu.SMEM)


def parts_of(table):
    high = table.astype(np.float32).astype(ml_dtypes.bfloat16)
    low = (table - high.astype(np.float64)).astype(np.float32).astype(ml_dtypes.bfloat16)
    return high, low


@functools.lru_cache(maxsize=None)
def tables(length):
    angle = np.outer(2 * np.arange(length) + 1, np.arange(length)) % (4 * length)
    angle = angle.astype(np.float64) * (math.pi / (2 * length))
    forward = np.concatenate([np.cos(angle), -np.sin(angle)], axis=0)
    high, low = parts_of(forward)
    back_high, back_low = parts_of(forward.T / length)
    return np.concatenate([high, low], axis=1), np.concatenate([back_high, back_low], axis=0)


def nn(a, b):
    return lax.dot_general(a, b, (((1,), (0,)), ((), ())), preferred_element_type=F32)


def nt(a, b):
    return lax.dot_general(a, b, (((1,), (1,)), ((), ())), preferred_element_type=F32)


def params(limit=VMEM):
    return pltpu.CompilerParams(vmem_limit_bytes=limit)


def lanes_at(tile):
    return pl.ds(pl.multiple_of(tile * LANES, LANES), LANES)


def write_facts(facts_ref, slot, docs_ref, block, length, end, inner, role):
    start = block * length
    stop = start + length - 1

    def visit(at, found):
        first, following, last = found
        here = docs_ref[at]
        first = jnp.minimum(first, jnp.where(here > start, here, end))
        following = jnp.minimum(following, jnp.where(here > stop, here, end))
        last = jnp.maximum(last, jnp.where(here <= stop, here, 0))
        return first, following, last

    whole = jnp.int32(end)
    first, following, last = lax.fori_loop(
        0, docs_ref.shape[0], visit, (whole, whole, jnp.int32(0))
    )
    facts_ref[slot, 0] = jnp.clip(first - start, 0, length)
    facts_ref[slot, 1] = jnp.clip(last - start, 0, length)
    for distance in range(1, REACH + 1):
        facts_ref[slot, 1 + distance] = jnp.clip(following - start - distance * length, 0, length)
    facts_ref[slot, 2 + REACH] = inner
    facts_ref[slot, 3 + REACH] = role


def prepare_kernel(pairs, *refs):
    place_ref, lane_ref, docs_ref, table_ref, back_ref, taps_ref = refs[:6]
    weight_ref, gate_ref, grad_ref = refs[6:9]
    spec_out, weight_out, gate_out, lower_out, table_out, back_out = refs[9:15]
    facts_out, token_out, sems = refs[15:]
    token_out[...] = jnp.zeros_like(token_out)
    copies = [
        pltpu.make_async_copy(source, target, sems.at[at])
        for at, (source, target) in enumerate(
            [
                (grad_ref.at[0, 0], lower_out),
                (weight_ref, weight_out),
                (gate_ref, gate_out),
                (back_ref, back_out),
            ]
        )
    ]
    step = pl.program_id(0)
    length = table_ref.shape[1] // 2

    @pl.when(step == 0)
    def _():
        for copy in copies:
            copy.start()
        table_out[...] = table_ref[:, :length]
        place = place_ref[0]
        odd = lax.rem(place, 2)
        role = jnp.where(place >= pairs - 3, pairs - place, 0)
        end = 2 * pairs * length
        for slot in range(2):
            facts_out[slot, 4 + REACH] = lane_ref[0]
        write_facts(facts_out, 0, docs_ref, place, length, end, 1 - odd, role)
        write_facts(facts_out, 1, docs_ref, 2 * pairs - 1 - place, length, end, odd, role)

    freq = lax.broadcasted_iota(jnp.int32, (length, 1), 0)
    sign = jnp.where(freq % 2 == 0, 1.0, -1.0).astype(F32)
    lanes = lanes_at(step)
    before = None
    for part in range(REACH + 1):
        if part < REACH:
            values = taps_ref[part * length : (part + 1) * length, :]
            high = values.astype(BF16)
            low = (values - high.astype(F32)).astype(BF16)
            full = nn(table_ref[...], jnp.concatenate([high, high], axis=0))
            full = full + nn(table_ref[:, :length], low)
            now = (full[:length], -full[length:])
        else:
            now = None
        if before is None:
            real, imag = now
        else:
            real, imag = sign * before[1], -sign * before[0]
            if now is not None:
                real, imag = now[0] + real, now[1] + imag
        spec_out[part, :length, lanes] = real
        spec_out[part, length:, lanes] = imag
        before = now

    @pl.when(step == pl.num_programs(0) - 1)
    def _():
        for copy in copies:
            copy.wait()


def prepare(pairs, place, lane, docs, table, back, taps, weight, gate, grad):
    count, width = taps.shape
    length = count // REACH
    return pl.pallas_call(
        functools.partial(prepare_kernel, pairs),
        grid=(width // LANES,),
        out_shape=(
            pltpu.VMEM((REACH + 1, 2 * length, width), F32),
            pltpu.VMEM(weight.shape, BF16),
            pltpu.VMEM(gate.shape, BF16),
            pltpu.VMEM(grad.shape[2:], BF16),
            pltpu.VMEM((2 * length, length), BF16),
            pltpu.VMEM(back.shape, BF16),
            pltpu.SMEM((2, 8), jnp.int32),
            pltpu.VMEM((8, 128), F32),
        ),
        in_specs=[
            SCALARS,
            SCALARS,
            SCALARS,
            pl.BlockSpec((2 * length, 2 * length), lambda c: (0, 0)),
            OUTSIDE,
            pl.BlockSpec((count, LANES), lambda c: (0, c)),
            OUTSIDE,
            OUTSIDE,
            OUTSIDE,
        ],
        out_specs=(WHOLE,) * 6 + (SCALARS, WHOLE),
        scratch_shapes=[pltpu.SemaphoreType.DMA((4,))],
        compiler_params=params(2 * VMEM),
        cost_estimate=pl.CostEstimate(
            flops=2 * 3 * 2 * count * length * width,
            bytes_accessed=4 * (count * width + 8 * length * width),
            transcendentals=0,
        ),
    )(place, lane, docs, table, back, taps, weight, gate, grad)


def project_kernel(hops, slot, first, last, facts_ref, *refs):
    shards, refs = refs[: len(hops)], refs[len(hops) :]
    weight_ref, gate_ref = refs[:2]
    before_ref = None if first else refs[2]
    out_ref, acc_ref = refs[-2:] if last else (refs[-1], refs[-1])
    depth = shards[0].shape[1]
    count = weight_ref.shape[1] // depth
    tiles = [pl.ds(tile * LANES, LANES) for tile in range(weight_ref.shape[0] // LANES)]
    if not first:
        acc_ref[...] = before_ref[...]
    for shard, hop in zip(shards, hops):
        at = facts_ref[0, 4 + REACH] + hop
        features = pl.ds(pl.multiple_of(jnp.clip(at, 0, count - 1) * depth, depth), depth)

        def add(shard=shard, hop=hop, features=features):
            for lanes in tiles:
                part = nt(shard[...], weight_ref[lanes, features])
                if hop == 0:
                    acc_ref[:, lanes] = part
                else:
                    acc_ref[:, lanes] += part

        if hop == 0:
            add()
        else:
            pl.when((at >= 0) & (at < count))(add)
    if last:
        out_ref[...] = (acc_ref[...] * gate_ref[0, slot].astype(F32)).astype(BF16)


def project(facts, shards, hops, weight, gate, slot, before=None, last=True, after=()):
    rows, depth = shards[0].shape
    width = weight.shape[0]
    operands = [facts, *shards, weight, gate]
    if before is not None:
        operands.append(before)
    return pl.pallas_call(
        functools.partial(project_kernel, hops, slot, before is None, last),
        out_shape=pltpu.VMEM((rows, width), BF16 if last else F32),
        in_specs=[SCALARS] + [WHOLE] * (len(operands) - 1) + [ANYWHERE] * len(after),
        out_specs=WHOLE,
        scratch_shapes=[pltpu.VMEM((rows, width), F32)] if last else [],
        compiler_params=params(),
        cost_estimate=pl.CostEstimate(
            flops=2 * rows * depth * (len(shards) + 1) // 2 * width,
            bytes_accessed=2 * (rows + width) * depth * len(shards),
            transcendentals=0,
        ),
    )(*operands, *after)


class Conv:
    def __init__(self, slot, facts, table, back, spectra):
        self.facts = [facts[slot, at] for at in range(4 + REACH)]
        self.table, self.back, self.spectra = table, back, spectra
        self.length = table.shape[0] // 2
        self.lanes = lanes_at(pl.program_id(0))
        self.row = lax.broadcasted_iota(jnp.int32, (self.length, LANES), 0)

    def joined(self, pieces):
        tiles = [piece[:, self.lanes] for piece in pieces]
        return tiles[0] if len(tiles) == 1 else jnp.concatenate(tiles, axis=0)

    def within(self, low, high):
        return (self.row >= low) & (self.row < high)

    def term(self, values, low, high, distance):
        length = self.length
        kept = jnp.where(self.within(low, high), values.astype(F32), 0.0).astype(BF16)
        full = nn(self.table[...], kept)
        real, imag = full[:length], full[length:]
        k_real = self.spectra[distance, :length, self.lanes]
        k_imag = self.spectra[distance, length:, self.lanes]
        return k_real * real - k_imag * imag, k_real * imag + k_imag * real

    def signal(self, real, imag):
        total = jnp.concatenate([real.astype(BF16), imag.astype(BF16)], axis=0)
        both = nn(self.back[...], total)
        return both[: self.length] + both[self.length :]

    def far_terms(self, acc, chosen, choices):
        for distance in range(1, REACH + 1):
            reach = self.facts[1 + distance]

            @pl.when(reach > 0)
            def _(distance=distance, reach=reach):
                for pieces, holds in choices(distance):

                    @pl.when(holds)
                    def _(pieces=pieces):
                        chosen[...] = self.joined(pieces)

                real, imag = self.term(chosen[...], 0, reach, distance)
                acc[: self.length, :] += real
                acc[self.length :, :] += imag

    def inner_documents(self, own, read, write):
        first_end, last_start = self.facts[0], self.facts[1]

        @pl.when(last_start > 0)
        def _():
            signal = self.signal(*self.term(own, 0, first_end, 0))
            write(jnp.where(self.row < first_end, signal, read()))

        @pl.when(last_start > first_end)
        def _():
            signal = self.signal(*self.term(own, first_end, last_start, 0))
            write(jnp.where(self.within(first_end, last_start), signal, read()))

    def halo(self, pieces, distance, mixed):
        sets = 3 if mixed else 4
        count = len(pieces) // sets
        kinds = [pieces[at * count : (at + 1) * count] for at in range(sets)]
        two, swapped, mate, far = kinds[0], kinds[1], kinds[2], kinds[-1]
        inner = self.facts[5]
        if distance == 2:
            return [(two, inner >= 0)]
        if distance == 1:
            return [(mate, inner == 1), (swapped, inner == 0)]
        return [(swapped, inner == 1), (far, inner == 0)]


def own_kernel(slot, pieces, facts_ref, table_ref, back_ref, spec_ref, *refs):
    own_refs, out_ref = refs[:pieces], refs[-1]
    conv = Conv(slot, facts_ref, table_ref, back_ref, spec_ref)
    own = conv.joined(own_refs)
    out_ref[:, conv.lanes] = conv.signal(*conv.term(own, conv.facts[1], conv.length, 0))

    def write(value):
        out_ref[:, conv.lanes] = value

    conv.inner_documents(own, lambda: out_ref[:, conv.lanes], write)


def far_kernel(slot, pieces, facts_ref, table_ref, back_ref, spec_ref, *refs):
    near_ref, refs = refs[0], refs[1:]
    if slot == 0:
        upper_ref, mate_ref, two_ref, fold_ref = refs[:4]
        halos = refs[4 : 4 + 3 * pieces]
    else:
        halos = refs[: 4 * pieces]
    out_ref, acc_ref, chosen_ref = refs[-3:]
    if slot == 1:
        out_ref, token_ref = refs[-4:-2]
        token_ref[...] = jnp.zeros_like(token_ref)
    conv = Conv(slot, facts_ref, table_ref, back_ref, spec_ref)
    role = conv.facts[6]

    def choices(distance):
        found = conv.halo(halos, distance, slot == 0)
        if slot == 0:
            folded = {
                1: [([upper_ref], role == 1)],
                2: [([mate_ref], (role == 1) | (role == 2))],
                3: [([two_ref], role == 1), ([upper_ref], role == 2), ([fold_ref], role == 3)],
            }
            found = found + folded[distance]
        return found

    reaches = conv.facts[2] > 0

    @pl.when(reaches)
    def _():
        acc_ref[...] = jnp.zeros_like(acc_ref)
        conv.far_terms(acc_ref, chosen_ref, choices)
        signal = conv.signal(acc_ref[: conv.length, :], acc_ref[conv.length :, :])
        kept = jnp.where(conv.row >= conv.facts[1], signal, 0.0)
        out_ref[0, 0] = near_ref[:, conv.lanes] + kept

    @pl.when(jnp.logical_not(reaches))
    def _():
        out_ref[0, 0] = near_ref[:, conv.lanes]


def conv_call(body, tabs, facts, arrays, out_shape, out_spec, scratch, after=(), result=None):
    table, back, spectra = tabs
    length = table.shape[0] // 2
    width = spectra.shape[2]
    operands = [facts, table, back, spectra, *arrays]
    specs = [SCALARS] + [WHOLE] * (len(operands) - 1) + [ANYWHERE] * len(after)
    operands.extend(after)
    aliases = {}
    if result is not None:
        aliases = {len(operands): 0}
        operands.append(result)
        specs.append(ANYWHERE)
    return pl.pallas_call(
        body,
        grid=(width // LANES,),
        out_shape=out_shape,
        in_specs=specs,
        out_specs=out_spec,
        scratch_shapes=scratch,
        input_output_aliases=aliases,
        compiler_params=params(),
        cost_estimate=pl.CostEstimate(
            flops=32 * length * length * width,
            bytes_accessed=4 * length * width,
            transcendentals=0,
        ),
    )(*operands)


def own_terms(slot, tabs, facts, pieces, after=()):
    _, back, spectra = tabs
    shape = pltpu.VMEM((back.shape[0] // 2, spectra.shape[2]), F32)
    body = functools.partial(own_kernel, slot, len(pieces))
    return conv_call(body, tabs, facts, pieces, shape, WHOLE, [], after)


def far_terms(slot, count, tabs, facts, arrays, result=None):
    _, back, spectra = tabs
    length, width = back.shape[0] // 2, spectra.shape[2]
    shape = jax.ShapeDtypeStruct((1, 2, length, width), F32)
    spec = pl.BlockSpec((1, 1, length, LANES), lambda c: (0, slot, 0, c))
    scratch = [pltpu.VMEM((2 * length, LANES), F32), pltpu.VMEM((length, LANES), BF16)]
    body = functools.partial(far_kernel, slot, count)
    if slot == 1:
        shape, spec = (shape, pltpu.VMEM((8, 128), F32)), (spec, WHOLE)
    return conv_call(body, tabs, facts, arrays, shape, spec, scratch, (), result)


def together(values, *earlier):
    return pl.pallas_call(
        lambda *refs: None,
        out_shape=[jax.ShapeDtypeStruct(one.shape, one.dtype) for one in values],
        in_specs=[ANYWHERE] * (len(values) + len(earlier)),
        out_specs=[ANYWHERE] * len(values),
        input_output_aliases={at: at for at in range(len(values))},
        compiler_params=params(VMEM // 20),
    )(*values, *earlier)


def ordered(value, *earlier):
    return together([value], *earlier)[0]


def shifted(value, steps):
    count = lax.axis_size("ctx")
    initial, last = (max(0, -steps), min(count, count - steps))
    return lax.ppermute(value, "ctx", [(source, source + steps) for source in range(initial, last)])


def core_swapped(value):
    count = lax.axis_size("ctx")
    return lax.ppermute(value, "ctx", [(source, source ^ 1) for source in range(count)])


def upper_halo_of(value):
    count = lax.axis_size("ctx")
    far = [(source, source + 3) for source in range(1, count - 3, 2)] + [(count - 1, count - 3)]
    two = shifted(value, 2)
    mate, far = core_swapped(value), lax.ppermute(value, "ctx", far)
    return [two, core_swapped(two), mate, far]


def lower_halo_of(value, *own):
    count = lax.axis_size("ctx")
    mixed = [(source, source - 1) for source in range(1, count, 2)]
    mixed += [(source, source - 3) for source in range(4, count, 2)]
    two = ordered(shifted(value, -2), *own)
    mixed = lax.ppermute(value, "ctx", mixed)
    return [two, core_swapped(two), mixed]


def on_device(grad_out, out_weight, gate, filter_taps, doc_starts):
    pairs = lax.axis_size("ctx")
    place = lax.axis_index("ctx")
    length = grad_out.shape[2]
    width = out_weight.shape[0]
    count = lax.axis_size("ch")
    lane = lax.axis_index("ch").astype(jnp.int32)[None]

    def sent(step, up, down):
        upward = [(source, source + 1) for source in range(step - 1, count - 1)]
        downward = [(source, source - 1) for source in range(1, count - step + 1)]
        return lax.ppermute(up, "ch", upward), lax.ppermute(down, "ch", downward)

    start = grad_out[0, 1]
    upper_in = [sent(1, start, start)]

    table, back = (jnp.asarray(one) for one in tables(length))
    spectra, weight, gates, lower_slice, table, back, facts, prepared = prepare(
        pairs,
        place.astype(jnp.int32)[None],
        lane,
        doc_starts,
        table,
        back,
        filter_taps,
        out_weight,
        gate,
        grad_out,
    )
    tabs = (table, back, spectra)

    def pass_on(chain, *earlier):
        if earlier:
            chain[-1] = together(chain[-1], *earlier)
        chain.append(sent(len(chain) + 1, *chain[-1]))

    hops = [0] + [way * step for step in range(1, count) for way in (-1, 1)]

    def partial_of(own, arrived, slot, after=()):
        shards = [own] + [one for pair in arrived[: count - 2] for one in pair]
        return project(
            facts, shards, hops[:-2], weight, gates, slot, last=False, after=after
        )

    def final_of(arrived, slot, partial, after=()):
        return project(facts, arrived[-1], hops[-2:], weight, gates, slot, partial, after=after)

    pass_on(upper_in, prepared)
    own = ordered(lower_slice, *upper_in[0])
    lower_in = [sent(1, own, own)]
    for _ in range(3, count):
        pass_on(upper_in)
        pass_on(lower_in, *upper_in[-2])
    partial = partial_of(start, upper_in, 1)
    upper = final_of(upper_in, 1, partial)
    upper_halo = upper_halo_of(upper)
    two, swapped, mate, fold = upper_halo
    pass_on(lower_in, upper, mate)

    partial = partial_of(own, lower_in, 0)
    lower = final_of(lower_in, 0, partial, [two])
    upper_near = own_terms(1, tabs, facts, [upper], after=[lower])
    result, _ = far_terms(1, 1, tabs, facts, [upper_near, *upper_halo])
    near = own_terms(0, tabs, facts, [lower], after=[fold])
    lower_halo = lower_halo_of(lower, near, upper_near)
    arrays = [near, upper, mate, two, fold, *lower_halo]
    return far_terms(0, 1, tabs, facts, arrays, result)


def solution(mesh):
    in_specs = (
        P("ctx", None, None, "ch"),
        P("ch", None),
        P("ctx", None, None, "ch"),
        P(None, "ch"),
        P(),
    )
    out_specs = P("ctx", None, None, "ch")
    return jax.shard_map(
        on_device, mesh=mesh, in_specs=in_specs, out_specs=out_specs, check_vma=False
    )
```

```python
import functools
import math

import jax
import jax.numpy as jnp
import ml_dtypes
import numpy as np
from jax import lax
from jax.experimental import pallas as pl
from jax.experimental.pallas import tpu as pltpu
from jax.sharding import PartitionSpec as P

REACH = 3
LANES = 1024
VMEM = 20 * 1024 * 1024
F32 = jnp.float32
BF16 = jnp.bfloat16
WHOLE = pl.BlockSpec(memory_space=pltpu.VMEM)
ANYWHERE = pl.BlockSpec(memory_space=pl.ANY)
OUTSIDE = pl.BlockSpec(memory_space=pltpu.HBM)
SCALARS = pl.BlockSpec(memory_space=pltpu.SMEM)


def parts_of(table):
    high = table.astype(np.float32).astype(ml_dtypes.bfloat16)
    low = (table - high.astype(np.float64)).astype(np.float32).astype(ml_dtypes.bfloat16)
    return high, low


@functools.lru_cache(maxsize=None)
def tables(length):
    angle = np.outer(2 * np.arange(length) + 1, np.arange(length)) % (4 * length)
    angle = angle.astype(np.float64) * (math.pi / (2 * length))
    forward = np.concatenate([np.cos(angle), -np.sin(angle)], axis=0)
    high, low = parts_of(forward)
    back_high, back_low = parts_of(forward.T / length)
    return np.concatenate([high, low], axis=1), np.concatenate([back_high, back_low], axis=0)


def nn(a, b):
    return lax.dot_general(a, b, (((1,), (0,)), ((), ())), preferred_element_type=F32)


def nt(a, b):
    return lax.dot_general(a, b, (((1,), (1,)), ((), ())), preferred_element_type=F32)


def params(limit=VMEM):
    return pltpu.CompilerParams(vmem_limit_bytes=limit)


def lanes_at(tile):
    return pl.ds(pl.multiple_of(tile * LANES, LANES), LANES)


def write_facts(facts_ref, slot, docs_ref, block, length, end, inner, role):
    start = block * length
    stop = start + length - 1

    def visit(at, found):
        first, following, last = found
        here = docs_ref[at]
        first = jnp.minimum(first, jnp.where(here > start, here, end))
        following = jnp.minimum(following, jnp.where(here > stop, here, end))
        last = jnp.maximum(last, jnp.where(here <= stop, here, 0))
        return first, following, last

    whole = jnp.int32(end)
    first, following, last = lax.fori_loop(
        0, docs_ref.shape[0], visit, (whole, whole, jnp.int32(0))
    )
    facts_ref[slot, 0] = jnp.clip(first - start, 0, length)
    facts_ref[slot, 1] = jnp.clip(last - start, 0, length)
    for distance in range(1, REACH + 1):
        facts_ref[slot, 1 + distance] = jnp.clip(following - start - distance * length, 0, length)
    facts_ref[slot, 2 + REACH] = inner
    facts_ref[slot, 3 + REACH] = role


def prepare_kernel(pairs, *refs):
    place_ref, lane_ref, docs_ref, table_ref, back_ref, taps_ref = refs[:6]
    weight_ref, gate_ref, grad_ref = refs[6:9]
    spec_out, weight_out, gate_out, lower_out, table_out, back_out = refs[9:15]
    facts_out, token_out, sems = refs[15:]
    token_out[...] = jnp.zeros_like(token_out)
    copies = [
        pltpu.make_async_copy(source, target, sems.at[at])
        for at, (source, target) in enumerate(
            [
                (grad_ref.at[0, 0], lower_out),
                (weight_ref, weight_out),
                (gate_ref, gate_out),
                (back_ref, back_out),
            ]
        )
    ]
    step = pl.program_id(0)
    length = table_ref.shape[1] // 2

    @pl.when(step == 0)
    def _():
        for copy in copies:
            copy.start()
        table_out[...] = table_ref[:, :length]
        place = place_ref[0]
        odd = lax.rem(place, 2)
        role = jnp.where(place >= pairs - 3, pairs - place, 0)
        end = 2 * pairs * length
        for slot in range(2):
            facts_out[slot, 4 + REACH] = lane_ref[0]
        write_facts(facts_out, 0, docs_ref, place, length, end, 1 - odd, role)
        write_facts(facts_out, 1, docs_ref, 2 * pairs - 1 - place, length, end, odd, role)

    freq = lax.broadcasted_iota(jnp.int32, (length, 1), 0)
    sign = jnp.where(freq % 2 == 0, 1.0, -1.0).astype(F32)
    lanes = lanes_at(step)
    before = None
    for part in range(REACH + 1):
        if part < REACH:
            values = taps_ref[part * length : (part + 1) * length, :]
            high = values.astype(BF16)
            low = (values - high.astype(F32)).astype(BF16)
            full = nn(table_ref[...], jnp.concatenate([high, high], axis=0))
            full = full + nn(table_ref[:, :length], low)
            now = (full[:length], -full[length:])
        else:
            now = None
        if before is None:
            real, imag = now
        else:
            real, imag = sign * before[1], -sign * before[0]
            if now is not None:
                real, imag = now[0] + real, now[1] + imag
        spec_out[part, :length, lanes] = real
        spec_out[part, length:, lanes] = imag
        before = now

    @pl.when(step == pl.num_programs(0) - 1)
    def _():
        for copy in copies:
            copy.wait()


def prepare(pairs, place, lane, docs, table, back, taps, weight, gate, grad):
    count, width = taps.shape
    length = count // REACH
    return pl.pallas_call(
        functools.partial(prepare_kernel, pairs),
        grid=(width // LANES,),
        out_shape=(
            pltpu.VMEM((REACH + 1, 2 * length, width), F32),
            pltpu.VMEM(weight.shape, BF16),
            pltpu.VMEM(gate.shape, BF16),
            pltpu.VMEM(grad.shape[2:], BF16),
            pltpu.VMEM((2 * length, length), BF16),
            pltpu.VMEM(back.shape, BF16),
            pltpu.SMEM((2, 8), jnp.int32),
            pltpu.VMEM((8, 128), F32),
        ),
        in_specs=[
            SCALARS,
            SCALARS,
            SCALARS,
            pl.BlockSpec((2 * length, 2 * length), lambda c: (0, 0)),
            OUTSIDE,
            pl.BlockSpec((count, LANES), lambda c: (0, c)),
            OUTSIDE,
            OUTSIDE,
            OUTSIDE,
        ],
        out_specs=(WHOLE,) * 6 + (SCALARS, WHOLE),
        scratch_shapes=[pltpu.SemaphoreType.DMA((4,))],
        compiler_params=params(2 * VMEM),
        cost_estimate=pl.CostEstimate(
            flops=2 * 3 * 2 * count * length * width,
            bytes_accessed=4 * (count * width + 8 * length * width),
            transcendentals=0,
        ),
    )(place, lane, docs, table, back, taps, weight, gate, grad)


def project_kernel(hops, slot, first, last, facts_ref, *refs):
    shards, refs = refs[: len(hops)], refs[len(hops) :]
    weight_ref, gate_ref = refs[:2]
    before_ref = None if first else refs[2]
    out_ref, acc_ref = refs[-2:] if last else (refs[-1], refs[-1])
    depth = shards[0].shape[1]
    count = weight_ref.shape[1] // depth
    tiles = [pl.ds(tile * LANES, LANES) for tile in range(weight_ref.shape[0] // LANES)]
    if not first:
        acc_ref[...] = before_ref[...]
    for shard, hop in zip(shards, hops):
        at = facts_ref[0, 4 + REACH] + hop
        features = pl.ds(pl.multiple_of(jnp.clip(at, 0, count - 1) * depth, depth), depth)

        def add(shard=shard, hop=hop, features=features):
            for lanes in tiles:
                part = nt(shard[...], weight_ref[lanes, features])
                if hop == 0:
                    acc_ref[:, lanes] = part
                else:
                    acc_ref[:, lanes] += part

        if hop == 0:
            add()
        else:
            pl.when((at >= 0) & (at < count))(add)
    if last:
        out_ref[...] = (acc_ref[...] * gate_ref[0, slot].astype(F32)).astype(BF16)


def project(facts, shards, hops, weight, gate, slot, before=None, last=True, after=()):
    rows, depth = shards[0].shape
    width = weight.shape[0]
    operands = [facts, *shards, weight, gate]
    if before is not None:
        operands.append(before)
    return pl.pallas_call(
        functools.partial(project_kernel, hops, slot, before is None, last),
        out_shape=pltpu.VMEM((rows, width), BF16 if last else F32),
        in_specs=[SCALARS] + [WHOLE] * (len(operands) - 1) + [ANYWHERE] * len(after),
        out_specs=WHOLE,
        scratch_shapes=[pltpu.VMEM((rows, width), F32)] if last else [],
        compiler_params=params(),
        cost_estimate=pl.CostEstimate(
            flops=2 * rows * depth * (len(shards) + 1) // 2 * width,
            bytes_accessed=2 * (rows + width) * depth * len(shards),
            transcendentals=0,
        ),
    )(*operands, *after)


class Conv:
    def __init__(self, slot, facts, table, back, spectra):
        self.facts = [facts[slot, at] for at in range(4 + REACH)]
        self.table, self.back, self.spectra = table, back, spectra
        self.length = table.shape[0] // 2
        self.lanes = lanes_at(pl.program_id(0))
        self.row = lax.broadcasted_iota(jnp.int32, (self.length, LANES), 0)

    def joined(self, pieces):
        tiles = [piece[:, self.lanes] for piece in pieces]
        return tiles[0] if len(tiles) == 1 else jnp.concatenate(tiles, axis=0)

    def within(self, low, high):
        return (self.row >= low) & (self.row < high)

    def term(self, values, low, high, distance):
        length = self.length
        kept = jnp.where(self.within(low, high), values.astype(F32), 0.0).astype(BF16)
        full = nn(self.table[...], kept)
        real, imag = full[:length], full[length:]
        k_real = self.spectra[distance, :length, self.lanes]
        k_imag = self.spectra[distance, length:, self.lanes]
        return k_real * real - k_imag * imag, k_real * imag + k_imag * real

    def signal(self, real, imag):
        total = jnp.concatenate([real.astype(BF16), imag.astype(BF16)], axis=0)
        both = nn(self.back[...], total)
        return both[: self.length] + both[self.length :]

    def far_terms(self, acc, chosen, choices):
        for distance in range(1, REACH + 1):
            reach = self.facts[1 + distance]

            @pl.when(reach > 0)
            def _(distance=distance, reach=reach):
                for pieces, holds in choices(distance):

                    @pl.when(holds)
                    def _(pieces=pieces):
                        chosen[...] = self.joined(pieces)

                real, imag = self.term(chosen[...], 0, reach, distance)
                acc[: self.length, :] += real
                acc[self.length :, :] += imag

    def inner_documents(self, own, read, write):
        first_end, last_start = self.facts[0], self.facts[1]

        @pl.when(last_start > 0)
        def _():
            signal = self.signal(*self.term(own, 0, first_end, 0))
            write(jnp.where(self.row < first_end, signal, read()))

        @pl.when(last_start > first_end)
        def _():
            signal = self.signal(*self.term(own, first_end, last_start, 0))
            write(jnp.where(self.within(first_end, last_start), signal, read()))

    def halo(self, pieces, distance, mixed):
        sets = 3 if mixed else 4
        count = len(pieces) // sets
        kinds = [pieces[at * count : (at + 1) * count] for at in range(sets)]
        two, swapped, mate, far = kinds[0], kinds[1], kinds[2], kinds[-1]
        inner = self.facts[5]
        if distance == 2:
            return [(two, inner >= 0)]
        if distance == 1:
            return [(mate, inner == 1), (swapped, inner == 0)]
        return [(swapped, inner == 1), (far, inner == 0)]


def own_kernel(slot, pieces, facts_ref, table_ref, back_ref, spec_ref, *refs):
    own_refs, out_ref = refs[:pieces], refs[-1]
    conv = Conv(slot, facts_ref, table_ref, back_ref, spec_ref)
    own = conv.joined(own_refs)
    out_ref[:, conv.lanes] = conv.signal(*conv.term(own, conv.facts[1], conv.length, 0))

    def write(value):
        out_ref[:, conv.lanes] = value

    conv.inner_documents(own, lambda: out_ref[:, conv.lanes], write)


def far_kernel(slot, pieces, facts_ref, table_ref, back_ref, spec_ref, *refs):
    near_ref, refs = refs[0], refs[1:]
    if slot == 0:
        upper_ref, mate_ref, two_ref, fold_ref = refs[:4]
        halos = refs[4 : 4 + 3 * pieces]
    else:
        halos = refs[: 4 * pieces]
    out_ref, acc_ref, chosen_ref = refs[-3:]
    if slot == 1:
        out_ref, token_ref = refs[-4:-2]
        token_ref[...] = jnp.zeros_like(token_ref)
    conv = Conv(slot, facts_ref, table_ref, back_ref, spec_ref)
    role = conv.facts[6]

    def choices(distance):
        found = conv.halo(halos, distance, slot == 0)
        if slot == 0:
            folded = {
                1: [([upper_ref], role == 1)],
                2: [([mate_ref], (role == 1) | (role == 2))],
                3: [([two_ref], role == 1), ([upper_ref], role == 2), ([fold_ref], role == 3)],
            }
            found = found + folded[distance]
        return found

    reaches = conv.facts[2] > 0

    @pl.when(reaches)
    def _():
        acc_ref[...] = jnp.zeros_like(acc_ref)
        conv.far_terms(acc_ref, chosen_ref, choices)
        signal = conv.signal(acc_ref[: conv.length, :], acc_ref[conv.length :, :])
        kept = jnp.where(conv.row >= conv.facts[1], signal, 0.0)
        out_ref[0, 0] = near_ref[:, conv.lanes] + kept

    @pl.when(jnp.logical_not(reaches))
    def _():
        out_ref[0, 0] = near_ref[:, conv.lanes]


def conv_call(body, tabs, facts, arrays, out_shape, out_spec, scratch, after=(), result=None):
    table, back, spectra = tabs
    length = table.shape[0] // 2
    width = spectra.shape[2]
    operands = [facts, table, back, spectra, *arrays]
    specs = [SCALARS] + [WHOLE] * (len(operands) - 1) + [ANYWHERE] * len(after)
    operands.extend(after)
    aliases = {}
    if result is not None:
        aliases = {len(operands): 0}
        operands.append(result)
        specs.append(ANYWHERE)
    return pl.pallas_call(
        body,
        grid=(width // LANES,),
        out_shape=out_shape,
        in_specs=specs,
        out_specs=out_spec,
        scratch_shapes=scratch,
        input_output_aliases=aliases,
        compiler_params=params(),
        cost_estimate=pl.CostEstimate(
            flops=32 * length * length * width,
            bytes_accessed=4 * length * width,
            transcendentals=0,
        ),
    )(*operands)


def own_terms(slot, tabs, facts, pieces, after=()):
    _, back, spectra = tabs
    shape = pltpu.VMEM((back.shape[0] // 2, spectra.shape[2]), F32)
    body = functools.partial(own_kernel, slot, len(pieces))
    return conv_call(body, tabs, facts, pieces, shape, WHOLE, [], after)


def far_terms(slot, count, tabs, facts, arrays, result=None):
    _, back, spectra = tabs
    length, width = back.shape[0] // 2, spectra.shape[2]
    shape = jax.ShapeDtypeStruct((1, 2, length, width), F32)
    spec = pl.BlockSpec((1, 1, length, LANES), lambda c: (0, slot, 0, c))
    scratch = [pltpu.VMEM((2 * length, LANES), F32), pltpu.VMEM((length, LANES), BF16)]
    body = functools.partial(far_kernel, slot, count)
    if slot == 1:
        shape, spec = (shape, pltpu.VMEM((8, 128), F32)), (spec, WHOLE)
    return conv_call(body, tabs, facts, arrays, shape, spec, scratch, (), result)


def together(values, *earlier):
    return pl.pallas_call(
        lambda *refs: None,
        out_shape=[jax.ShapeDtypeStruct(one.shape, one.dtype) for one in values],
        in_specs=[ANYWHERE] * (len(values) + len(earlier)),
        out_specs=[ANYWHERE] * len(values),
        input_output_aliases={at: at for at in range(len(values))},
        compiler_params=params(VMEM // 20),
    )(*values, *earlier)


def ordered(value, *earlier):
    return together([value], *earlier)[0]


def shifted(value, steps):
    count = lax.axis_size("ctx")
    initial, last = (max(0, -steps), min(count, count - steps))
    return lax.ppermute(value, "ctx", [(source, source + steps) for source in range(initial, last)])


def core_swapped(value):
    count = lax.axis_size("ctx")
    return lax.ppermute(value, "ctx", [(source, source ^ 1) for source in range(count)])


def upper_halo_of(value):
    count = lax.axis_size("ctx")
    far = [(source, source + 3) for source in range(1, count - 3, 2)] + [(count - 1, count - 3)]
    two = shifted(value, 2)
    mate, far = core_swapped(value), lax.ppermute(value, "ctx", far)
    return [two, mate, far]


def lower_halo_of(value, *own):
    count = lax.axis_size("ctx")
    mixed = [(source, source - 1) for source in range(1, count, 2)]
    mixed += [(source, source - 3) for source in range(4, count, 2)]
    two = ordered(shifted(value, -2), *own)
    mixed = lax.ppermute(value, "ctx", mixed)
    return [two, core_swapped(two), mixed]


def on_device(grad_out, out_weight, gate, filter_taps, doc_starts):
    pairs = lax.axis_size("ctx")
    place = lax.axis_index("ctx")
    length = grad_out.shape[2]
    width = out_weight.shape[0]
    count = lax.axis_size("ch")
    lane = lax.axis_index("ch").astype(jnp.int32)[None]

    def sent(step, up, down):
        upward = [(source, source + 1) for source in range(step - 1, count - 1)]
        downward = [(source, source - 1) for source in range(1, count - step + 1)]
        return lax.ppermute(up, "ch", upward), lax.ppermute(down, "ch", downward)

    start = grad_out[0, 1]
    upper_in = [sent(1, start, start)]

    table, back = (jnp.asarray(one) for one in tables(length))
    spectra, weight, gates, lower_slice, table, back, facts, prepared = prepare(
        pairs,
        place.astype(jnp.int32)[None],
        lane,
        doc_starts,
        table,
        back,
        filter_taps,
        out_weight,
        gate,
        grad_out,
    )
    tabs = (table, back, spectra)

    def pass_on(chain, *earlier):
        if earlier:
            chain[-1] = together(chain[-1], *earlier)
        chain.append(sent(len(chain) + 1, *chain[-1]))

    hops = [0] + [way * step for step in range(1, count) for way in (-1, 1)]

    def partial_of(own, arrived, slot, after=()):
        shards = [own] + [one for pair in arrived[: count - 2] for one in pair]
        return project(
            facts, shards, hops[:-2], weight, gates, slot, last=False, after=after
        )

    def final_of(arrived, slot, partial, after=()):
        return project(facts, arrived[-1], hops[-2:], weight, gates, slot, partial, after=after)

    pass_on(upper_in, prepared)
    own = ordered(lower_slice, *upper_in[0])
    lower_in = [sent(1, own, own)]
    for _ in range(3, count):
        pass_on(upper_in)
        pass_on(lower_in, *upper_in[-2])
    partial = partial_of(start, upper_in, 1)
    upper = final_of(upper_in, 1, partial)
    upper_halo = upper_halo_of(upper)
    two, mate, fold = upper_halo
    pass_on(lower_in, upper, mate)

    partial = partial_of(own, lower_in, 0)
    lower = final_of(lower_in, 0, partial, [two])
    near = own_terms(0, tabs, facts, [lower], after=[fold])
    two = ordered(two, near)
    upper_halo = [two, core_swapped(two), mate, fold]
    upper_near = own_terms(1, tabs, facts, [upper], after=[lower])
    result, _ = far_terms(1, 1, tabs, facts, [upper_near, *upper_halo])
    lower_halo = lower_halo_of(lower, near, upper_near)
    arrays = [near, upper, mate, two, fold, *lower_halo]
    return far_terms(0, 1, tabs, facts, arrays, result)


def solution(mesh):
    in_specs = (
        P("ctx", None, None, "ch"),
        P("ch", None),
        P("ctx", None, None, "ch"),
        P(None, "ch"),
        P(),
    )
    out_specs = P("ctx", None, None, "ch")
    return jax.shard_map(
        on_device, mesh=mesh, in_specs=in_specs, out_specs=out_specs, check_vma=False
    )
```

```python
import functools
import math

import jax
import jax.numpy as jnp
import ml_dtypes
import numpy as np
from jax import lax
from jax.experimental import pallas as pl
from jax.experimental.pallas import tpu as pltpu
from jax.sharding import PartitionSpec as P

REACH = 3
LANES = 1024
VMEM = 20 * 1024 * 1024
F32 = jnp.float32
BF16 = jnp.bfloat16
WHOLE = pl.BlockSpec(memory_space=pltpu.VMEM)
ANYWHERE = pl.BlockSpec(memory_space=pl.ANY)
OUTSIDE = pl.BlockSpec(memory_space=pltpu.HBM)
SCALARS = pl.BlockSpec(memory_space=pltpu.SMEM)


def parts_of(table):
    high = table.astype(np.float32).astype(ml_dtypes.bfloat16)
    low = (table - high.astype(np.float64)).astype(np.float32).astype(ml_dtypes.bfloat16)
    return high, low


@functools.lru_cache(maxsize=None)
def tables(length):
    angle = np.outer(2 * np.arange(length) + 1, np.arange(length)) % (4 * length)
    angle = angle.astype(np.float64) * (math.pi / (2 * length))
    forward = np.concatenate([np.cos(angle), -np.sin(angle)], axis=0)
    high, low = parts_of(forward)
    back_high, back_low = parts_of(forward.T / length)
    return np.concatenate([high, low], axis=1), np.concatenate([back_high, back_low], axis=0)


def nn(a, b):
    return lax.dot_general(a, b, (((1,), (0,)), ((), ())), preferred_element_type=F32)


def nt(a, b):
    return lax.dot_general(a, b, (((1,), (1,)), ((), ())), preferred_element_type=F32)


def params(limit=VMEM):
    return pltpu.CompilerParams(vmem_limit_bytes=limit)


def lanes_at(tile):
    return pl.ds(pl.multiple_of(tile * LANES, LANES), LANES)


def write_facts(facts_ref, slot, docs_ref, block, length, end, inner, role):
    start = block * length
    stop = start + length - 1

    def visit(at, found):
        first, following, last = found
        here = docs_ref[at]
        first = jnp.minimum(first, jnp.where(here > start, here, end))
        following = jnp.minimum(following, jnp.where(here > stop, here, end))
        last = jnp.maximum(last, jnp.where(here <= stop, here, 0))
        return first, following, last

    whole = jnp.int32(end)
    first, following, last = lax.fori_loop(
        0, docs_ref.shape[0], visit, (whole, whole, jnp.int32(0))
    )
    facts_ref[slot, 0] = jnp.clip(first - start, 0, length)
    facts_ref[slot, 1] = jnp.clip(last - start, 0, length)
    for distance in range(1, REACH + 1):
        facts_ref[slot, 1 + distance] = jnp.clip(following - start - distance * length, 0, length)
    facts_ref[slot, 2 + REACH] = inner
    facts_ref[slot, 3 + REACH] = role


def prepare_kernel(pairs, *refs):
    place_ref, lane_ref, docs_ref, table_ref, back_ref, taps_ref = refs[:6]
    weight_ref, gate_ref, grad_ref = refs[6:9]
    spec_out, weight_out, gate_out, lower_out, table_out, back_out = refs[9:15]
    facts_out, token_out, sems = refs[15:]
    token_out[...] = jnp.zeros_like(token_out)
    copies = [
        pltpu.make_async_copy(source, target, sems.at[at])
        for at, (source, target) in enumerate(
            [
                (grad_ref.at[0, 0], lower_out),
                (weight_ref, weight_out),
                (gate_ref, gate_out),
                (back_ref, back_out),
            ]
        )
    ]
    step = pl.program_id(0)
    length = table_ref.shape[1] // 2

    @pl.when(step == 0)
    def _():
        for copy in copies:
            copy.start()
        table_out[...] = table_ref[:, :length]
        place = place_ref[0]
        odd = lax.rem(place, 2)
        role = jnp.where(place >= pairs - 3, pairs - place, 0)
        end = 2 * pairs * length
        for slot in range(2):
            facts_out[slot, 4 + REACH] = lane_ref[0]
        write_facts(facts_out, 0, docs_ref, place, length, end, 1 - odd, role)
        write_facts(facts_out, 1, docs_ref, 2 * pairs - 1 - place, length, end, odd, role)

    freq = lax.broadcasted_iota(jnp.int32, (length, 1), 0)
    sign = jnp.where(freq % 2 == 0, 1.0, -1.0).astype(F32)
    lanes = lanes_at(step)
    before = None
    for part in range(REACH + 1):
        if part < REACH:
            values = taps_ref[part * length : (part + 1) * length, :]
            high = values.astype(BF16)
            low = (values - high.astype(F32)).astype(BF16)
            full = nn(table_ref[...], jnp.concatenate([high, high], axis=0))
            full = full + nn(table_ref[:, :length], low)
            now = (full[:length], -full[length:])
        else:
            now = None
        if before is None:
            real, imag = now
        else:
            real, imag = sign * before[1], -sign * before[0]
            if now is not None:
                real, imag = now[0] + real, now[1] + imag
        spec_out[part, :length, lanes] = real
        spec_out[part, length:, lanes] = imag
        before = now

    @pl.when(step == pl.num_programs(0) - 1)
    def _():
        for copy in copies:
            copy.wait()


def prepare(pairs, place, lane, docs, table, back, taps, weight, gate, grad):
    count, width = taps.shape
    length = count // REACH
    return pl.pallas_call(
        functools.partial(prepare_kernel, pairs),
        grid=(width // LANES,),
        out_shape=(
            pltpu.VMEM((REACH + 1, 2 * length, width), F32),
            pltpu.VMEM(weight.shape, BF16),
            pltpu.VMEM(gate.shape, BF16),
            pltpu.VMEM(grad.shape[2:], BF16),
            pltpu.VMEM((2 * length, length), BF16),
            pltpu.VMEM(back.shape, BF16),
            pltpu.SMEM((2, 8), jnp.int32),
            pltpu.VMEM((8, 128), F32),
        ),
        in_specs=[
            SCALARS,
            SCALARS,
            SCALARS,
            pl.BlockSpec((2 * length, 2 * length), lambda c: (0, 0)),
            OUTSIDE,
            pl.BlockSpec((count, LANES), lambda c: (0, c)),
            OUTSIDE,
            OUTSIDE,
            OUTSIDE,
        ],
        out_specs=(WHOLE,) * 6 + (SCALARS, WHOLE),
        scratch_shapes=[pltpu.SemaphoreType.DMA((4,))],
        compiler_params=params(2 * VMEM),
        cost_estimate=pl.CostEstimate(
            flops=2 * 3 * 2 * count * length * width,
            bytes_accessed=4 * (count * width + 8 * length * width),
            transcendentals=0,
        ),
    )(place, lane, docs, table, back, taps, weight, gate, grad)


def project_kernel(hops, slot, first, last, facts_ref, *refs):
    shards, refs = refs[: len(hops)], refs[len(hops) :]
    weight_ref, gate_ref = refs[:2]
    before_ref = None if first else refs[2]
    out_ref, acc_ref = refs[-2:] if last else (refs[-1], refs[-1])
    depth = shards[0].shape[1]
    count = weight_ref.shape[1] // depth
    tiles = [pl.ds(tile * LANES, LANES) for tile in range(weight_ref.shape[0] // LANES)]
    if not first:
        acc_ref[...] = before_ref[...]
    for shard, hop in zip(shards, hops):
        at = facts_ref[0, 4 + REACH] + hop
        features = pl.ds(pl.multiple_of(jnp.clip(at, 0, count - 1) * depth, depth), depth)

        def add(shard=shard, hop=hop, features=features):
            for lanes in tiles:
                part = nt(shard[...], weight_ref[lanes, features])
                if hop == 0:
                    acc_ref[:, lanes] = part
                else:
                    acc_ref[:, lanes] += part

        if hop == 0:
            add()
        else:
            pl.when((at >= 0) & (at < count))(add)
    if last:
        out_ref[...] = (acc_ref[...] * gate_ref[0, slot].astype(F32)).astype(BF16)


def project(facts, shards, hops, weight, gate, slot, before=None, last=True, after=()):
    rows, depth = shards[0].shape
    width = weight.shape[0]
    operands = [facts, *shards, weight, gate]
    if before is not None:
        operands.append(before)
    return pl.pallas_call(
        functools.partial(project_kernel, hops, slot, before is None, last),
        out_shape=pltpu.VMEM((rows, width), BF16 if last else F32),
        in_specs=[SCALARS] + [WHOLE] * (len(operands) - 1) + [ANYWHERE] * len(after),
        out_specs=WHOLE,
        scratch_shapes=[pltpu.VMEM((rows, width), F32)] if last else [],
        compiler_params=params(),
        cost_estimate=pl.CostEstimate(
            flops=2 * rows * depth * (len(shards) + 1) // 2 * width,
            bytes_accessed=2 * (rows + width) * depth * len(shards),
            transcendentals=0,
        ),
    )(*operands, *after)


class Conv:
    def __init__(self, slot, facts, table, back, spectra):
        self.facts = [facts[slot, at] for at in range(4 + REACH)]
        self.table, self.back, self.spectra = table, back, spectra
        self.length = table.shape[0] // 2
        self.lanes = lanes_at(pl.program_id(0))
        self.row = lax.broadcasted_iota(jnp.int32, (self.length, LANES), 0)

    def joined(self, pieces):
        tiles = [piece[:, self.lanes] for piece in pieces]
        return tiles[0] if len(tiles) == 1 else jnp.concatenate(tiles, axis=0)

    def within(self, low, high):
        return (self.row >= low) & (self.row < high)

    def term(self, values, low, high, distance):
        length = self.length
        kept = jnp.where(self.within(low, high), values.astype(F32), 0.0).astype(BF16)
        full = nn(self.table[...], kept)
        real, imag = full[:length], full[length:]
        k_real = self.spectra[distance, :length, self.lanes]
        k_imag = self.spectra[distance, length:, self.lanes]
        return k_real * real - k_imag * imag, k_real * imag + k_imag * real

    def signal(self, real, imag):
        total = jnp.concatenate([real.astype(BF16), imag.astype(BF16)], axis=0)
        both = nn(self.back[...], total)
        return both[: self.length] + both[self.length :]

    def far_terms(self, acc, chosen, choices):
        for distance in range(1, REACH + 1):
            reach = self.facts[1 + distance]

            @pl.when(reach > 0)
            def _(distance=distance, reach=reach):
                for pieces, holds in choices(distance):

                    @pl.when(holds)
                    def _(pieces=pieces):
                        chosen[...] = self.joined(pieces)

                real, imag = self.term(chosen[...], 0, reach, distance)
                acc[: self.length, :] += real
                acc[self.length :, :] += imag

    def inner_documents(self, own, read, write):
        first_end, last_start = self.facts[0], self.facts[1]

        @pl.when(last_start > 0)
        def _():
            signal = self.signal(*self.term(own, 0, first_end, 0))
            write(jnp.where(self.row < first_end, signal, read()))

        @pl.when(last_start > first_end)
        def _():
            signal = self.signal(*self.term(own, first_end, last_start, 0))
            write(jnp.where(self.within(first_end, last_start), signal, read()))

    def halo(self, pieces, distance, mixed):
        sets = 3 if mixed else 4
        count = len(pieces) // sets
        kinds = [pieces[at * count : (at + 1) * count] for at in range(sets)]
        two, swapped, mate, far = kinds[0], kinds[1], kinds[2], kinds[-1]
        inner = self.facts[5]
        if distance == 2:
            return [(two, inner >= 0)]
        if distance == 1:
            return [(mate, inner == 1), (swapped, inner == 0)]
        return [(swapped, inner == 1), (far, inner == 0)]


def own_kernel(slot, pieces, facts_ref, table_ref, back_ref, spec_ref, *refs):
    own_refs, out_ref = refs[:pieces], refs[-1]
    conv = Conv(slot, facts_ref, table_ref, back_ref, spec_ref)
    own = conv.joined(own_refs)
    out_ref[:, conv.lanes] = conv.signal(*conv.term(own, conv.facts[1], conv.length, 0))

    def write(value):
        out_ref[:, conv.lanes] = value

    conv.inner_documents(own, lambda: out_ref[:, conv.lanes], write)


def far_kernel(slot, pieces, facts_ref, table_ref, back_ref, spec_ref, *refs):
    near_ref, refs = refs[0], refs[1:]
    if slot == 0:
        upper_ref, mate_ref, two_ref, fold_ref = refs[:4]
        halos = refs[4 : 4 + 3 * pieces]
    else:
        halos = refs[: 4 * pieces]
    out_ref, acc_ref, chosen_ref = refs[-3:]
    if slot == 1:
        out_ref, token_ref = refs[-4:-2]
        token_ref[...] = jnp.zeros_like(token_ref)
    conv = Conv(slot, facts_ref, table_ref, back_ref, spec_ref)
    role = conv.facts[6]

    def choices(distance):
        found = conv.halo(halos, distance, slot == 0)
        if slot == 0:
            folded = {
                1: [([upper_ref], role == 1)],
                2: [([mate_ref], (role == 1) | (role == 2))],
                3: [([two_ref], role == 1), ([upper_ref], role == 2), ([fold_ref], role == 3)],
            }
            found = found + folded[distance]
        return found

    reaches = conv.facts[2] > 0

    @pl.when(reaches)
    def _():
        acc_ref[...] = jnp.zeros_like(acc_ref)
        conv.far_terms(acc_ref, chosen_ref, choices)
        signal = conv.signal(acc_ref[: conv.length, :], acc_ref[conv.length :, :])
        kept = jnp.where(conv.row >= conv.facts[1], signal, 0.0)
        out_ref[0, 0] = near_ref[:, conv.lanes] + kept

    @pl.when(jnp.logical_not(reaches))
    def _():
        out_ref[0, 0] = near_ref[:, conv.lanes]


def conv_call(body, tabs, facts, arrays, out_shape, out_spec, scratch, after=(), result=None):
    table, back, spectra = tabs
    length = table.shape[0] // 2
    width = spectra.shape[2]
    operands = [facts, table, back, spectra, *arrays]
    specs = [SCALARS] + [WHOLE] * (len(operands) - 1) + [ANYWHERE] * len(after)
    operands.extend(after)
    aliases = {}
    if result is not None:
        aliases = {len(operands): 0}
        operands.append(result)
        specs.append(ANYWHERE)
    return pl.pallas_call(
        body,
        grid=(width // LANES,),
        out_shape=out_shape,
        in_specs=specs,
        out_specs=out_spec,
        scratch_shapes=scratch,
        input_output_aliases=aliases,
        compiler_params=params(),
        cost_estimate=pl.CostEstimate(
            flops=32 * length * length * width,
            bytes_accessed=4 * length * width,
            transcendentals=0,
        ),
    )(*operands)


def own_terms(slot, tabs, facts, pieces, after=()):
    _, back, spectra = tabs
    shape = pltpu.VMEM((back.shape[0] // 2, spectra.shape[2]), F32)
    body = functools.partial(own_kernel, slot, len(pieces))
    return conv_call(body, tabs, facts, pieces, shape, WHOLE, [], after)


def far_terms(slot, count, tabs, facts, arrays, result=None):
    _, back, spectra = tabs
    length, width = back.shape[0] // 2, spectra.shape[2]
    shape = jax.ShapeDtypeStruct((1, 2, length, width), F32)
    spec = pl.BlockSpec((1, 1, length, LANES), lambda c: (0, slot, 0, c))
    scratch = [pltpu.VMEM((2 * length, LANES), F32), pltpu.VMEM((length, LANES), BF16)]
    body = functools.partial(far_kernel, slot, count)
    if slot == 1:
        shape, spec = (shape, pltpu.VMEM((8, 128), F32)), (spec, WHOLE)
    return conv_call(body, tabs, facts, arrays, shape, spec, scratch, (), result)


def ordered(value, *earlier):
    return pl.pallas_call(
        lambda *refs: None,
        out_shape=jax.ShapeDtypeStruct(value.shape, value.dtype),
        in_specs=[ANYWHERE] * (1 + len(earlier)),
        out_specs=ANYWHERE,
        input_output_aliases={0: 0},
        compiler_params=params(VMEM // 20),
    )(value, *earlier)


def shifted(value, steps):
    count = lax.axis_size("ctx")
    initial, last = (max(0, -steps), min(count, count - steps))
    return lax.ppermute(value, "ctx", [(source, source + steps) for source in range(initial, last)])


def core_swapped(value):
    count = lax.axis_size("ctx")
    return lax.ppermute(value, "ctx", [(source, source ^ 1) for source in range(count)])


def upper_halo_of(value):
    count = lax.axis_size("ctx")
    far = [(source, source + 3) for source in range(1, count - 3, 2)] + [(count - 1, count - 3)]
    two = shifted(value, 2)
    mate, far = core_swapped(value), lax.ppermute(value, "ctx", far)
    return [two, core_swapped(two), mate, far]


def lower_halo_of(value, own):
    count = lax.axis_size("ctx")
    mixed = [(source, source - 1) for source in range(1, count, 2)]
    mixed += [(source, source - 3) for source in range(4, count, 2)]
    two = ordered(shifted(value, -2), own)
    mixed = lax.ppermute(value, "ctx", mixed)
    return [two, core_swapped(two), mixed]


def on_device(grad_out, out_weight, gate, filter_taps, doc_starts):
    pairs = lax.axis_size("ctx")
    place = lax.axis_index("ctx")
    length = grad_out.shape[2]
    width = out_weight.shape[0]
    count = lax.axis_size("ch")
    lane = lax.axis_index("ch").astype(jnp.int32)[None]

    def sent(step, up, down):
        upward = [(source, source + 1) for source in range(step - 1, count - 1)]
        downward = [(source, source - 1) for source in range(1, count - step + 1)]
        return lax.ppermute(up, "ch", upward), lax.ppermute(down, "ch", downward)

    start = grad_out[0, 1]
    upper_in = [sent(1, start, start)]

    table, back = (jnp.asarray(one) for one in tables(length))
    spectra, weight, gates, lower_slice, table, back, facts, prepared = prepare(
        pairs,
        place.astype(jnp.int32)[None],
        lane,
        doc_starts,
        table,
        back,
        filter_taps,
        out_weight,
        gate,
        grad_out,
    )
    tabs = (table, back, spectra)

    def pass_on(chain, *earlier):
        if earlier:
            chain[-1] = [ordered(one, *earlier) for one in chain[-1]]
        chain.append(sent(len(chain) + 1, *chain[-1]))

    hops = [0] + [way * step for step in range(1, count) for way in (-1, 1)]

    def partial_of(own, arrived, slot, after=()):
        shards = [own] + [one for pair in arrived[: count - 2] for one in pair]
        return project(
            facts, shards, hops[:-2], weight, gates, slot, last=False, after=after
        )

    def final_of(arrived, slot, partial, after=()):
        return project(facts, arrived[-1], hops[-2:], weight, gates, slot, partial, after=after)

    pass_on(upper_in, prepared)
    own = ordered(lower_slice, *upper_in[0])
    lower_in = [sent(1, own, own)]
    for _ in range(3, count):
        pass_on(upper_in)
        pass_on(lower_in, *upper_in[-2])
    partial = partial_of(start, upper_in, 1)
    upper = final_of(upper_in, 1, partial)
    pass_on(lower_in, upper)

    upper_halo = upper_halo_of(upper)
    two, swapped, mate, fold = upper_halo
    near = own_terms(1, tabs, facts, [upper])
    result, _ = far_terms(1, 1, tabs, facts, [near, *upper_halo])

    partial = partial_of(own, lower_in, 0, [near])
    lower = final_of(lower_in, 0, partial, [two, mate])
    near = own_terms(0, tabs, facts, [lower], after=[fold])
    lower_halo = lower_halo_of(lower, near)
    arrays = [near, upper, mate, two, fold, *lower_halo]
    return far_terms(0, 1, tabs, facts, arrays, result)


def solution(mesh):
    in_specs = (
        P("ctx", None, None, "ch"),
        P("ch", None),
        P("ctx", None, None, "ch"),
        P(None, "ch"),
        P(),
    )
    out_specs = P("ctx", None, None, "ch")
    return jax.shard_map(
        on_device, mesh=mesh, in_specs=in_specs, out_specs=out_specs, check_vma=False
    )
```
